32 devices in a mesh: row: 4 (over y, x), seq: 8 (over z, core).
Axes of the slice: x: 2, y: 2, z: 4, core: 2. Of those that a mesh axis runs over, the one named last changes fastest.
Arguments:
- tokens: bfloat16 [4, 1024, 2048], P('row', 'seq'), may hold values from -6 to 6
- cotangent: bfloat16 [4, 1024, 2048], P('row', 'seq'), may hold values from -6 to 6
- modality: int32 [4, 1024], P(None, 'seq'), may hold values from 0 to 2
- starts: int32 [4, 1024], P(None, 'seq'), may hold values from 0 to 1, as said below
- row_lengths: int32 [4], replicated, may hold values from 960 to 1024
- norm_gain: bfloat16 [2048], P('seq'), may hold values from 0.5 to 1.5
- in_x_weight: bfloat16 [2048, 3, 4096], P('seq', None, 'row'), may hold values from -0.125 to 0.125
- in_z_weight: bfloat16 [2048, 3, 4096], P('seq', None, 'row'), may hold values from -0.125 to 0.125
- xdt_weight: bfloat16 [4096, 3, 128], P(('row', 'seq')), may hold values from -0.09375 to 0.09375
- xbc_weight: bfloat16 [32, 3, 4096], P(None, None, ('row', 'seq')), may hold values from -0.09375 to 0.09375
- dt_weight: bfloat16 [128, 3, 4096], P(None, None, ('row', 'seq')), may hold values from -0.5 to 0.5
- dt_bias: bfloat16 [3, 4096], P(None, ('row', 'seq')), may hold values from -11 to -2
- conv_weight: bfloat16 [4, 4096], P(None, ('row', 'seq')), may hold values from -3 to 3
- conv_bias: bfloat16 [4096], P(('row', 'seq')), may hold values from -3 to 3
- log_rates: bfloat16 [16, 4096], P(None, ('row', 'seq')), may hold values from 0 to 2.765625
- skip_gain: bfloat16 [4096], P(('row', 'seq')), may hold values from 0.5 to 1.5
- out_weight: bfloat16 [2048, 3, 4096], P('seq', None, 'row'), may hold values from -0.1875 to 0.1875
Outputs:
- block_out: bfloat16 [4, 1024, 2048], P('row', 'seq')
- tokens_grad: bfloat16 [4, 1024, 2048], P('row', 'seq')
- norm_gain_grad: float32 [2048], P('seq')
- in_x_grad: float32 [2048, 3, 4096], P('seq', None, 'row')
- in_z_grad: float32 [2048, 3, 4096], P('seq', None, 'row')
- xdt_grad: float32 [4096, 3, 128], P(('row', 'seq'))
- xbc_grad: float32 [32, 3, 4096], P(None, None, ('row', 'seq'))
- dt_weight_grad: float32 [128, 3, 4096], P(None, None, ('row', 'seq'))
- dt_bias_grad: float32 [3, 4096], P(None, ('row', 'seq'))
- conv_weight_grad: float32 [4, 4096], P(None, ('row', 'seq'))
- conv_bias_grad: float32 [4096], P(('row', 'seq'))
- log_rates_grad: float32 [16, 4096], P(None, ('row', 'seq'))
- skip_gain_grad: float32 [4096], P(('row', 'seq'))
- out_weight_grad: float32 [2048, 3, 4096], P('seq', None, 'row')
The draws below stay inside these ranges and needn't reach their ends.
Inputs may be any that keep to these rules, and one draw needn't show every extreme that they name: `starts`: the first position of every row is 1.
All inputs are finite; a program needn't handle non-finite values.
Results may differ from the reference program's by a relative error of at most 0.013.
Values may be sent and summed in bfloat16 or wider, within the bound.
No kernel may reach another device: no remote copies, remote signals or barrier semaphores. Data moves between devices by JAX's collectives and lax.ppermute only.
A program may use at most 320 MiB of HBM per device.

```python
import math
import jax
import jax.numpy as jnp
from jax import lax

D = 2048
INNER = 4096
STATE = 16
RANK = 128
KERNEL = 4
MODS = 3
TOK_DEV = 128
ROWS = 4
LEN = 1024


def draw_starts(key, part):
    key = jax.random.fold_in(key, 11)
    subkeys = jax.random.split(key, 3)
    position = jnp.arange(LEN, dtype=jnp.int32)[None, :]
    long_first = jax.random.randint(subkeys[0], (ROWS, 1), 1, TOK_DEV)
    long_last = jax.random.randint(subkeys[1], (ROWS, 1), LEN - TOK_DEV + 1, LEN)
    coin_flip = jax.random.randint(subkeys[2], (ROWS, LEN), 0, 24)
    outside = (position < long_first) | (position > long_last)
    start_flags = (coin_flip == 0) & outside | (position == 0) | (position == long_first) | (position == long_last)
    return start_flags.astype(jnp.int32)


def draw_row_lengths(key, part):
    key = jax.random.fold_in(key, 23)
    subkeys = jax.random.split(key, 2)
    shortened = jax.random.randint(subkeys[0], (ROWS,), 0, TOK_DEV // 2 + 1)
    ranking = jax.random.permutation(subkeys[1], ROWS)
    shortened = jnp.where(ranking == 0, 0, jnp.where(ranking == 1, TOK_DEV // 2, shortened))
    return (LEN - shortened).astype(jnp.int32)


def draw_dt_bias(key, part):
    key = jax.random.fold_in(key, 37)
    subkeys = jax.random.split(key, 3)
    slow_share = 0.5
    is_slow = jax.random.uniform(subkeys[0], (MODS, INNER), dtype=jnp.float32) < slow_share
    slow_rate = jnp.exp(jax.random.uniform(subkeys[1], (MODS, INNER), dtype=jnp.float32, minval=math.log(0.2), maxval=math.log(2.0))) / LEN
    fast_rate = jnp.exp(jax.random.uniform(subkeys[2], (MODS, INNER), dtype=jnp.float32, minval=math.log(0.01), maxval=math.log(0.1)))
    chosen_rate = jnp.where(is_slow, slow_rate, fast_rate)
    return jnp.log(jnp.expm1(chosen_rate)).astype(jnp.bfloat16)


def set_ends(values, own_key, low, top_value):
    extent = values.shape
    spot = [jax.random.randint(jax.random.fold_in(own_key, axis), (), 0, extent[axis]) for axis in range(len(extent))]
    values = values.at[tuple(spot)].set(low)
    longest = extent.index(max(extent))
    spot[longest] = (spot[longest] + 1) % extent[longest]
    return values.at[tuple(spot)].set(top_value)


def levels(own_key, shape, cuts, low, largest):
    level, own = 1.0, jax.random.fold_in(own_key, 6)
    for dim, shards_of in cuts:
        draws = jnp.exp(jax.random.uniform(jax.random.fold_in(own, dim), (shards_of,), jnp.float32, low / len(cuts), largest / len(cuts)))
        level = level * jnp.repeat(draws, shape[dim] // shards_of).reshape([-1 if axis == dim else 1 for axis in range(len(shape))])
    return level


def gaussian(stream_key, shape, width, bound, cuts=(), kind=jnp.bfloat16):
    entries = width * jax.random.normal(stream_key, shape, jnp.float32)
    if cuts:
        entries = entries * levels(stream_key, shape, cuts, -0.22, 0.18)
    return jnp.clip(entries, -bound, bound).astype(kind)


def setup_inputs(seed: int = 0) -> dict:
    key_list = jax.random.split(jax.random.key(seed), 18)
    return {
        "tokens": gaussian(key_list[0], (ROWS, LEN, D), 1.0, 6.0, ((0, 4), (1, 8))),
        "cotangent": gaussian(key_list[1], (ROWS, LEN, D), 1.0, 6.0, ((0, 4), (1, 8))),
        "modality": set_ends(jax.random.randint(key_list[2], (ROWS, LEN), 0, MODS), jax.random.fold_in(key_list[2], 1), 0, MODS - 1).astype(jnp.int32),
        "starts": draw_starts(jax.random.fold_in(key_list[17], 71), 0),
        "row_lengths": draw_row_lengths(jax.random.fold_in(key_list[17], 71), 0),
        "norm_gain": jnp.clip(1.0 + 0.1 * jax.random.normal(key_list[5], (D,), jnp.float32), 0.5, 1.5).astype(jnp.bfloat16),
        "in_x_weight": gaussian(key_list[6], (D, MODS, INNER), D ** -0.5, 0.125, ((0, 8), (2, 4))),
        "in_z_weight": gaussian(key_list[7], (D, MODS, INNER), D ** -0.5, 0.125, ((0, 8), (2, 4))),
        "xdt_weight": gaussian(key_list[8], (INNER, MODS, RANK), INNER ** -0.5, 0.09375, ((0, 32),)),
        "xbc_weight": gaussian(key_list[9], (2 * STATE, MODS, INNER), INNER ** -0.5, 0.09375, ((2, 32),)),
        "dt_weight": gaussian(key_list[10], (RANK, MODS, INNER), RANK ** -0.5, 0.5, ((2, 32),)),
        "dt_bias": draw_dt_bias(jax.random.fold_in(key_list[17], 71), 0),
        "conv_weight": gaussian(key_list[12], (KERNEL, INNER), KERNEL ** -0.5, 3.0, ((1, 32),)),
        "conv_bias": gaussian(key_list[13], (INNER,), 0.5, 3.0, ((0, 32),)),
        "log_rates": jnp.clip(2.765625 * jax.random.uniform(key_list[14], (STATE, INNER), jnp.float32) ** levels(key_list[14], (STATE, INNER), ((1, 32),), -0.2, 0.2), 0.0, 2.765625).astype(jnp.bfloat16),
        "skip_gain": jnp.clip(0.5 + 1.0 * jax.random.uniform(key_list[15], (INNER,), jnp.float32) ** levels(key_list[15], (INNER,), ((0, 32),), -0.2, 0.2), 0.5, 1.5).astype(jnp.bfloat16),
        "out_weight": gaussian(key_list[16], (D, MODS, INNER), (INNER // 4) ** -0.5, 0.1875, ((0, 8), (2, 4))),
    }


@jax.custom_vjp
def low(v):
    return lax.optimization_barrier(v.astype(jnp.bfloat16)).astype(jnp.float32)

@jax.custom_vjp
def low_back(v):
    return v

def low_keep(v):
    return (low(v), None)

def low_pass(kept, grad):
    return (grad,)

def back_keep(v):
    return (v, None)

def back_low(kept, grad):
    return (low(grad),)
low.defvjp(low_keep, low_pass)
low_back.defvjp(back_keep, back_low)
epsilon = 1e-05
highest = lax.Precision.HIGHEST
scan_span = 32

def apply_silu(values):
    return values * jax.nn.sigmoid(values)

def modal_lead(values, weight, onehot):
    return jnp.einsum('lk,kmn,lm->ln', values, weight, onehot, precision=highest)

def modal_trail(values, weight, onehot):
    return jnp.einsum('lk,nmk,lm->ln', values, weight, onehot, precision=highest)

def scan_row(step_size, in_coef, out_coef, activated, keep_rate, decay_coef):
    length, channels = step_size.shape
    blocks = length // scan_span

    def shaped(values):
        return values.reshape((blocks, scan_span) + values.shape[1:])

    def one_block(state_now, block_piece):

        def one_step(held_state, step_item):
            step_delta, step_in, step_out, step_act, step_keep = step_item
            held_state = jnp.exp(step_delta[None, :] * decay_coef) * step_keep * held_state + (step_delta * step_act)[None, :] * step_in[:, None]
            return (held_state, lax.optimization_barrier(jnp.sum(step_out[:, None] * held_state, axis=0)))
        return lax.scan(one_step, state_now, block_piece)
    initial = jnp.zeros(decay_coef.shape, jnp.float32)
    pieces = tuple((shaped(values) for values in (step_size, in_coef, out_coef, activated, keep_rate)))
    _, outputs = lax.scan(jax.checkpoint(one_block), initial, pieces)
    return outputs.reshape(length, channels)

def row_forward(weights, row_data):
    norm_gain, in_x, in_z, xdt, xbc, dt_w, dt_b, conv_w, conv_b, log_rates, skip_gain, out_w = weights
    inputs, onehot, doc_ids, keep_rate, valid_mask = row_data
    inv_rms = lax.rsqrt(lax.optimization_barrier(jnp.mean(inputs * inputs, axis=-1, keepdims=True)) + epsilon)
    normed = low(inputs * inv_rms * norm_gain)
    conv_in = low(low_back(modal_lead(normed, in_x, onehot)))
    gate_in = low_back(modal_lead(normed, in_z, onehot))
    margin = KERNEL - 1
    padded = jnp.concatenate([jnp.zeros((margin, conv_in.shape[1]), jnp.float32), conv_in], axis=0)
    doc_pad = jnp.concatenate([jnp.full((margin,), -1, jnp.int32), doc_ids], axis=0)
    conv_pre = conv_b
    for lag_index in range(KERNEL):
        same_doc = (doc_pad[margin - lag_index:margin - lag_index + LEN] == doc_ids).astype(jnp.float32)
        conv_pre = conv_pre + conv_w[lag_index] * same_doc[:, None] * padded[margin - lag_index:margin - lag_index + LEN]
    activated = apply_silu(conv_pre)
    activated_low = low(activated)
    low_rank = low(low_back(modal_lead(activated_low, xdt, onehot)))
    proj_bc = low_back(modal_trail(activated_low, xbc, onehot))
    in_coef = proj_bc[:, :STATE]
    out_coef = proj_bc[:, STATE:]
    dt_pre = low_back(modal_lead(low_rank, dt_w, onehot) + jnp.dot(onehot, dt_b, precision=highest))
    step_size = jax.nn.softplus(dt_pre)
    decay_coef = -jnp.exp(log_rates)
    scanned = scan_row(step_size, in_coef, out_coef, activated, keep_rate, decay_coef) + skip_gain * activated
    gated_out = low(scanned * apply_silu(gate_in))
    branch = modal_trail(gated_out, out_w, onehot)
    return inputs + valid_mask[:, None] * branch

def reference(tokens, cotangent, modality, starts, row_lengths, norm_gain, in_x_weight, in_z_weight, xdt_weight, xbc_weight, dt_weight, dt_bias, conv_weight, conv_bias, log_rates, skip_gain, out_weight):
    onehot = (modality[:, :, None] == jnp.arange(MODS, dtype=jnp.int32)[None, None, :]).astype(jnp.float32)
    doc_ids = jnp.cumsum(starts, axis=1).astype(jnp.int32)
    keep_rate = 1.0 - starts.astype(jnp.float32)
    valid_mask = (jnp.arange(LEN, dtype=jnp.int32)[None, :] < row_lengths[:, None]).astype(jnp.float32)
    params = tuple((weight.astype(jnp.float32) for weight in (norm_gain, in_x_weight, in_z_weight, xdt_weight, xbc_weight, dt_weight, dt_bias, conv_weight, conv_bias, log_rates, skip_gain, out_weight)))

    def forward(inputs, *weights):

        def one_row(carried, row_data):
            return (carried, row_forward(weights, row_data))
        _, outputs = lax.scan(jax.checkpoint(one_row), jnp.zeros((), jnp.float32), (inputs, onehot, doc_ids, keep_rate, valid_mask))
        return outputs
    outputs, pullback = jax.vjp(forward, tokens.astype(jnp.float32), *params)
    gradients = pullback(cotangent.astype(jnp.float32))
    return (outputs.astype(jnp.bfloat16), gradients[0].astype(jnp.bfloat16), gradients[1], gradients[2], gradients[3], gradients[4], gradients[5], gradients[6], gradients[7], gradients[8], gradients[9], gradients[10], gradients[11], gradients[12])
```

```python
import functools
import math

import jax
import jax.numpy as jnp
from jax import lax
from jax.experimental import pallas as pl
from jax.experimental.pallas import tpu as pltpu
from jax.sharding import Mesh
from jax.sharding import PartitionSpec as P

epsilon = 1e-05
row_axes = ("y", "x")
group_axes = ("z", "c")
seq_axes = ("o", "z", "c")
team_axes = ("y", "x", "z", "c")
bf16 = jnp.bfloat16
f32 = jnp.float32
lanes = 128
huge_step = 1e6
vmem_bytes = 48 * 1024 * 1024


def apply_silu(values):
    return values * jax.nn.sigmoid(values)


def silu_slope(values):
    sigmoid_of = jax.nn.sigmoid(values)
    return sigmoid_of * (1.0 + values * (1.0 - sigmoid_of))


def softplus(values):
    tail = jnp.exp(-jnp.abs(values))
    series = tail * (1.0 + tail * (-1 / 2 + tail * (1 / 3 + tail * (-1 / 4 + tail * (1 / 5 - tail * (1 / 6))))))
    return jnp.maximum(values, 0.0) + jnp.where(tail < 0.05, series, jnp.log(1.0 + tail))


def dot(a, b, contract):
    return lax.dot_general(a, b, (contract, ((), ())), preferred_element_type=f32)


def chosen(values, label, mods, axis=1):
    wide = values.shape[axis] // mods
    parts = [lax.slice_in_dim(values, m * wide, (m + 1) * wide, axis=axis) for m in range(mods)]
    picked = parts[0]
    for m in range(1, mods):
        picked = jnp.where(label == m, parts[m], picked)
    return picked


def placed(values, label, mods, axis=1):
    wide = values.astype(f32)
    return jnp.concatenate([jnp.where(label == m, wide, 0.0) for m in range(mods)], axis=axis).astype(values.dtype)


start_column, label_column, fact_columns = 3, 4, 8


def columns_of(facts):
    missing = facts.shape[1] - facts.shape[0]
    return jnp.transpose(jnp.concatenate([facts, jnp.zeros((missing, facts.shape[1]), f32)], axis=0))


def label_column_of(facts_ref):
    return jnp.concatenate(
        [columns_of(facts_ref[j])[:, label_column : label_column + 1] for j in range(facts_ref.shape[0])], axis=0
    )


params = functools.partial(pltpu.CompilerParams, vmem_limit_bytes=vmem_bytes)


def everything(array):
    return pl.BlockSpec(array.shape, lambda i, rank=len(array.shape): (0,) * rank)


def scalars():
    return pl.BlockSpec(memory_space=pltpu.SMEM)


def shape(dims, dtype):
    return jax.ShapeDtypeStruct(dims, dtype)


def cost(flops, nbytes):
    return pl.CostEstimate(flops=int(flops), bytes_accessed=int(nbytes), transcendentals=0)


def assemble(weight_ref, whole):
    pieces, mods, some, wide = weight_ref.shape
    for i in range(pieces):
        for m in range(mods):
            whole[i * some : (i + 1) * some, m * wide : (m + 1) * wide] = weight_ref[i, m]


def lead_kernel(mods, places, x_ref, facts_ref, weight_ref, out_ref, whole):
    @pl.when(pl.program_id(0) == 0)
    def _():
        assemble(weight_ref, whole)

    some, here, wide = x_ref.shape
    label = label_column_of(facts_ref)
    picked = chosen(dot(x_ref[...].reshape(some * here, wide), whole[...], ((1,), (0,))), label, mods)
    for j in range(some):
        out_ref[places[pl.program_id(0) * some + j]] = picked[j * here : (j + 1) * here].astype(out_ref.dtype)


def lead_product(places, x, facts, weight, dtype):
    pieces, here, wide = x.shape
    groups, mods, some, mine = weight.shape
    outs = [shape((pieces, here, mine), dtype), shape((groups * some, mods * mine), bf16)]
    return pl.pallas_call(
        functools.partial(lead_kernel, mods),
        grid=(pieces // 4,),
        in_specs=[
            scalars(),
            pl.BlockSpec((4, here, wide), lambda i: (i, 0, 0)),
            pl.BlockSpec((4, fact_columns, here), lambda i: (i, 0, 0)),
            everything(weight),
        ],
        out_specs=[everything(out) for out in outs],
        out_shape=outs,
        compiler_params=params(),
        cost_estimate=cost(2 * pieces * here * wide * mods * mine, 2 * pieces * here * wide),
        name="lead_product",
    )(places, x, facts, weight)


def lead_pieces_kernel(mods, count, places, facts_ref, weight_ref, *refs):
    pieces = refs[:count]
    out_ref, whole, all_ref, buffer, in_sems, out_sems = refs[count:]
    _, some, here, wide = buffer.shape
    assemble(weight_ref, whole)

    def fetch(i):
        return [
            pltpu.make_async_copy(pieces[i * some + j], buffer.at[i % 2, j], in_sems.at[i % 2, j]) for j in range(some)
        ]

    def store(i):
        return pltpu.make_async_copy(buffer.at[i % 2], all_ref.at[pl.ds(i * some, some)], out_sems.at[i % 2])

    steps = count // some
    for copy in fetch(0):
        copy.start()
    for i in range(steps):
        if i + 1 < steps:
            if i:
                store(i - 1).wait()
            for copy in fetch(i + 1):
                copy.start()
        for copy in fetch(i):
            copy.wait()
        store(i).start()
        label = label_column_of(facts_ref.at[i * some : (i + 1) * some])
        picked = chosen(dot(buffer[i % 2].reshape(some * here, wide), whole[...], ((1,), (0,))), label, mods)
        for j in range(some):
            out_ref[places[i * some + j]] = picked[j * here : (j + 1) * here].astype(out_ref.dtype)
    for i in range(max(steps - 2, 0), steps):
        store(i).wait()


def lead_pieces(places, pieces, facts, weight, dtype):
    here, wide = pieces[0].shape
    count, some = len(pieces), 4
    groups, mods, features, mine = weight.shape
    outs = [
        shape((count, here, mine), dtype),
        shape((groups * features, mods * mine), bf16),
        shape((count, here, wide), bf16),
    ]
    vmem, there = pl.BlockSpec(memory_space=pltpu.VMEM), pl.BlockSpec(memory_space=pl.ANY)
    return pl.pallas_call(
        functools.partial(lead_pieces_kernel, mods, count),
        in_specs=[scalars(), vmem, vmem] + [there] * count,
        out_specs=[vmem, vmem, there],
        out_shape=outs,
        scratch_shapes=[
            pltpu.VMEM((2, some, here, wide), bf16),
            pltpu.SemaphoreType.DMA((2, some)),
            pltpu.SemaphoreType.DMA((2,)),
        ],
        compiler_params=params(),
        cost_estimate=cost(2 * count * here * wide * mods * mine, 4 * count * here * wide),
        name="lead_pieces",
    )(places, facts, weight, *pieces)


def trail_kernel(mods, count, first, *refs):
    lefts, facts_ref, weights = refs[:count], refs[count], refs[count + 1 : 2 * count + 1]
    outs = refs[2 * count + 1 :]
    some, here, mine = lefts[0].shape
    label = label_column_of(facts_ref)
    total = None
    for left, weight in zip(lefts, weights):
        term = dot(placed(left[...].reshape(some * here, mine), label, mods), weight[...], ((1,), (1,)))
        total = term if total is None else total + term
    total = total.astype(bf16).reshape(some, here, -1)
    if len(outs) == 1:
        outs[0][...] = total
    else:
        for i, out in enumerate(outs):

            @pl.when(pl.program_id(0) == i)
            def _():
                out[...] = total


def trail_product(lefts, facts, weights, mods, k=None):
    pieces, here, mine = lefts[0].shape
    features = weights[0].shape[0]
    if k is None:
        steps, outs = pieces // 4, [shape((pieces, here, features), bf16)]
        out_specs = [pl.BlockSpec((4, here, features), lambda i: (i, 0, 0))]

        def block(i):
            return (i, 0, 0)
    else:
        steps, outs = 2, [shape((4, here, features), bf16)] * 2
        out_specs = [everything(out) for out in outs]

        def block(i):
            return (2 * k + 1 - i, 0, 0)

    return pl.pallas_call(
        functools.partial(trail_kernel, mods, len(lefts), k),
        grid=(steps,),
        in_specs=[pl.BlockSpec((4, here, mine), block) for _ in lefts]
        + [pl.BlockSpec((4, fact_columns, here), block)]
        + [everything(weight) for weight in weights],
        out_specs=out_specs,
        out_shape=outs,
        compiler_params=params(),
        cost_estimate=cost(
            8 * steps * here * features * mods * mine * len(lefts), 8 * steps * here * features
        ),
        name="trail_product",
    )(*lefts, facts, *weights)


def grad_kernel(mods, x_ref, d_ref, facts_ref, out_ref, spread):
    pieces, here, mine = d_ref.shape

    @pl.when(pl.program_id(0) == 0)
    def _():
        for i in range(pieces):
            label = columns_of(facts_ref[i])[:, label_column : label_column + 1]
            spread[i * here : (i + 1) * here] = placed(d_ref[i], label, mods)

    out_ref[0] = dot(x_ref[...], spread[...], ((0,), (0,))).astype(out_ref.dtype)


def feature_grad(x, d, facts, mods, groups, dtype):
    pieces, here, wide = x.shape
    mine = d.shape[2]
    some = min(256, wide)
    out = shape((wide // some, some, mods * mine), dtype)
    grad = pl.pallas_call(
        functools.partial(grad_kernel, mods),
        grid=(wide // some,),
        in_specs=[
            pl.BlockSpec((pieces * here, some), lambda i: (0, i)),
            everything(d),
            everything(facts),
        ],
        out_specs=pl.BlockSpec((1, some, mods * mine), lambda i: (i, 0, 0)),
        out_shape=out,
        scratch_shapes=[pltpu.VMEM((pieces * here, mods * mine), bf16)],
        compiler_params=params(),
        cost_estimate=cost(6 * pieces * here * wide * mods * mine, 2 * pieces * here * wide),
        name="feature_grad",
    )(x.reshape(pieces * here, wide), d, facts)
    return grad.reshape(groups, wide // groups, mods * mine)


def settle_kernel(got_ref, weight_ref, out_ref, sum_ref):
    mods, _, mine = out_ref.shape

    @pl.when(pl.program_id(0) == 0)
    def _():
        sum_ref[...] = jnp.zeros_like(sum_ref)

    for m in range(mods):
        grad = got_ref[0, :, m * mine : (m + 1) * mine].astype(f32)
        out_ref[m] = grad
        sum_ref[...] += grad * weight_ref[m].astype(f32)


def settle(got, weight):
    sources, some, columns = got.shape
    mods, _, wide = weight.shape
    mine = wide // sources
    item = pl.BlockSpec((mods, some, mine), lambda i: (0, 0, i))
    outs = [shape(weight.shape, f32), shape((some, mine), f32)]
    return pl.pallas_call(
        settle_kernel,
        grid=(sources,),
        in_specs=[pl.BlockSpec((1, some, columns), lambda i: (i, 0, 0)), item],
        out_specs=[item, everything(outs[1])],
        out_shape=outs,
        compiler_params=params(),
        cost_estimate=cost(0, 8 * mods * some * wide),
        name="settle",
    )(got, weight)


def conv_kernel(mods, conv_ref, before_ref, facts_ref, row_label_ref, taps_ref, bias_ref, xdt_ref, xbc_ref, pre_ref, proj_ref, carried, line):
    rows, here, mine = conv_ref.shape

    @pl.when(pl.program_id(0) == 0)
    def _():
        carried[...] = before_ref[...]

    for r in range(rows):
        block = conv_ref[r].astype(f32)
        line[:8] = carried[r]
        line[8:] = block
        facts = columns_of(facts_ref[r, 0])
        pre = bias_ref[...] + taps_ref[0:1] * block
        for lag in range(1, taps_ref.shape[0]):
            pre = pre + taps_ref[lag : lag + 1] * (facts[:, lag - 1 : lag] * line[8 - lag : 8 - lag + here])
        carried[r] = block[here - 8 :]
        pre_ref[r] = pre
        low = apply_silu(pre).astype(bf16)
        wide = chosen(dot(low, xdt_ref[...], ((1,), (0,))), facts[:, label_column : label_column + 1], mods)
        small = chosen(dot(xbc_ref[...], low, ((1,), (1,))), row_label_ref[0, r : r + 1], mods, 0)
        proj_ref[r, 0, :here] = wide.astype(bf16)
        proj_ref[r, 0, here:] = small.astype(bf16)


def conv_block(conv_in, before, facts, row_label, taps, bias, xdt, xbc):
    rows, length, mine = conv_in.shape
    blocks, _, here = row_label.shape
    mods = xdt.shape[1] // here
    narrow = xbc.shape[0] // mods
    item = pl.BlockSpec((rows, here, mine), lambda i: (0, i, 0))
    return pl.pallas_call(
        functools.partial(conv_kernel, mods),
        grid=(blocks,),
        in_specs=[
            item,
            everything(before),
            pl.BlockSpec((rows, 1, fact_columns, here), lambda i: (0, i, 0, 0)),
            pl.BlockSpec((1, rows, here), lambda i: (i, 0, 0)),
        ]
        + [everything(array) for array in (taps, bias, xdt, xbc)],
        out_specs=[item, pl.BlockSpec((rows, 1, here + narrow, here), lambda i: (0, i, 0, 0))],
        out_shape=[shape(conv_in.shape, f32), shape((rows, blocks, here + narrow, here), bf16)],
        scratch_shapes=[pltpu.VMEM((rows, 8, mine), f32), pltpu.VMEM((8 + here, mine), f32)],
        compiler_params=params(),
        cost_estimate=cost(20000 * rows * length * mine, 10 * rows * length * mine),
        name="conv_block",
    )(conv_in, before, facts, row_label, taps, bias, xdt, xbc)


def coefficient_lines(proj_ref, rows, here, line):
    narrow = proj_ref.shape[2] - here
    for r in range(rows):
        small = proj_ref[r, 0, here:].astype(f32)
        small = jnp.concatenate([small, jnp.zeros((here - narrow, here), f32)], axis=0)
        turned = jnp.transpose(small)
        line[r * here : (r + 1) * here] = turned
        line[(rows + r) * here : (rows + r + 1) * here] = pltpu.roll(turned, here - narrow // 2, 1)


def scan_lines(r, rows, here, value, line):
    line[r * here : (r + 1) * here] = value
    line[(rows + r) * here : (rows + r + 1) * here] = value


def forward_kernel(
    mods, proj_ref, pre_ref, facts_ref, gate_ref, dtw_ref, dtb_ref, rate_ref, skip_ref, start_ref,
    gated_ref, scanned_ref, dt_ref, kept_ref, end_ref, held, step_line, drive_line, coef_line, out_line,
):
    rows, here, mine = pre_ref.shape
    pieces, subl, _ = rate_ref.shape

    @pl.when(pl.program_id(0) == 0)
    def _():
        held[...] = start_ref[...]

    coefficient_lines(proj_ref, rows, here, coef_line)
    for r in range(rows):
        facts = columns_of(facts_ref[r, 0])
        label = facts[:, label_column : label_column + 1]
        dt_pre = chosen(dot(proj_ref[r, 0, :here], dtw_ref[...], ((1,), (0,))) + dtb_ref[...], label, mods)
        dt_ref[r] = dt_pre
        step = softplus(dt_pre)
        scan_lines(r, rows, here, step * apply_silu(pre_ref[r]), drive_line)
        scan_lines(r, rows, here, jnp.where(facts[:, start_column : start_column + 1] > 0, huge_step, step), step_line)

    def one(t, state):
        lines = pl.ds(t, subl, stride=here)
        step, drive, coefs = step_line[lines, :], drive_line[lines, :], coef_line[lines, :]
        emitted = None
        following = []
        for j in range(pieces):
            kept_ref[t, j] = state[j]
            decay = jnp.exp2(step * rate_ref[j])
            now = decay * state[j] + drive * jnp.broadcast_to(coefs[:, j : j + 1], step.shape)
            term = now * jnp.broadcast_to(coefs[:, pieces + j : pieces + j + 1], step.shape)
            emitted = term if emitted is None else emitted + term
            following.append(now)
        out_line[lines, :] = emitted
        return tuple(following)

    def eight(block, state):
        for i in range(8):
            state = one(block * 8 + i, state)
        return state

    state = lax.fori_loop(0, here // 8, eight, tuple(held[j] for j in range(pieces)))
    for j in range(pieces):
        held[j] = state[j]
        end_ref[j] = state[j]
    for r in range(rows):
        emitted = out_line[r * here : (r + 1) * here] + out_line[(rows + r) * here : (rows + r + 1) * here]
        scanned = emitted + skip_ref[...] * apply_silu(pre_ref[r])
        scanned_ref[r] = scanned
        gated_ref[r] = (scanned * apply_silu(gate_ref[r])).astype(bf16)


def scan_forward(proj, pre, facts, gate, dtw, dtb, rates2, skip, start):
    rows, length, mine = pre.shape
    _, blocks, deep, here = proj.shape
    pieces, subl, _ = rates2.shape
    item = pl.BlockSpec((rows, here, mine), lambda i: (0, i, 0))
    line = pltpu.VMEM((subl * here, mine), f32)
    return pl.pallas_call(
        functools.partial(forward_kernel, dtw.shape[1] // mine),
        grid=(blocks,),
        in_specs=[
            pl.BlockSpec((rows, 1, deep, here), lambda i: (0, i, 0, 0)),
            item,
            pl.BlockSpec((rows, 1, fact_columns, here), lambda i: (0, i, 0, 0)),
            item,
        ]
        + [everything(array) for array in (dtw, dtb, rates2, skip, start)],
        out_specs=[
            item,
            item,
            item,
            pl.BlockSpec((here, pieces, subl, mine), lambda i: (i, 0, 0, 0)),
            everything(start),
        ],
        out_shape=[
            shape(pre.shape, bf16),
            shape(pre.shape, f32),
            shape(pre.shape, f32),
            shape((length, pieces, subl, mine), f32),
            shape(start.shape, f32),
        ],
        scratch_shapes=[pltpu.VMEM(start.shape, f32), line, line, line, line],
        compiler_params=params(),
        cost_estimate=cost(5500 * length * pieces * subl * mine, 5 * length * pieces * subl * mine),
        name="scan_forward",
    )(proj, pre, facts, gate, dtw, dtb, rates2, skip, start)


def backward_kernel(
    mods, tables, proj_ref, pre_ref, facts_ref, gate_ref, scanned_ref, dt_ref, d_gated_ref, kept_ref, dtw_ref, rate2_ref,
    rate_ref, skip_ref, last_ref, carry_ref, sum_ref, d_gate_ref, d_proj_ref, d_act_ref, dtw_grad_ref, dtb_grad_ref,
    skip_grad_ref, rate_sum_ref, carry_out_ref, carried, later, products, step_line, drive_line, coef_line, back_line,
    pulled_line, weighted_line, small_line,
):
    rows, here, mine = pre_ref.shape
    blocks = tables.shape[0] // rows
    narrow = proj_ref.shape[2] - here
    pieces, subl, _ = rate_ref.shape
    place = blocks - 1 - pl.program_id(0)

    @pl.when(pl.program_id(0) == 0)
    def _():
        carried[...] = carry_ref[...]
        later[...] = last_ref[...]
        for ref in (rate_sum_ref, dtw_grad_ref, dtb_grad_ref, skip_grad_ref):
            ref[...] = jnp.zeros_like(ref)

    coefficient_lines(proj_ref, rows, here, coef_line)
    for r in range(rows):
        facts = columns_of(facts_ref[r, 0])
        step, activated = softplus(dt_ref[r]), apply_silu(pre_ref[r])
        gate, d_gated = gate_ref[r], d_gated_ref[r]
        d_scan = d_gated * apply_silu(gate)
        d_gate_ref[tables[r * blocks + place]] = (d_gated * scanned_ref[r] * silu_slope(gate)).astype(bf16)
        skip_grad_ref[...] += jnp.sum(d_scan * activated, axis=0, keepdims=True)
        scan_lines(r, rows, here, d_scan, back_line)
        scan_lines(r, rows, here, step * activated, drive_line)
        scan_lines(r, rows, here, jnp.where(facts[:, start_column : start_column + 1] > 0, huge_step, step), step_line)

    def one(t, carry, state):
        lines = pl.ds(t, subl, stride=here)
        step, drive, coefs, back = step_line[lines, :], drive_line[lines, :], coef_line[lines, :], back_line[lines, :]
        pulled_sum, weighted_sum = None, None
        new_carry, new_state, terms, sums = [], [], [], []
        for j in range(pieces):
            before = kept_ref[t, j]
            decay = jnp.exp2(step * rate2_ref[j])
            adjoint = back * jnp.broadcast_to(coefs[:, pieces + j : pieces + j + 1], step.shape) + carry[j]
            passed = decay * adjoint
            pulled = passed * before
            weighted = adjoint * jnp.broadcast_to(coefs[:, j : j + 1], step.shape)
            first = pulled * rate_ref[j]
            pulled_sum = first if pulled_sum is None else pulled_sum + first
            weighted_sum = weighted if weighted_sum is None else weighted_sum + weighted
            terms.append((adjoint * drive, back * state[j]))
            sums.append(pulled * step)
            new_carry.append(passed)
            new_state.append(before)
        pulled_line[lines, :] = pulled_sum
        weighted_line[lines, :] = weighted_sum
        return new_carry, new_state, terms, sums

    def eight(k, loop):
        carry, state, rates = loop
        block = here // 8 - 1 - k
        rates = list(rates)
        for i in (6, 4, 2, 0):
            t = block * 8 + i
            carry, state, terms_b, sums_b = one(t + 1, carry, state)
            carry, state, terms_a, sums_a = one(t, carry, state)
            spot = pl.ds(pl.multiple_of(t * subl, 16), 16)
            for j in range(pieces):
                rates[j] = rates[j] + (sums_a[j] + sums_b[j])
                for part in range(2):
                    column = (part * pieces + j) * mine
                    products[spot, column : column + mine] = jnp.concatenate(
                        [terms_a[j][part], terms_b[j][part]], axis=0
                    ).astype(bf16)
        return tuple(carry), tuple(state), tuple(rates)

    begin = tuple(tuple(ref[j] for j in range(pieces)) for ref in (carried, later, rate_sum_ref))
    carry, state, rates = lax.fori_loop(0, here // 8, eight, begin)
    for j in range(pieces):
        carried[j] = carry[j]
        later[j] = state[j]
        rate_sum_ref[j] = rates[j]
        carry_out_ref[j] = carry[j]
    small_line[...] = dot(products[...], sum_ref[...], ((1,), (0,)))
    for r in range(rows):
        label = columns_of(facts_ref[r, 0])[:, label_column : label_column + 1]
        dt_pre, activated = dt_ref[r], apply_silu(pre_ref[r])
        near, far = slice(r * here, (r + 1) * here), slice((rows + r) * here, (rows + r + 1) * here)
        weighted = weighted_line[near] + weighted_line[far]
        d_step = pulled_line[near] + pulled_line[far] + activated * weighted
        d_act_ref[r] = back_line[near] * skip_ref[...] + softplus(dt_pre) * weighted
        d_dt = placed((d_step * jax.nn.sigmoid(dt_pre)).astype(bf16), label, mods)
        dtw_grad_ref[...] += dot(proj_ref[r, 0, :here], d_dt, ((0,), (0,)))
        dtb_grad_ref[...] += jnp.sum(d_dt.astype(f32), axis=0, keepdims=True)
        d_proj_ref[r, 0, :here] = dot(d_dt, dtw_ref[...], ((1,), (1,))).astype(bf16)
        one_half = small_line[pl.ds(r, here, stride=subl), :]
        other_half = small_line[pl.ds(rows + r, here, stride=subl), :]
        small = jnp.transpose(one_half + pltpu.roll(other_half, narrow // 2, 1))
        d_proj_ref[r, 0, here:] = small[:narrow].astype(bf16)


def scan_backward(tables, proj, pre, facts, gate, scanned, dt_pre, d_gated, kept, dtw, rates2, rates, skip, last, carry):
    rows, length, mine = pre.shape
    _, blocks, deep, here = proj.shape
    pieces, subl, _ = rates2.shape
    item = pl.BlockSpec((rows, here, mine), lambda i: (0, blocks - 1 - i, 0))
    proj_item = pl.BlockSpec((rows, 1, deep, here), lambda i: (0, blocks - 1 - i, 0, 0))
    columns = 2 * pieces * mine
    summing = (jnp.arange(columns)[:, None] // mine == jnp.arange(lanes)[None, :]).astype(bf16)
    d_gate = shape((rows * blocks, here, mine), bf16)
    line = pltpu.VMEM((subl * here, mine), f32)
    small = [shape((here, dtw.shape[1]), f32), shape((1, dtw.shape[1]), f32), shape((1, mine), f32), shape(carry.shape, f32)]
    return pl.pallas_call(
        functools.partial(backward_kernel, dtw.shape[1] // mine),
        grid=(blocks,),
        in_specs=[
            scalars(),
            proj_item,
            item,
            pl.BlockSpec((rows, 1, fact_columns, here), lambda i: (0, blocks - 1 - i, 0, 0)),
            item,
            item,
            item,
            item,
            pl.BlockSpec((here, pieces, subl, mine), lambda i: (blocks - 1 - i, 0, 0, 0)),
        ]
        + [everything(array) for array in (dtw, rates2, rates, skip, last, carry, summing)],
        out_specs=[everything(d_gate), proj_item, item] + [everything(array) for array in small + [carry]],
        out_shape=[d_gate, shape(proj.shape, bf16), shape(pre.shape, f32)] + small + [shape(carry.shape, f32)],
        scratch_shapes=[pltpu.VMEM(carry.shape, f32)] * 2 + [pltpu.VMEM((subl * here, columns), bf16)] + [line] * 7,
        compiler_params=params(),
        cost_estimate=cost(7500 * length * pieces * subl * mine, 5 * length * pieces * subl * mine),
        name="scan_backward",
    )(tables, proj, pre, facts, gate, scanned, dt_pre, d_gated, kept, dtw, rates2, rates, skip, last, carry, summing)


def deconv_kernel(
    mods, tables, d_proj_ref, conv_ref, pre_ref, d_act_ref, facts_ref, row_label_ref, taps_ref, xdt_ref, xbc_ref,
    d_conv_ref, xdt_grad_ref, xbc_grad_ref, taps_grad_ref, bias_grad_ref, head_ref, tail_ref, carried, line,
):
    rows, here, mine = pre_ref.shape
    blocks = tables.shape[0] // rows
    taps = taps_ref.shape[0]
    place = blocks - 1 - pl.program_id(0)

    @pl.when(pl.program_id(0) == 0)
    def _():
        carried[...] = jnp.zeros_like(carried)
        for ref in (xdt_grad_ref, xbc_grad_ref, taps_grad_ref, bias_grad_ref):
            ref[...] = jnp.zeros_like(ref)

    for r in range(rows):
        facts = columns_of(facts_ref[r, 0])
        pre = pre_ref[r]
        low = apply_silu(pre).astype(bf16)
        d_rank = placed(d_proj_ref[r, 0, :here], facts[:, label_column : label_column + 1], mods)
        d_small = placed(d_proj_ref[r, 0, here:], row_label_ref[0, r : r + 1], mods, 0)
        xdt_grad_ref[...] += dot(low, d_rank, ((0,), (0,)))
        xbc_grad_ref[...] += dot(d_small, low, ((1,), (0,)))
        d_act = d_act_ref[r] + dot(d_rank, xdt_ref[...], ((1,), (1,))) + dot(d_small, xbc_ref[...], ((0,), (0,)))
        d_pre = d_act * silu_slope(pre)
        source = conv_ref[r].astype(f32)
        total = taps_ref[0:1] * d_pre
        bias_grad_ref[...] += jnp.sum(d_pre, axis=0, keepdims=True)
        taps_grad_ref[0:1] += jnp.sum(source * d_pre, axis=0, keepdims=True)
        for lag in range(1, taps):
            kept = facts[:, lag - 1 : lag] * d_pre
            line[:here] = kept
            line[here:] = carried[r, lag - 1]
            carried[r, lag - 1] = kept[:8]
            moved = line[lag : lag + here]
            total = total + taps_ref[lag : lag + 1] * moved
            taps_grad_ref[lag : lag + 1] += jnp.sum(source * moved, axis=0, keepdims=True)
        d_conv_ref[tables[r * blocks + place]] = total.astype(bf16)

        @pl.when(pl.program_id(0) == 0)
        def _():
            tail_ref[r] = total[here - 8 :]

    head_ref[...] = carried[...]


def deconv_block(tables, d_proj, conv_in, pre, d_act, facts, row_label, taps, xdt, xbc):
    rows, length, mine = pre.shape
    _, blocks, deep, here = d_proj.shape
    item = pl.BlockSpec((rows, here, mine), lambda i: (0, blocks - 1 - i, 0))
    outs = [
        shape((rows * blocks, here, mine), bf16),
        shape(xdt.shape, f32),
        shape(xbc.shape, f32),
        shape(taps.shape, f32),
        shape((1, mine), f32),
        shape((rows, taps.shape[0] - 1, 8, mine), f32),
        shape((rows, 8, mine), f32),
    ]
    return pl.pallas_call(
        functools.partial(deconv_kernel, xdt.shape[1] // here),
        grid=(blocks,),
        in_specs=[
            scalars(),
            pl.BlockSpec((rows, 1, deep, here), lambda i: (0, blocks - 1 - i, 0, 0)),
            item,
            item,
            item,
            pl.BlockSpec((rows, 1, fact_columns, here), lambda i: (0, blocks - 1 - i, 0, 0)),
            pl.BlockSpec((1, rows, here), lambda i: (blocks - 1 - i, 0, 0)),
        ]
        + [everything(array) for array in (taps, xdt, xbc)],
        out_specs=[everything(array) for array in outs],
        out_shape=outs,
        scratch_shapes=[pltpu.VMEM(outs[5].shape, f32), pltpu.VMEM((here + 8, mine), f32)],
        compiler_params=params(),
        cost_estimate=cost(30000 * rows * length * mine, 14 * rows * length * mine),
        name="deconv_block",
    )(tables, d_proj, conv_in, pre, d_act, facts, row_label, taps, xdt, xbc)


def passed_along(value, axis, by):
    size = lax.axis_size(axis)
    return lax.ppermute(value, axis, [(i, i + by) for i in range(size) if 0 <= i + by < size])


def shifted(value, by):
    size = lax.axis_size("z")
    return value if by % size == 0 else lax.ppermute(value, "z", [(i, (i + by) % size) for i in range(size)])


def swapped(value):
    return lax.ppermute(value, "c", [(0, 1), (1, 0)])


def hop(value, second):
    depth = lax.axis_size("z")

    def place(y, x, z, c):
        return ((y * 2 + x) * depth + z) * 2 + c

    pairs = [
        (place(y, x, z, c), place(y, 1 - x, z, c) if (c == 1) == second else place(1 - y, x, z, c))
        for y in range(2)
        for x in range(2)
        for z in range(depth)
        for c in range(2)
    ]
    return lax.ppermute(value, team_axes, pairs)


def relative_places():
    depth = lax.axis_size("z")
    y, x, z, c = (lax.axis_index(name) for name in team_axes)
    n = jnp.arange(4)[None, None, :]
    core = (c + jnp.arange(2)[None, :, None]) % 2
    back = (z - jnp.arange(depth)[:, None, None]) % depth
    one, two = n % 2, n // 2
    flip_x = jnp.where(core == 0, one, two)
    flip_y = jnp.where(core == 0, two, one)
    return (((((y + flip_y) % 2) * 2 + (x + flip_x) % 2) * depth + back) * 2 + core).reshape(-1)


def team_gather(value):
    parts = []
    for k in range(lax.axis_size("z")):
        near = shifted(value, k)
        first, second = hop(near, False), hop(near, True)
        pieces = [near, first, second, hop(first, True)]
        parts += pieces + [swapped(piece) for piece in pieces]
    return parts


def team_scatter(made):
    total = None
    depth = lax.axis_size("z")

    def added(*terms):
        return sum(term.astype(f32) for term in terms)

    for k in list(range(1, depth)) + [0]:
        far, near = made(k)
        far = swapped(far)
        come = hop(added(near[2:], far[2:]).astype(bf16), True)
        last = hop(added(near[1], far[1], come[1]).astype(bf16), False)
        held = added(near[0], far[0], come[0], last)
        if k:
            held = shifted(held.astype(bf16), -k).astype(f32)
        total = held if total is None else total + held
    return total


def exchanged(parts):
    return lax.all_to_all(parts, group_axes, 0, 0, tiled=True)


def spread_weight(weight):
    outer, group = lax.axis_size("o"), lax.axis_size(group_axes)
    mods, here, wide = weight.shape
    each = wide // (outer * group)
    parts = weight.reshape(mods, here, outer, group, each)
    parts = jnp.transpose(parts, (3, 0, 1, 2, 4)).reshape(group, mods, here, outer * each)
    return parts


def spread_done(parts):
    got = exchanged(parts)
    return got if lax.axis_size("o") == 1 else lax.all_gather(got, "o", axis=0, tiled=True)


def collect_grad(parts, weight):
    outer, group = lax.axis_size("o"), lax.axis_size(group_axes)
    mods, here, wide = weight.shape
    if outer > 1:
        parts = lax.psum_scatter(parts, "o", scatter_dimension=0, tiled=True)
    got = exchanged(parts.astype(bf16))
    if outer == 1:
        grad, sums = settle(got, weight)
        return grad, jnp.sum(sums, axis=1)
    got = got.astype(f32).reshape(group, here, mods, outer, wide // (outer * group))
    grad = jnp.transpose(got, (2, 1, 3, 0, 4)).reshape(weight.shape)
    return grad, jnp.sum(grad * weight.astype(f32), axis=(0, 2))


def outer_gathered(value, axis):
    return value if lax.axis_size("o") == 1 else lax.all_gather(value, "o", axis=axis, tiled=True)


def outer_summed(value, axis):
    if lax.axis_size("o") == 1:
        return value
    return lax.psum_scatter(value, "o", scatter_dimension=axis, tiled=True)


def half_of(value, axis, name, other):
    return lax.dynamic_index_in_dim(value, (lax.axis_index(name) + other) % 2, axis, False)


def team_sum(value):
    depth = lax.axis_size("z")
    z = lax.axis_index("z")

    def halved(value, axis, name, pairs):
        sent = lax.ppermute(half_of(value, axis, name, 1).astype(bf16), name, pairs)
        return half_of(value, axis, name, 0).astype(f32) + sent.astype(f32)

    swap = [(0, 1), (1, 0)]
    held = halved(value, 3, "c", swap)
    held = halved(held, 0, "y", swap)
    held = halved(held, 0, "x", swap)
    own = lax.dynamic_index_in_dim(held, z, 0, False)
    for k in range(1, depth):
        own = own + shifted(lax.dynamic_index_in_dim(held, (z + k) % depth, 0, False).astype(bf16), k).astype(f32)
    own = own.astype(bf16)
    back = jnp.stack([own] + [shifted(own, k) for k in range(1, depth)])
    rolled = back[(z - jnp.arange(depth)) % depth]

    def doubled(value, axis, name):
        other = lax.ppermute(value, name, swap)
        flag = lax.axis_index(name) == 0
        return jnp.stack([jnp.where(flag, value, other), jnp.where(flag, other, value)], axis=axis)

    return doubled(doubled(doubled(rolled, 0, "x"), 0, "y"), 3, "c")


def entering_state(passing, local_end, backward):
    count, place = lax.axis_size("o"), lax.axis_index("o")
    decays = lax.all_gather(passing.astype(bf16), "o")
    ends = lax.all_gather(local_end.astype(bf16), "o")
    state = jnp.zeros_like(local_end)
    for i in range(count):
        source = count - 1 - i if backward else i
        ahead = source > place if backward else source < place
        state = jnp.where(ahead, decays[source].astype(f32) * state + ends[source].astype(f32), state)
    return state


def on_device(
    tokens,
    cotangent,
    modality,
    starts,
    row_lengths,
    norm_gain,
    in_x_weight,
    in_z_weight,
    xdt_weight,
    xbc_weight,
    dt_weight,
    dt_bias,
    conv_weight,
    conv_bias,
    log_rates,
    skip_gain,
    out_weight,
):
    outer, group = lax.axis_size("o"), lax.axis_size(group_axes)
    rows, here = modality.shape
    width = tokens.shape[-1]
    mods = in_x_weight.shape[1]
    taps, states, rank = conv_weight.shape[0], log_rates.shape[0], dt_weight.shape[0]
    margin = taps - 1
    local_len = group * here
    own_row = lax.axis_index(row_axes)
    count = rows * local_len

    depth = lax.axis_size("z")
    place_z = lax.axis_index("z")

    def lead(weight):
        return jnp.transpose(weight, (1, 0, 2))

    features = norm_gain.shape[0]
    packed = jnp.concatenate(
        [modality.astype(f32).reshape(-1), starts.astype(f32).reshape(-1), norm_gain.astype(f32)]
    )
    packed = jnp.stack([packed] + [shifted(packed, k) for k in range(1, depth)])
    packed = packed[(place_z - jnp.arange(depth)) % depth]
    others, first_core = swapped(packed), lax.axis_index("c") == 0
    packed = jnp.stack([jnp.where(first_core, packed, others), jnp.where(first_core, others, packed)], axis=1)
    labels = packed[:, :, : 2 * rows * here].astype(jnp.int32).reshape(depth, 2, 2, rows, here)
    labels = jnp.transpose(labels, (2, 3, 0, 1, 4)).reshape(2, rows, local_len)
    modality, starts = labels[0], labels[1]
    gain = outer_gathered(packed[:, :, 2 * rows * here :].reshape(-1, features), 0).reshape(width)

    inputs = tokens[0].astype(f32)
    inv_rms = lax.rsqrt(jnp.mean(inputs * inputs, axis=-1, keepdims=True) + epsilon)
    scaled = inputs * inv_rms
    normed_pieces = team_gather((scaled * gain).astype(bf16))
    wx = spread_done(spread_weight(lead(in_x_weight)))
    wz_parts, wo_parts = in_z_weight, out_weight
    wz_parts, wx = lax.optimization_barrier((wz_parts, wx))
    wz = spread_done(spread_weight(lead(wz_parts)))
    wo_parts, wz = lax.optimization_barrier((wo_parts, wz))
    wo = spread_done(spread_weight(lead(wo_parts)))
    position = lax.axis_index(seq_axes) * here + jnp.arange(here, dtype=jnp.int32)
    own_valid = (position < lax.dynamic_index_in_dim(row_lengths, own_row, 0, False)).astype(f32)[:, None]
    upstream = cotangent[0].astype(f32)
    own_back = (upstream * own_valid).astype(bf16)
    own_back, normed_pieces[-1] = lax.optimization_barrier((own_back, normed_pieces[-1]))
    d_branch = lax.all_gather(own_back, team_axes)
    xdt = outer_gathered(xdt_weight, 0)
    xbc = outer_gathered(xbc_weight, 2)
    dtw = outer_gathered(dt_weight, 2)
    dtb = outer_gathered(dt_bias, 1).astype(f32)
    conv_w = outer_gathered(conv_weight, 1).astype(f32)
    conv_b = outer_gathered(conv_bias, 0).astype(f32)
    log_r = outer_gathered(log_rates, 1).astype(f32)
    skip = outer_gathered(skip_gain, 0).astype(f32)
    mine = skip.shape[0]
    places = relative_places()
    pieces_of = lax.axis_size(team_axes)
    relative = jnp.zeros((pieces_of,), jnp.int32).at[places].set(jnp.arange(pieces_of, dtype=jnp.int32))

    counted = jnp.cumsum(starts, axis=1)
    send_keep = counted[:, -1:] - counted[:, local_len - margin :] == 0
    counted_ext = jnp.concatenate([jnp.zeros((rows, margin), jnp.int32), counted], axis=1)
    facts = [counted - counted_ext[:, margin - lag : margin - lag + local_len] == 0 for lag in range(1, taps)]
    facts = [f.astype(f32) for f in facts] + [starts.astype(f32), modality.astype(f32)]
    facts += [jnp.zeros_like(facts[0])] * (fact_columns - len(facts))
    facts = jnp.stack([f.reshape(rows, group, here) for f in facts], axis=2)
    row_label = jnp.transpose(modality.reshape(rows, group, here), (1, 0, 2)).astype(f32)
    facts_flat = facts.reshape(pieces_of, fact_columns, here)
    facts_there = facts_flat[places]
    in_order = jnp.arange(pieces_of, dtype=jnp.int32)

    conv_in, wx_f, normed = lead_pieces(places, normed_pieces, facts_there, wx, bf16)
    conv_in = conv_in.reshape(rows, local_len, mine)
    gate_in, wz_f = lead_product(places, normed, facts_there, wz, f32)
    gate_in = gate_in.reshape(rows, local_len, mine)
    d_gated, wo_f = lead_product(in_order, d_branch, facts_flat, wo, f32)
    d_gated = d_gated.reshape(rows, local_len, mine)

    before = jnp.zeros((rows, 8, mine), f32)
    if outer > 1:
        outgoing = jnp.where(send_keep[:, :, None], conv_in[:, local_len - margin :, :], jnp.zeros((), bf16))
        incoming = passed_along(outgoing, "o", 1).astype(f32)
        before = jnp.pad(incoming, ((0, 0), (8 - margin, 0), (0, 0)))
    halves = 2
    pieces = states // halves
    narrow = 2 * states
    xdt_f = xdt.reshape(mine, mods * rank)
    xbc_f = jnp.transpose(xbc.reshape(2, halves, pieces, mods, mine), (3, 1, 0, 2, 4)).reshape(mods * narrow, mine)
    dt_f = dtw.reshape(rank, mods * mine)
    pre, proj_part = conv_block(conv_in, before, facts, row_label, conv_w, conv_b[None], xdt_f, xbc_f)

    def summed(part):
        return team_sum(part.reshape((2, 2, depth, 2) + part.shape[2:])).reshape(part.shape)

    proj = summed(proj_part)
    decay_coef = -jnp.exp(log_r)

    def per_state(values):
        split = jnp.transpose(values.reshape(halves, pieces, mine), (1, 0, 2))
        return jnp.repeat(split, rows, axis=1)

    rates = per_state(decay_coef)
    rates2 = rates * (1.0 / math.log(2.0))
    zero_state = jnp.zeros((pieces, halves * rows, mine), f32)
    skip_row = skip[None]
    dtb_row = dtb.reshape(1, mods * mine)

    def ahead(start):
        return scan_forward(proj, pre, facts, gate_in, dt_f, dtb_row, rates2, skip_row, start)

    gated, scanned, dt_pre, kept, last_state = ahead(zero_state)
    if outer > 1:
        steps = jnp.sum(jax.nn.softplus(dt_pre), axis=1)
        unbroken = (jnp.sum(starts, axis=1) == 0).astype(f32)[:, None]
        passing = jnp.exp2(jnp.concatenate([steps] * halves, axis=0)[None] * rates2)
        passing = passing * jnp.concatenate([unbroken] * halves, axis=0)[None]
        gated, scanned, dt_pre, kept, last_state = ahead(entering_state(passing, last_state, False))
    gated = gated.reshape(pieces_of, here, mine)
    branch = trail_product([gated], facts_flat, [wo_f], mods)[0].reshape(count, width)
    own_branch = lax.psum_scatter(branch, team_axes, scatter_dimension=0, tiled=True).astype(f32)
    block_out = (inputs + own_valid * own_branch).astype(bf16)[None]
    grad_type = f32 if outer > 1 else bf16

    def weight_grad(x, d, there, weight):
        return collect_grad(feature_grad(x, d, there, mods, outer * group, grad_type), lead(weight))

    out_weight_grad = lead(weight_grad(d_branch, gated, facts_flat, out_weight)[0])

    def back(carry):
        return scan_backward(
            relative, proj, pre, facts, gate_in, scanned, dt_pre, d_gated, kept, dt_f, rates2, rates, skip_row, last_state,
            carry,
        )

    results = back(zero_state)
    if outer > 1:
        results = back(entering_state(passing, results[-1], True))
    d_gate, d_proj_part, d_act, dtw_grad, dtb_grad, skip_grad, rate_total, _ = results
    in_z_grad, gain_z = weight_grad(normed, d_gate, facts_there, in_z_weight)
    d_proj = summed(d_proj_part)
    rate_total = jnp.sum(rate_total.reshape(pieces, halves, rows, mine), axis=2)
    rate_total = jnp.transpose(rate_total, (1, 0, 2)).reshape(states, mine)
    log_rates_grad = outer_summed(decay_coef * rate_total, 1)
    skip_gain_grad = outer_summed(skip_grad[0], 0)
    dt_weight_grad = outer_summed(dtw_grad.reshape(rank, mods, mine), 2)
    dt_bias_grad = outer_summed(dtb_grad.reshape(mods, mine), 1)
    d_conv, xdt_grad, xbc_grad, taps_grad, bias_grad, head, tail = deconv_block(
        relative, d_proj, conv_in, pre, d_act, facts, row_label, conv_w, xdt_f, xbc_f
    )
    if outer > 1:
        early = jnp.stack(
            [jnp.pad(head[:, lag - 1, :lag], ((0, 0), (margin - lag, 0), (0, 0))) for lag in range(1, taps)], axis=1
        )
        taps_grad = taps_grad.at[1:].add(jnp.sum(early * incoming[:, None], axis=(0, 2)))
        returned = jnp.sum(early * conv_w[None, 1:, None, :], axis=1)
        returned = passed_along(returned.astype(bf16), "o", -1).astype(f32)
        returned = jnp.where(send_keep[:, :, None], returned, 0.0)
        fixed = (tail[:, 8 - margin :] + returned).astype(bf16)
        spots = relative[jnp.arange(rows) * group + group - 1]
        d_conv = d_conv.at[spots, here - margin :].set(fixed)
    xdt_grad = outer_summed(xdt_grad.reshape(mine, mods, rank), 0)
    xbc_grad = jnp.transpose(xbc_grad.reshape(mods, halves, 2, pieces, mine), (2, 1, 3, 0, 4)).reshape(narrow, mods, mine)
    xbc_grad = outer_summed(xbc_grad, 2)
    conv_weight_grad = outer_summed(taps_grad, 1)
    conv_bias_grad = outer_summed(bias_grad[0], 0)
    d_scaled = team_scatter(lambda k: trail_product([d_conv, d_gate], facts_there, [wx_f, wz_f], mods, k)) * gain
    in_x_grad, gain_x = weight_grad(normed, d_conv, facts_there, in_x_weight)
    d_inputs = inv_rms * (d_scaled - scaled * jnp.mean(d_scaled * scaled, axis=-1, keepdims=True))
    tokens_grad = (upstream + d_inputs).astype(bf16)[None]
    gain_part = gain_x + gain_z
    for name in row_axes:
        gain_part = gain_part + lax.ppermute(gain_part, name, [(0, 1), (1, 0)])
    norm_gain_grad = gain_part / norm_gain.astype(f32)
    in_x_grad, in_z_grad = lead(in_x_grad), lead(in_z_grad)
    return (
        block_out,
        tokens_grad,
        norm_gain_grad,
        in_x_grad,
        in_z_grad,
        xdt_grad,
        xbc_grad,
        dt_weight_grad,
        dt_bias_grad,
        conv_weight_grad,
        conv_bias_grad,
        log_rates_grad,
        skip_gain_grad,
        out_weight_grad,
    )


def solution(mesh):
    rows, seq = mesh.shape["row"], mesh.shape["seq"]
    across = 2 if rows % 2 == 0 else 1
    cores = 2 if seq % 2 == 0 else 1
    along = next(n for n in (4, 3, 2, 1) if (seq // cores) % n == 0)
    fine = Mesh(
        mesh.devices.reshape(rows // across, across, seq // (along * cores), along, cores), ("y", "x", "o", "z", "c")
    )
    row, seq, both = row_axes, seq_axes, row_axes + seq_axes
    in_specs = (
        P(row, seq, None),
        P(row, seq, None),
        P(None, seq),
        P(None, seq),
        P(),
        P(seq),
        P(seq, None, row),
        P(seq, None, row),
        P(both, None, None),
        P(None, None, both),
        P(None, None, both),
        P(None, both),
        P(None, both),
        P(both),
        P(None, both),
        P(both),
        P(seq, None, row),
    )
    out_specs = (
        P(row, seq, None),
        P(row, seq, None),
        P(seq),
        P(seq, None, row),
        P(seq, None, row),
        P(both, None, None),
        P(None, None, both),
        P(None, None, both),
        P(None, both),
        P(None, both),
        P(both),
        P(None, both),
        P(both),
        P(seq, None, row),
    )
    return jax.shard_map(on_device, mesh=fine, in_specs=in_specs, out_specs=out_specs, check_vma=False)
```

```python
import functools
import math

import jax
import jax.numpy as jnp
from jax import lax
from jax.experimental import pallas as pl
from jax.experimental.pallas import tpu as pltpu
from jax.sharding import Mesh
from jax.sharding import PartitionSpec as P

epsilon = 1e-05
row_axes = ("y", "x")
group_axes = ("z", "c")
seq_axes = ("o", "z", "c")
team_axes = ("y", "x", "z", "c")
bf16 = jnp.bfloat16
f32 = jnp.float32
lanes = 128
huge_step = 1e6
vmem_bytes = 48 * 1024 * 1024


def apply_silu(values):
    return values * jax.nn.sigmoid(values)


def silu_slope(values):
    sigmoid_of = jax.nn.sigmoid(values)
    return sigmoid_of * (1.0 + values * (1.0 - sigmoid_of))


def softplus(values):
    tail = jnp.exp(-jnp.abs(values))
    series = tail * (1.0 + tail * (-1 / 2 + tail * (1 / 3 + tail * (-1 / 4 + tail * (1 / 5 - tail * (1 / 6))))))
    return jnp.maximum(values, 0.0) + jnp.where(tail < 0.05, series, jnp.log(1.0 + tail))


def dot(a, b, contract):
    return lax.dot_general(a, b, (contract, ((), ())), preferred_element_type=f32)


def chosen(values, label, mods, axis=1):
    wide = values.shape[axis] // mods
    parts = [lax.slice_in_dim(values, m * wide, (m + 1) * wide, axis=axis) for m in range(mods)]
    picked = parts[0]
    for m in range(1, mods):
        picked = jnp.where(label == m, parts[m], picked)
    return picked


def placed(values, label, mods, axis=1):
    wide = values.astype(f32)
    return jnp.concatenate([jnp.where(label == m, wide, 0.0) for m in range(mods)], axis=axis).astype(values.dtype)


start_column, label_column, fact_columns = 3, 4, 8


def columns_of(facts):
    missing = facts.shape[1] - facts.shape[0]
    return jnp.transpose(jnp.concatenate([facts, jnp.zeros((missing, facts.shape[1]), f32)], axis=0))


def label_column_of(facts_ref):
    return jnp.concatenate(
        [columns_of(facts_ref[j])[:, label_column : label_column + 1] for j in range(facts_ref.shape[0])], axis=0
    )


params = functools.partial(pltpu.CompilerParams, vmem_limit_bytes=vmem_bytes)


def everything(array):
    return pl.BlockSpec(array.shape, lambda i, rank=len(array.shape): (0,) * rank)


def scalars():
    return pl.BlockSpec(memory_space=pltpu.SMEM)


def shape(dims, dtype):
    return jax.ShapeDtypeStruct(dims, dtype)


def cost(flops, nbytes):
    return pl.CostEstimate(flops=int(flops), bytes_accessed=int(nbytes), transcendentals=0)


def assemble(weight_ref, whole):
    pieces, mods, some, wide = weight_ref.shape
    for i in range(pieces):
        for m in range(mods):
            whole[i * some : (i + 1) * some, m * wide : (m + 1) * wide] = weight_ref[i, m]


def lead_kernel(mods, places, x_ref, facts_ref, weight_ref, out_ref, whole):
    @pl.when(pl.program_id(0) == 0)
    def _():
        assemble(weight_ref, whole)

    some, here, wide = x_ref.shape
    label = label_column_of(facts_ref)
    picked = chosen(dot(x_ref[...].reshape(some * here, wide), whole[...], ((1,), (0,))), label, mods)
    for j in range(some):
        out_ref[places[pl.program_id(0) * some + j]] = picked[j * here : (j + 1) * here].astype(out_ref.dtype)


def lead_product(places, x, facts, weight, dtype):
    pieces, here, wide = x.shape
    groups, mods, some, mine = weight.shape
    outs = [shape((pieces, here, mine), dtype), shape((groups * some, mods * mine), bf16)]
    return pl.pallas_call(
        functools.partial(lead_kernel, mods),
        grid=(pieces // 4,),
        in_specs=[
            scalars(),
            pl.BlockSpec((4, here, wide), lambda i: (i, 0, 0)),
            pl.BlockSpec((4, fact_columns, here), lambda i: (i, 0, 0)),
            everything(weight),
        ],
        out_specs=[everything(out) for out in outs],
        out_shape=outs,
        compiler_params=params(),
        cost_estimate=cost(2 * pieces * here * wide * mods * mine, 2 * pieces * here * wide),
        name="lead_product",
    )(places, x, facts, weight)


def lead_pieces_kernel(mods, count, places, facts_ref, weight_ref, *refs):
    pieces = refs[:count]
    out_ref, whole, all_ref, buffer, in_sems, out_sems = refs[count:]
    _, some, here, wide = buffer.shape
    assemble(weight_ref, whole)

    def fetch(i):
        return [
            pltpu.make_async_copy(pieces[i * some + j], buffer.at[i % 2, j], in_sems.at[i % 2, j]) for j in range(some)
        ]

    def store(i):
        return pltpu.make_async_copy(buffer.at[i % 2], all_ref.at[pl.ds(i * some, some)], out_sems.at[i % 2])

    steps = count // some
    for copy in fetch(0):
        copy.start()
    for i in range(steps):
        if i + 1 < steps:
            if i:
                store(i - 1).wait()
            for copy in fetch(i + 1):
                copy.start()
        for copy in fetch(i):
            copy.wait()
        store(i).start()
        label = label_column_of(facts_ref.at[i * some : (i + 1) * some])
        picked = chosen(dot(buffer[i % 2].reshape(some * here, wide), whole[...], ((1,), (0,))), label, mods)
        for j in range(some):
            out_ref[places[i * some + j]] = picked[j * here : (j + 1) * here].astype(out_ref.dtype)
    for i in range(max(steps - 2, 0), steps):
        store(i).wait()


def lead_pieces(places, pieces, facts, weight, dtype):
    here, wide = pieces[0].shape
    count, some = len(pieces), 4
    groups, mods, features, mine = weight.shape
    outs = [
        shape((count, here, mine), dtype),
        shape((groups * features, mods * mine), bf16),
        shape((count, here, wide), bf16),
    ]
    vmem, there = pl.BlockSpec(memory_space=pltpu.VMEM), pl.BlockSpec(memory_space=pl.ANY)
    return pl.pallas_call(
        functools.partial(lead_pieces_kernel, mods, count),
        in_specs=[scalars(), vmem, vmem] + [there] * count,
        out_specs=[vmem, vmem, there],
        out_shape=outs,
        scratch_shapes=[
            pltpu.VMEM((2, some, here, wide), bf16),
            pltpu.SemaphoreType.DMA((2, some)),
            pltpu.SemaphoreType.DMA((2,)),
        ],
        compiler_params=params(),
        cost_estimate=cost(2 * count * here * wide * mods * mine, 4 * count * here * wide),
        name="lead_pieces",
    )(places, facts, weight, *pieces)


def trail_kernel(mods, count, skipped, *refs):
    lefts, facts_ref, weights = refs[:count], refs[count], refs[count + 1 : 2 * count + 1]
    outs = refs[2 * count + 1 + skipped :]
    some, here, mine = lefts[0].shape
    label = label_column_of(facts_ref)
    total = None
    for left, weight in zip(lefts, weights):
        term = dot(placed(left[...].reshape(some * here, mine), label, mods), weight[...], ((1,), (1,)))
        total = term if total is None else total + term
    total = total.astype(bf16).reshape(some, here, -1)
    if len(outs) == 1:
        outs[0][...] = total
    else:
        for i, out in enumerate(outs):

            @pl.when(pl.program_id(0) == i)
            def _():
                out[...] = total


def trail_product(lefts, facts, weights, mods, k=None, beside=()):
    pieces, here, mine = lefts[0].shape
    features = weights[0].shape[0]
    if k is None:
        steps, outs = pieces // 4, [shape((pieces, here, features), bf16)]
        out_specs = [pl.BlockSpec((4, here, features), lambda i: (i, 0, 0))]

        def block(i):
            return (i, 0, 0)
    else:
        steps, outs = 2, [shape((4, here, features), bf16)] * 2
        out_specs = [everything(out) for out in outs]

        def block(i):
            return (2 * k + 1 - i, 0, 0)

    return pl.pallas_call(
        functools.partial(trail_kernel, mods, len(lefts), len(beside)),
        grid=(steps,),
        in_specs=[pl.BlockSpec((4, here, mine), block) for _ in lefts]
        + [pl.BlockSpec((4, fact_columns, here), block)]
        + [everything(weight) for weight in weights]
        + [pl.BlockSpec(memory_space=pl.ANY) for _ in beside],
        out_specs=out_specs,
        out_shape=outs,
        compiler_params=params(),
        cost_estimate=cost(
            8 * steps * here * features * mods * mine * len(lefts), 8 * steps * here * features
        ),
        name="trail_product",
    )(*lefts, facts, *weights, *beside)


def grad_kernel(mods, x_ref, d_ref, facts_ref, *refs):
    out_ref, spread = refs[-2:]
    pieces, here, mine = d_ref.shape

    @pl.when(pl.program_id(0) == 0)
    def _():
        for i in range(pieces):
            label = columns_of(facts_ref[i])[:, label_column : label_column + 1]
            spread[i * here : (i + 1) * here] = placed(d_ref[i], label, mods)

    out_ref[0] = dot(x_ref[...], spread[...], ((0,), (0,))).astype(out_ref.dtype)


def feature_grad(x, d, facts, mods, groups, dtype, beside=()):
    pieces, here, wide = x.shape
    mine = d.shape[2]
    some = min(256, wide)
    out = shape((wide // some, some, mods * mine), dtype)
    grad = pl.pallas_call(
        functools.partial(grad_kernel, mods),
        grid=(wide // some,),
        in_specs=[
            pl.BlockSpec((pieces * here, some), lambda i: (0, i)),
            everything(d),
            everything(facts),
        ]
        + [pl.BlockSpec(memory_space=pl.ANY) for _ in beside],
        out_specs=pl.BlockSpec((1, some, mods * mine), lambda i: (i, 0, 0)),
        out_shape=out,
        scratch_shapes=[pltpu.VMEM((pieces * here, mods * mine), bf16)],
        compiler_params=params(),
        cost_estimate=cost(6 * pieces * here * wide * mods * mine, 2 * pieces * here * wide),
        name="feature_grad",
    )(x.reshape(pieces * here, wide), d, facts, *beside)
    return grad.reshape(groups, wide // groups, mods * mine)


def settle_kernel(got_ref, weight_ref, out_ref, sum_ref):
    mods, _, mine = out_ref.shape

    @pl.when(pl.program_id(0) == 0)
    def _():
        sum_ref[...] = jnp.zeros_like(sum_ref)

    for m in range(mods):
        grad = got_ref[0, :, m * mine : (m + 1) * mine].astype(f32)
        out_ref[m] = grad
        sum_ref[...] += grad * weight_ref[m].astype(f32)


def settle(got, weight):
    sources, some, columns = got.shape
    mods, _, wide = weight.shape
    mine = wide // sources
    item = pl.BlockSpec((mods, some, mine), lambda i: (0, 0, i))
    outs = [shape(weight.shape, f32), shape((some, mine), f32)]
    return pl.pallas_call(
        settle_kernel,
        grid=(sources,),
        in_specs=[pl.BlockSpec((1, some, columns), lambda i: (i, 0, 0)), item],
        out_specs=[item, everything(outs[1])],
        out_shape=outs,
        compiler_params=params(),
        cost_estimate=cost(0, 8 * mods * some * wide),
        name="settle",
    )(got, weight)


def conv_kernel(mods, conv_ref, before_ref, facts_ref, row_label_ref, taps_ref, bias_ref, xdt_ref, xbc_ref, pre_ref, proj_ref, carried, line):
    rows, here, mine = conv_ref.shape

    @pl.when(pl.program_id(0) == 0)
    def _():
        carried[...] = before_ref[...]

    for r in range(rows):
        block = conv_ref[r].astype(f32)
        line[:8] = carried[r]
        line[8:] = block
        facts = columns_of(facts_ref[r, 0])
        pre = bias_ref[...] + taps_ref[0:1] * block
        for lag in range(1, taps_ref.shape[0]):
            pre = pre + taps_ref[lag : lag + 1] * (facts[:, lag - 1 : lag] * line[8 - lag : 8 - lag + here])
        carried[r] = block[here - 8 :]
        pre_ref[r] = pre
        low = apply_silu(pre).astype(bf16)
        wide = chosen(dot(low, xdt_ref[...], ((1,), (0,))), facts[:, label_column : label_column + 1], mods)
        small = chosen(dot(xbc_ref[...], low, ((1,), (1,))), row_label_ref[0, r : r + 1], mods, 0)
        proj_ref[r, 0, :here] = wide.astype(bf16)
        proj_ref[r, 0, here:] = small.astype(bf16)


def conv_block(conv_in, before, facts, row_label, taps, bias, xdt, xbc):
    rows, length, mine = conv_in.shape
    blocks, _, here = row_label.shape
    mods = xdt.shape[1] // here
    narrow = xbc.shape[0] // mods
    item = pl.BlockSpec((rows, here, mine), lambda i: (0, i, 0))
    return pl.pallas_call(
        functools.partial(conv_kernel, mods),
        grid=(blocks,),
        in_specs=[
            item,
            everything(before),
            pl.BlockSpec((rows, 1, fact_columns, here), lambda i: (0, i, 0, 0)),
            pl.BlockSpec((1, rows, here), lambda i: (i, 0, 0)),
        ]
        + [everything(array) for array in (taps, bias, xdt, xbc)],
        out_specs=[item, pl.BlockSpec((rows, 1, here + narrow, here), lambda i: (0, i, 0, 0))],
        out_shape=[shape(conv_in.shape, f32), shape((rows, blocks, here + narrow, here), bf16)],
        scratch_shapes=[pltpu.VMEM((rows, 8, mine), f32), pltpu.VMEM((8 + here, mine), f32)],
        compiler_params=params(),
        cost_estimate=cost(20000 * rows * length * mine, 10 * rows * length * mine),
        name="conv_block",
    )(conv_in, before, facts, row_label, taps, bias, xdt, xbc)


def coefficient_lines(proj_ref, rows, here, line):
    narrow = proj_ref.shape[2] - here
    for r in range(rows):
        small = proj_ref[r, 0, here:].astype(f32)
        small = jnp.concatenate([small, jnp.zeros((here - narrow, here), f32)], axis=0)
        turned = jnp.transpose(small)
        line[r * here : (r + 1) * here] = turned
        line[(rows + r) * here : (rows + r + 1) * here] = pltpu.roll(turned, here - narrow // 2, 1)


def coefficient_tiles(proj_ref, rows, here, expand_ref, turned, tiles):
    narrow = proj_ref.shape[2] - here
    for r in range(rows):
        small = proj_ref[r, 0, here:].astype(f32)
        small = jnp.transpose(jnp.concatenate([small, jnp.zeros((here - narrow, here), f32)], axis=0))
        turned[pl.ds(r, here, stride=2 * rows), :] = small
        turned[pl.ds(rows + r, here, stride=2 * rows), :] = pltpu.roll(small, here - narrow // 2, 1)
    some = 256
    for i in range(turned.shape[0] // some):
        part = slice(i * some, (i + 1) * some)
        tiles[part] = dot(turned[part].astype(bf16), expand_ref[...], ((1,), (0,)))


def scan_lines(r, rows, here, value, line):
    line[r * here : (r + 1) * here] = value
    line[(rows + r) * here : (rows + r + 1) * here] = value


def forward_kernel(
    mods, proj_ref, pre_ref, facts_ref, gate_ref, dtw_ref, dtb_ref, rate_ref, skip_ref, start_ref, expand_ref,
    gated_ref, scanned_ref, dt_ref, kept_ref, end_ref, held, step_line, drive_line, turned, tiles, out_line,
):
    rows, here, mine = pre_ref.shape
    pieces, subl, _ = rate_ref.shape

    @pl.when(pl.program_id(0) == 0)
    def _():
        held[...] = start_ref[...]

    coefficient_tiles(proj_ref, rows, here, expand_ref, turned, tiles)
    for r in range(rows):
        facts = columns_of(facts_ref[r, 0])
        label = facts[:, label_column : label_column + 1]
        dt_pre = chosen(dot(proj_ref[r, 0, :here], dtw_ref[...], ((1,), (0,))) + dtb_ref[...], label, mods)
        dt_ref[r] = dt_pre
        step = softplus(dt_pre)
        scan_lines(r, rows, here, step * apply_silu(pre_ref[r]), drive_line)
        scan_lines(r, rows, here, jnp.where(facts[:, start_column : start_column + 1] > 0, huge_step, step), step_line)

    def one(t, state):
        lines = pl.ds(t, subl, stride=here)
        step, drive = step_line[lines, :], drive_line[lines, :]
        spot = pl.ds(pl.multiple_of(t * subl, subl), subl)
        emitted = None
        following = []
        for j in range(pieces):
            kept_ref[t, j] = state[j]
            decay = jnp.exp2(step * rate_ref[j])
            now = decay * state[j] + drive * tiles[spot, j * mine : (j + 1) * mine]
            term = now * tiles[spot, (pieces + j) * mine : (pieces + j + 1) * mine]
            emitted = term if emitted is None else emitted + term
            following.append(now)
        out_line[lines, :] = emitted
        return tuple(following)

    def eight(block, state):
        for i in range(8):
            state = one(block * 8 + i, state)
        return state

    state = lax.fori_loop(0, here // 8, eight, tuple(held[j] for j in range(pieces)))
    for j in range(pieces):
        held[j] = state[j]
        end_ref[j] = state[j]
    for r in range(rows):
        emitted = out_line[r * here : (r + 1) * here] + out_line[(rows + r) * here : (rows + r + 1) * here]
        scanned = emitted + skip_ref[...] * apply_silu(pre_ref[r])
        scanned_ref[r] = scanned
        gated_ref[r] = (scanned * apply_silu(gate_ref[r])).astype(bf16)


def scan_forward(proj, pre, facts, gate, dtw, dtb, rates2, skip, start):
    rows, length, mine = pre.shape
    _, blocks, deep, here = proj.shape
    pieces, subl, _ = rates2.shape
    item = pl.BlockSpec((rows, here, mine), lambda i: (0, i, 0))
    line = pltpu.VMEM((subl * here, mine), f32)
    expand = (jnp.arange(here)[:, None] == jnp.arange(2 * pieces * mine)[None, :] // mine).astype(bf16)
    return pl.pallas_call(
        functools.partial(forward_kernel, dtw.shape[1] // mine),
        grid=(blocks,),
        in_specs=[
            pl.BlockSpec((rows, 1, deep, here), lambda i: (0, i, 0, 0)),
            item,
            pl.BlockSpec((rows, 1, fact_columns, here), lambda i: (0, i, 0, 0)),
            item,
        ]
        + [everything(array) for array in (dtw, dtb, rates2, skip, start, expand)],
        out_specs=[
            item,
            item,
            item,
            pl.BlockSpec((here, pieces, subl, mine), lambda i: (i, 0, 0, 0)),
            everything(start),
        ],
        out_shape=[
            shape(pre.shape, bf16),
            shape(pre.shape, f32),
            shape(pre.shape, f32),
            shape((length, pieces, subl, mine), f32),
            shape(start.shape, f32),
        ],
        scratch_shapes=[pltpu.VMEM(start.shape, f32), line, line, line]
        + [pltpu.VMEM((subl * here, 2 * pieces * mine), f32), line],
        compiler_params=params(),
        cost_estimate=cost(5500 * length * pieces * subl * mine, 5 * length * pieces * subl * mine),
        name="scan_forward",
    )(proj, pre, facts, gate, dtw, dtb, rates2, skip, start, expand)


def backward_kernel(
    mods, tables, proj_ref, pre_ref, facts_ref, gate_ref, scanned_ref, dt_ref, d_gated_ref, kept_ref, dtw_ref, rate2_ref,
    rate_ref, skip_ref, last_ref, carry_ref, sum_ref, expand_ref, d_gate_ref, d_proj_ref, d_act_ref, dtw_grad_ref, dtb_grad_ref,
    skip_grad_ref, rate_sum_ref, carry_out_ref, carried, later, products, step_line, drive_line, turned, tiles, back_line,
    pulled_line, weighted_line, small_line,
):
    rows, here, mine = pre_ref.shape
    blocks = tables.shape[0] // rows
    narrow = proj_ref.shape[2] - here
    pieces, subl, _ = rate_ref.shape
    place = blocks - 1 - pl.program_id(0)

    @pl.when(pl.program_id(0) == 0)
    def _():
        carried[...] = carry_ref[...]
        later[...] = last_ref[...]
        for ref in (rate_sum_ref, dtw_grad_ref, dtb_grad_ref, skip_grad_ref):
            ref[...] = jnp.zeros_like(ref)

    coefficient_tiles(proj_ref, rows, here, expand_ref, turned, tiles)
    for r in range(rows):
        facts = columns_of(facts_ref[r, 0])
        step, activated = softplus(dt_ref[r]), apply_silu(pre_ref[r])
        gate, d_gated = gate_ref[r], d_gated_ref[r]
        d_scan = d_gated * apply_silu(gate)
        d_gate_ref[tables[r * blocks + place]] = (d_gated * scanned_ref[r] * silu_slope(gate)).astype(bf16)
        skip_grad_ref[...] += jnp.sum(d_scan * activated, axis=0, keepdims=True)
        scan_lines(r, rows, here, d_scan, back_line)
        scan_lines(r, rows, here, step * activated, drive_line)
        scan_lines(r, rows, here, jnp.where(facts[:, start_column : start_column + 1] > 0, huge_step, step), step_line)

    def one(t, carry, state):
        lines = pl.ds(t, subl, stride=here)
        step, drive, back = step_line[lines, :], drive_line[lines, :], back_line[lines, :]
        row = pl.ds(pl.multiple_of(t * subl, subl), subl)
        pulled_sum, weighted_sum = None, None
        new_carry, new_state, terms, sums = [], [], [], []
        for j in range(pieces):
            before = kept_ref[t, j]
            decay = jnp.exp2(step * rate2_ref[j])
            adjoint = back * tiles[row, (pieces + j) * mine : (pieces + j + 1) * mine] + carry[j]
            passed = decay * adjoint
            pulled = passed * before
            weighted = adjoint * tiles[row, j * mine : (j + 1) * mine]
            first = pulled * rate_ref[j]
            pulled_sum = first if pulled_sum is None else pulled_sum + first
            weighted_sum = weighted if weighted_sum is None else weighted_sum + weighted
            terms.append((adjoint * drive, back * state[j]))
            sums.append(pulled * step)
            new_carry.append(passed)
            new_state.append(before)
        pulled_line[lines, :] = pulled_sum
        weighted_line[lines, :] = weighted_sum
        return new_carry, new_state, terms, sums

    def eight(k, loop):
        carry, state, rates = loop
        block = here // 8 - 1 - k
        rates = list(rates)
        for i in (6, 4, 2, 0):
            t = block * 8 + i
            carry, state, terms_b, sums_b = one(t + 1, carry, state)
            carry, state, terms_a, sums_a = one(t, carry, state)
            spot = pl.ds(pl.multiple_of(t * subl, 16), 16)
            for j in range(pieces):
                rates[j] = rates[j] + (sums_a[j] + sums_b[j])
                for part in range(2):
                    column = (part * pieces + j) * mine
                    products[spot, column : column + mine] = jnp.concatenate(
                        [terms_a[j][part], terms_b[j][part]], axis=0
                    ).astype(bf16)
        return tuple(carry), tuple(state), tuple(rates)

    begin = tuple(tuple(ref[j] for j in range(pieces)) for ref in (carried, later, rate_sum_ref))
    carry, state, rates = lax.fori_loop(0, here // 8, eight, begin)
    for j in range(pieces):
        carried[j] = carry[j]
        later[j] = state[j]
        rate_sum_ref[j] = rates[j]
        carry_out_ref[j] = carry[j]
    small_line[...] = dot(products[...], sum_ref[...], ((1,), (0,)))
    for r in range(rows):
        label = columns_of(facts_ref[r, 0])[:, label_column : label_column + 1]
        dt_pre, activated = dt_ref[r], apply_silu(pre_ref[r])
        near, far = slice(r * here, (r + 1) * here), slice((rows + r) * here, (rows + r + 1) * here)
        weighted = weighted_line[near] + weighted_line[far]
        d_step = pulled_line[near] + pulled_line[far] + activated * weighted
        d_act_ref[r] = back_line[near] * skip_ref[...] + softplus(dt_pre) * weighted
        d_dt = placed((d_step * jax.nn.sigmoid(dt_pre)).astype(bf16), label, mods)
        dtw_grad_ref[...] += dot(proj_ref[r, 0, :here], d_dt, ((0,), (0,)))
        dtb_grad_ref[...] += jnp.sum(d_dt.astype(f32), axis=0, keepdims=True)
        d_proj_ref[r, 0, :here] = dot(d_dt, dtw_ref[...], ((1,), (1,))).astype(bf16)
        one_half = small_line[pl.ds(r, here, stride=subl), :]
        other_half = small_line[pl.ds(rows + r, here, stride=subl), :]
        small = jnp.transpose(one_half + pltpu.roll(other_half, narrow // 2, 1))
        d_proj_ref[r, 0, here:] = small[:narrow].astype(bf16)


def scan_backward(tables, proj, pre, facts, gate, scanned, dt_pre, d_gated, kept, dtw, rates2, rates, skip, last, carry):
    rows, length, mine = pre.shape
    _, blocks, deep, here = proj.shape
    pieces, subl, _ = rates2.shape
    item = pl.BlockSpec((rows, here, mine), lambda i: (0, blocks - 1 - i, 0))
    proj_item = pl.BlockSpec((rows, 1, deep, here), lambda i: (0, blocks - 1 - i, 0, 0))
    columns = 2 * pieces * mine
    expand = (jnp.arange(here)[:, None] == jnp.arange(columns)[None, :] // mine).astype(bf16)
    summing = (jnp.arange(columns)[:, None] // mine == jnp.arange(lanes)[None, :]).astype(bf16)
    d_gate = shape((rows * blocks, here, mine), bf16)
    line = pltpu.VMEM((subl * here, mine), f32)
    small = [shape((here, dtw.shape[1]), f32), shape((1, dtw.shape[1]), f32), shape((1, mine), f32), shape(carry.shape, f32)]
    return pl.pallas_call(
        functools.partial(backward_kernel, dtw.shape[1] // mine),
        grid=(blocks,),
        in_specs=[
            scalars(),
            proj_item,
            item,
            pl.BlockSpec((rows, 1, fact_columns, here), lambda i: (0, blocks - 1 - i, 0, 0)),
            item,
            item,
            item,
            item,
            pl.BlockSpec((here, pieces, subl, mine), lambda i: (blocks - 1 - i, 0, 0, 0)),
        ]
        + [everything(array) for array in (dtw, rates2, rates, skip, last, carry, summing, expand)],
        out_specs=[everything(d_gate), proj_item, item] + [everything(array) for array in small + [carry]],
        out_shape=[d_gate, shape(proj.shape, bf16), shape(pre.shape, f32)] + small + [shape(carry.shape, f32)],
        scratch_shapes=[pltpu.VMEM(carry.shape, f32)] * 2 + [pltpu.VMEM((subl * here, columns), bf16)] + [line] * 3
        + [pltpu.VMEM((subl * here, columns), f32)] + [line] * 4,
        compiler_params=params(),
        cost_estimate=cost(7500 * length * pieces * subl * mine, 5 * length * pieces * subl * mine),
        name="scan_backward",
    )(tables, proj, pre, facts, gate, scanned, dt_pre, d_gated, kept, dtw, rates2, rates, skip, last, carry, summing, expand)


def deconv_kernel(
    mods, tables, d_proj_ref, conv_ref, pre_ref, d_act_ref, facts_ref, row_label_ref, taps_ref, xdt_ref, xbc_ref,
    d_conv_ref, xdt_grad_ref, xbc_grad_ref, taps_grad_ref, bias_grad_ref, head_ref, tail_ref, carried, line,
):
    rows, here, mine = pre_ref.shape
    blocks = tables.shape[0] // rows
    taps = taps_ref.shape[0]
    place = blocks - 1 - pl.program_id(0)

    @pl.when(pl.program_id(0) == 0)
    def _():
        carried[...] = jnp.zeros_like(carried)
        for ref in (xdt_grad_ref, xbc_grad_ref, taps_grad_ref, bias_grad_ref):
            ref[...] = jnp.zeros_like(ref)

    for r in range(rows):
        facts = columns_of(facts_ref[r, 0])
        pre = pre_ref[r]
        low = apply_silu(pre).astype(bf16)
        d_rank = placed(d_proj_ref[r, 0, :here], facts[:, label_column : label_column + 1], mods)
        d_small = placed(d_proj_ref[r, 0, here:], row_label_ref[0, r : r + 1], mods, 0)
        xdt_grad_ref[...] += dot(low, d_rank, ((0,), (0,)))
        xbc_grad_ref[...] += dot(d_small, low, ((1,), (0,)))
        d_act = d_act_ref[r] + dot(d_rank, xdt_ref[...], ((1,), (1,))) + dot(d_small, xbc_ref[...], ((0,), (0,)))
        d_pre = d_act * silu_slope(pre)
        source = conv_ref[r].astype(f32)
        total = taps_ref[0:1] * d_pre
        bias_grad_ref[...] += jnp.sum(d_pre, axis=0, keepdims=True)
        taps_grad_ref[0:1] += jnp.sum(source * d_pre, axis=0, keepdims=True)
        for lag in range(1, taps):
            kept = facts[:, lag - 1 : lag] * d_pre
            line[:here] = kept
            line[here:] = carried[r, lag - 1]
            carried[r, lag - 1] = kept[:8]
            moved = line[lag : lag + here]
            total = total + taps_ref[lag : lag + 1] * moved
            taps_grad_ref[lag : lag + 1] += jnp.sum(source * moved, axis=0, keepdims=True)
        d_conv_ref[tables[r * blocks + place]] = total.astype(bf16)

        @pl.when(pl.program_id(0) == 0)
        def _():
            tail_ref[r] = total[here - 8 :]

    head_ref[...] = carried[...]


def deconv_block(tables, d_proj, conv_in, pre, d_act, facts, row_label, taps, xdt, xbc):
    rows, length, mine = pre.shape
    _, blocks, deep, here = d_proj.shape
    item = pl.BlockSpec((rows, here, mine), lambda i: (0, blocks - 1 - i, 0))
    outs = [
        shape((rows * blocks, here, mine), bf16),
        shape(xdt.shape, f32),
        shape(xbc.shape, f32),
        shape(taps.shape, f32),
        shape((1, mine), f32),
        shape((rows, taps.shape[0] - 1, 8, mine), f32),
        shape((rows, 8, mine), f32),
    ]
    return pl.pallas_call(
        functools.partial(deconv_kernel, xdt.shape[1] // here),
        grid=(blocks,),
        in_specs=[
            scalars(),
            pl.BlockSpec((rows, 1, deep, here), lambda i: (0, blocks - 1 - i, 0, 0)),
            item,
            item,
            item,
            pl.BlockSpec((rows, 1, fact_columns, here), lambda i: (0, blocks - 1 - i, 0, 0)),
            pl.BlockSpec((1, rows, here), lambda i: (blocks - 1 - i, 0, 0)),
        ]
        + [everything(array) for array in (taps, xdt, xbc)],
        out_specs=[everything(array) for array in outs],
        out_shape=outs,
        scratch_shapes=[pltpu.VMEM(outs[5].shape, f32), pltpu.VMEM((here + 8, mine), f32)],
        compiler_params=params(),
        cost_estimate=cost(30000 * rows * length * mine, 14 * rows * length * mine),
        name="deconv_block",
    )(tables, d_proj, conv_in, pre, d_act, facts, row_label, taps, xdt, xbc)


def passed_along(value, axis, by):
    size = lax.axis_size(axis)
    return lax.ppermute(value, axis, [(i, i + by) for i in range(size) if 0 <= i + by < size])


def shifted(value, by):
    size = lax.axis_size("z")
    return value if by % size == 0 else lax.ppermute(value, "z", [(i, (i + by) % size) for i in range(size)])


def swapped(value):
    return lax.ppermute(value, "c", [(0, 1), (1, 0)])


def hop(value, second):
    depth = lax.axis_size("z")

    def place(y, x, z, c):
        return ((y * 2 + x) * depth + z) * 2 + c

    pairs = [
        (place(y, x, z, c), place(y, 1 - x, z, c) if (c == 1) == second else place(1 - y, x, z, c))
        for y in range(2)
        for x in range(2)
        for z in range(depth)
        for c in range(2)
    ]
    return lax.ppermute(value, team_axes, pairs)


def relative_places():
    depth = lax.axis_size("z")
    y, x, z, c = (lax.axis_index(name) for name in team_axes)
    n = jnp.arange(4)[None, None, :]
    core = (c + jnp.arange(2)[None, :, None]) % 2
    back = (z - jnp.arange(depth)[:, None, None]) % depth
    one, two = n % 2, n // 2
    flip_x = jnp.where(core == 0, one, two)
    flip_y = jnp.where(core == 0, two, one)
    return (((((y + flip_y) % 2) * 2 + (x + flip_x) % 2) * depth + back) * 2 + core).reshape(-1)


def nothing(*refs):
    pass


def tied(value, *others):
    there = pl.BlockSpec(memory_space=pl.ANY)
    return pl.pallas_call(
        nothing,
        in_specs=[there] * (1 + len(others)),
        out_specs=there,
        out_shape=shape(value.shape, value.dtype),
        input_output_aliases={0: 0},
        name="tied",
    )(value, *others)


def team_gather(value, weight):
    near, first, second, third = {0: value}, {}, {}, {}

    def hops(k):
        first[k], second[k] = hop(near[k], False), hop(near[k], True)

    near[1], near[3] = shifted(value, 1), shifted(value, 3)
    weight = exchanged(tied(weight, near[1]))
    hops(0)
    near[2] = shifted(tied(value, first[0], second[0]), 2)
    third[0] = hop(first[0], True)
    near[1] = tied(near[1], first[0], second[0])
    hops(1)
    third[1] = hop(first[1], True)
    near[3] = tied(near[3], third[0], first[1], second[1])
    hops(3)
    third[3] = hop(first[3], True)
    near[2] = tied(near[2], third[1], first[3], second[3], weight)
    hops(2)
    third[2] = hop(first[2], True)
    parts = []
    for k in range(4):
        pieces = [near[k], first[k], second[k], third[k]]
        parts += pieces + [swapped(piece) for piece in pieces]
    return parts, [first[2], second[2], third[3]], weight


def team_scatter(made, beside):
    def added(*terms):
        return sum(term.astype(f32) for term in terms)

    order = list(range(1, lax.axis_size("z"))) + [0]
    far, near, first, second = {}, {}, {}, {}

    def make(i, *others):
        away, near[i] = made(order[i], list(others))
        far[i] = swapped(away)

    def send_first(i):
        first[i] = added(near[i][2:], far[i][2:]).astype(bf16)
        return first[i]

    def send_second(i):
        come = hop(first[i], True)
        second[i] = (added(near[i][1], far[i][1], come[1]).astype(bf16), come[0])
        return second[i][0]

    make(0)
    make(1)
    make(2, send_first(0))
    make(3, send_first(1), send_second(0))
    extra = beside([send_first(2), send_second(1), send_first(3)])
    total = None
    for i, k in enumerate(order):
        if i > 1:
            send_second(i)
        last = hop(second[i][0], False)
        total_k = added(near[i][0], far[i][0], second[i][1], last)
        if k:
            total_k = shifted(total_k.astype(bf16), -k).astype(f32)
        total = total_k if total is None else total + total_k
    return total, extra


def exchanged(parts):
    return lax.all_to_all(parts, group_axes, 0, 0, tiled=True)


def spread_weight(weight):
    outer, group = lax.axis_size("o"), lax.axis_size(group_axes)
    mods, here, wide = weight.shape
    each = wide // (outer * group)
    parts = weight.reshape(mods, here, outer, group, each)
    parts = jnp.transpose(parts, (3, 0, 1, 2, 4)).reshape(group, mods, here, outer * each)
    return parts


def through_outer(got):
    return got if lax.axis_size("o") == 1 else lax.all_gather(got, "o", axis=0, tiled=True)


def spread_done(parts):
    return through_outer(exchanged(parts))


def collect(parts):
    if lax.axis_size("o") > 1:
        parts = lax.psum_scatter(parts, "o", scatter_dimension=0, tiled=True)
    return exchanged(parts.astype(bf16))


def settled(got, weight):
    outer, group = lax.axis_size("o"), lax.axis_size(group_axes)
    mods, here, wide = weight.shape
    if outer == 1:
        grad, sums = settle(got, weight)
        return grad, jnp.sum(sums, axis=1)
    got = got.astype(f32).reshape(group, here, mods, outer, wide // (outer * group))
    grad = jnp.transpose(got, (2, 1, 3, 0, 4)).reshape(weight.shape)
    return grad, jnp.sum(grad * weight.astype(f32), axis=(0, 2))


def outer_gathered(value, axis):
    return value if lax.axis_size("o") == 1 else lax.all_gather(value, "o", axis=axis, tiled=True)


def outer_summed(value, axis):
    if lax.axis_size("o") == 1:
        return value
    return lax.psum_scatter(value, "o", scatter_dimension=axis, tiled=True)


def half_of(value, axis, name, other):
    return lax.dynamic_index_in_dim(value, (lax.axis_index(name) + other) % 2, axis, False)


def team_sum(value, beside, final):
    depth = lax.axis_size("z")
    z = lax.axis_index("z")

    def halved(value, axis, name, pairs, *others):
        sent = half_of(value, axis, name, 1).astype(bf16)
        sent = lax.ppermute(tied(sent, *others) if others else sent, name, pairs)
        return half_of(value, axis, name, 0).astype(f32) + sent.astype(f32)

    swap = [(0, 1), (1, 0)]
    held = halved(value, 3, "c", swap)
    held = halved(held, 0, "y", swap)
    held = halved(held, 0, "x", swap, *beside[:1])
    if beside[1:]:
        held = tied(held, *beside[1:])
    own = lax.dynamic_index_in_dim(held, z, 0, False)
    for k in range(1, depth):
        own = own + shifted(lax.dynamic_index_in_dim(held, (z + k) % depth, 0, False).astype(bf16), k).astype(f32)
    own = own.astype(bf16)
    back = jnp.stack([own] + [shifted(own, k) for k in range(1, depth)])
    rolled = back[(z - jnp.arange(depth)) % depth]

    def doubled(value, axis, name):
        other = lax.ppermute(value, name, swap)
        flag = lax.axis_index(name) == 0
        return jnp.stack([jnp.where(flag, value, other), jnp.where(flag, other, value)], axis=axis)

    wide = doubled(doubled(rolled, 0, "x"), 0, "y")
    return doubled(tied(wide, *final) if final else wide, 3, "c")


def entering_state(passing, local_end, backward):
    count, place = lax.axis_size("o"), lax.axis_index("o")
    decays = lax.all_gather(passing.astype(bf16), "o")
    ends = lax.all_gather(local_end.astype(bf16), "o")
    state = jnp.zeros_like(local_end)
    for i in range(count):
        source = count - 1 - i if backward else i
        ahead = source > place if backward else source < place
        state = jnp.where(ahead, decays[source].astype(f32) * state + ends[source].astype(f32), state)
    return state


def on_device(
    tokens,
    cotangent,
    modality,
    starts,
    row_lengths,
    norm_gain,
    in_x_weight,
    in_z_weight,
    xdt_weight,
    xbc_weight,
    dt_weight,
    dt_bias,
    conv_weight,
    conv_bias,
    log_rates,
    skip_gain,
    out_weight,
):
    outer, group = lax.axis_size("o"), lax.axis_size(group_axes)
    rows, here = modality.shape
    width = tokens.shape[-1]
    mods = in_x_weight.shape[1]
    taps, states, rank = conv_weight.shape[0], log_rates.shape[0], dt_weight.shape[0]
    margin = taps - 1
    local_len = group * here
    own_row = lax.axis_index(row_axes)
    count = rows * local_len

    depth = lax.axis_size("z")
    place_z = lax.axis_index("z")

    def lead(weight):
        return jnp.transpose(weight, (1, 0, 2))

    features = norm_gain.shape[0]
    packed = jnp.concatenate(
        [modality.astype(f32).reshape(-1), starts.astype(f32).reshape(-1), norm_gain.astype(f32)]
    )
    packed = jnp.stack([packed] + [shifted(packed, k) for k in range(1, depth)])
    packed = packed[(place_z - jnp.arange(depth)) % depth]
    others, first_core = swapped(packed), lax.axis_index("c") == 0
    packed = jnp.stack([jnp.where(first_core, packed, others), jnp.where(first_core, others, packed)], axis=1)
    labels = packed[:, :, : 2 * rows * here].astype(jnp.int32).reshape(depth, 2, 2, rows, here)
    labels = jnp.transpose(labels, (2, 3, 0, 1, 4)).reshape(2, rows, local_len)
    modality, starts = labels[0], labels[1]
    gain = outer_gathered(packed[:, :, 2 * rows * here :].reshape(-1, features), 0).reshape(width)

    inputs = tokens[0].astype(f32)
    inv_rms = lax.rsqrt(jnp.mean(inputs * inputs, axis=-1, keepdims=True) + epsilon)
    scaled = inputs * inv_rms
    wz = spread_done(spread_weight(lead(in_z_weight)))
    normed_pieces, last_pieces, wx = team_gather((scaled * gain).astype(bf16), spread_weight(lead(in_x_weight)))
    wx = through_outer(wx)
    position = lax.axis_index(seq_axes) * here + jnp.arange(here, dtype=jnp.int32)
    own_valid = (position < lax.dynamic_index_in_dim(row_lengths, own_row, 0, False)).astype(f32)[:, None]
    upstream = cotangent[0].astype(f32)
    own_back = (upstream * own_valid).astype(bf16)
    own_back = tied(own_back, *last_pieces)
    d_branch = lax.all_gather(own_back, team_axes)
    xdt = outer_gathered(xdt_weight, 0)
    xbc = outer_gathered(xbc_weight, 2)
    dtw = outer_gathered(dt_weight, 2)
    dtb = outer_gathered(dt_bias, 1).astype(f32)
    conv_w = outer_gathered(conv_weight, 1).astype(f32)
    conv_b = outer_gathered(conv_bias, 0).astype(f32)
    log_r = outer_gathered(log_rates, 1).astype(f32)
    skip = outer_gathered(skip_gain, 0).astype(f32)
    mine = skip.shape[0]
    places = relative_places()
    pieces_of = lax.axis_size(team_axes)
    relative = jnp.zeros((pieces_of,), jnp.int32).at[places].set(jnp.arange(pieces_of, dtype=jnp.int32))

    counted = jnp.cumsum(starts, axis=1)
    send_keep = counted[:, -1:] - counted[:, local_len - margin :] == 0
    counted_ext = jnp.concatenate([jnp.zeros((rows, margin), jnp.int32), counted], axis=1)
    facts = [counted - counted_ext[:, margin - lag : margin - lag + local_len] == 0 for lag in range(1, taps)]
    facts = [f.astype(f32) for f in facts] + [starts.astype(f32), modality.astype(f32)]
    facts += [jnp.zeros_like(facts[0])] * (fact_columns - len(facts))
    facts = jnp.stack([f.reshape(rows, group, here) for f in facts], axis=2)
    row_label = jnp.transpose(modality.reshape(rows, group, here), (1, 0, 2)).astype(f32)
    facts_flat = facts.reshape(pieces_of, fact_columns, here)
    facts_there = facts_flat[places]
    in_order = jnp.arange(pieces_of, dtype=jnp.int32)

    conv_in, wx_f, normed = lead_pieces(places, normed_pieces, facts_there, wx, bf16)
    conv_in = conv_in.reshape(rows, local_len, mine)
    gate_in, wz_f = lead_product(places, normed, facts_there, wz, f32)
    gate_in = gate_in.reshape(rows, local_len, mine)

    before = jnp.zeros((rows, 8, mine), f32)
    if outer > 1:
        outgoing = jnp.where(send_keep[:, :, None], conv_in[:, local_len - margin :, :], jnp.zeros((), bf16))
        incoming = passed_along(outgoing, "o", 1).astype(f32)
        before = jnp.pad(incoming, ((0, 0), (8 - margin, 0), (0, 0)))
    halves = 2
    pieces = states // halves
    narrow = 2 * states
    xdt_f = xdt.reshape(mine, mods * rank)
    xbc_f = jnp.transpose(xbc.reshape(2, halves, pieces, mods, mine), (3, 1, 0, 2, 4)).reshape(mods * narrow, mine)
    dt_f = dtw.reshape(rank, mods * mine)
    pre, proj_part = conv_block(conv_in, before, facts, row_label, conv_w, conv_b[None], xdt_f, xbc_f)

    def summed(part, beside, final):
        return team_sum(part.reshape((2, 2, depth, 2) + part.shape[2:]), beside, final).reshape(part.shape)

    proj = summed(proj_part, [gate_in], [])
    wo = spread_done(tied(spread_weight(lead(out_weight)), proj))
    d_gated, wo_f = lead_product(in_order, d_branch, facts_flat, wo, f32)
    d_gated = d_gated.reshape(rows, local_len, mine)
    decay_coef = -jnp.exp(log_r)

    def per_state(values):
        split = jnp.transpose(values.reshape(halves, pieces, mine), (1, 0, 2))
        return jnp.repeat(split, rows, axis=1)

    rates = per_state(decay_coef)
    rates2 = rates * (1.0 / math.log(2.0))
    zero_state = jnp.zeros((pieces, halves * rows, mine), f32)
    skip_row = skip[None]
    dtb_row = dtb.reshape(1, mods * mine)

    def ahead(start):
        return scan_forward(proj, pre, facts, gate_in, dt_f, dtb_row, rates2, skip_row, start)

    gated, scanned, dt_pre, kept, last_state = ahead(zero_state)
    if outer > 1:
        steps = jnp.sum(jax.nn.softplus(dt_pre), axis=1)
        unbroken = (jnp.sum(starts, axis=1) == 0).astype(f32)[:, None]
        passing = jnp.exp2(jnp.concatenate([steps] * halves, axis=0)[None] * rates2)
        passing = passing * jnp.concatenate([unbroken] * halves, axis=0)[None]
        gated, scanned, dt_pre, kept, last_state = ahead(entering_state(passing, last_state, False))
    gated = gated.reshape(pieces_of, here, mine)
    branch = trail_product([gated], facts_flat, [wo_f], mods)[0].reshape(count, width)
    own_branch = lax.psum_scatter(branch, team_axes, scatter_dimension=0, tiled=True).astype(f32)
    block_out = (inputs + own_valid * own_branch).astype(bf16)[None]
    grad_type = f32 if outer > 1 else bf16

    def weight_grad(x, d, there, *beside):
        return feature_grad(x, d, there, mods, outer * group, grad_type, beside)

    out_parts = weight_grad(d_branch, gated, facts_flat)

    def back(carry):
        return scan_backward(
            relative, proj, pre, facts, gate_in, scanned, dt_pre, d_gated, kept, dt_f, rates2, rates, skip_row, last_state,
            carry,
        )

    results = back(zero_state)
    if outer > 1:
        results = back(entering_state(passing, results[-1], True))
    d_gate, d_proj_part, d_act, dtw_grad, dtb_grad, skip_grad, rate_total, _ = results
    z_parts = weight_grad(normed, d_gate, facts_there)
    out_got, z_got = collect(out_parts), collect(z_parts)
    d_proj = summed(d_proj_part, [out_parts, z_parts], [])
    out_weight_grad = lead(settled(out_got, lead(out_weight))[0])
    in_z_grad, gain_z = settled(z_got, lead(in_z_weight))
    rate_total = jnp.sum(rate_total.reshape(pieces, halves, rows, mine), axis=2)
    rate_total = jnp.transpose(rate_total, (1, 0, 2)).reshape(states, mine)
    log_rates_grad = outer_summed(decay_coef * rate_total, 1)
    skip_gain_grad = outer_summed(skip_grad[0], 0)
    dt_weight_grad = outer_summed(dtw_grad.reshape(rank, mods, mine), 2)
    dt_bias_grad = outer_summed(dtb_grad.reshape(mods, mine), 1)
    d_conv, xdt_grad, xbc_grad, taps_grad, bias_grad, head, tail = deconv_block(
        relative, d_proj, conv_in, pre, d_act, facts, row_label, conv_w, xdt_f, xbc_f
    )
    if outer > 1:
        early = jnp.stack(
            [jnp.pad(head[:, lag - 1, :lag], ((0, 0), (margin - lag, 0), (0, 0))) for lag in range(1, taps)], axis=1
        )
        taps_grad = taps_grad.at[1:].add(jnp.sum(early * incoming[:, None], axis=(0, 2)))
        returned = jnp.sum(early * conv_w[None, 1:, None, :], axis=1)
        returned = passed_along(returned.astype(bf16), "o", -1).astype(f32)
        returned = jnp.where(send_keep[:, :, None], returned, 0.0)
        fixed = (tail[:, 8 - margin :] + returned).astype(bf16)
        spots = relative[jnp.arange(rows) * group + group - 1]
        d_conv = d_conv.at[spots, here - margin :].set(fixed)
    xdt_grad = outer_summed(xdt_grad.reshape(mine, mods, rank), 0)
    xbc_grad = jnp.transpose(xbc_grad.reshape(mods, halves, 2, pieces, mine), (2, 1, 3, 0, 4)).reshape(narrow, mods, mine)
    xbc_grad = outer_summed(xbc_grad, 2)
    conv_weight_grad = outer_summed(taps_grad, 1)
    conv_bias_grad = outer_summed(bias_grad[0], 0)
    d_scaled, x_parts = team_scatter(
        lambda k, others: trail_product([d_conv, d_gate], facts_there, [wx_f, wz_f], mods, k, others),
        lambda others: weight_grad(normed, d_conv, facts_there, out_got, *others),
    )
    d_scaled = d_scaled * gain
    in_x_grad, gain_x = settled(collect(tied(x_parts, z_got)), lead(in_x_weight))
    d_inputs = inv_rms * (d_scaled - scaled * jnp.mean(d_scaled * scaled, axis=-1, keepdims=True))
    tokens_grad = (upstream + d_inputs).astype(bf16)[None]
    gain_part = gain_x + gain_z
    for name in row_axes:
        gain_part = gain_part + lax.ppermute(gain_part, name, [(0, 1), (1, 0)])
    norm_gain_grad = gain_part / norm_gain.astype(f32)
    in_x_grad, in_z_grad = lead(in_x_grad), lead(in_z_grad)
    return (
        block_out,
        tokens_grad,
        norm_gain_grad,
        in_x_grad,
        in_z_grad,
        xdt_grad,
        xbc_grad,
        dt_weight_grad,
        dt_bias_grad,
        conv_weight_grad,
        conv_bias_grad,
        log_rates_grad,
        skip_gain_grad,
        out_weight_grad,
    )


def solution(mesh):
    rows, seq = mesh.shape["row"], mesh.shape["seq"]
    across = 2 if rows % 2 == 0 else 1
    cores = 2 if seq % 2 == 0 else 1
    along = next(n for n in (4, 3, 2, 1) if (seq // cores) % n == 0)
    fine = Mesh(
        mesh.devices.reshape(rows // across, across, seq // (along * cores), along, cores), ("y", "x", "o", "z", "c")
    )
    row, seq, both = row_axes, seq_axes, row_axes + seq_axes
    in_specs = (
        P(row, seq, None),
        P(row, seq, None),
        P(None, seq),
        P(None, seq),
        P(),
        P(seq),
        P(seq, None, row),
        P(seq, None, row),
        P(both, None, None),
        P(None, None, both),
        P(None, None, both),
        P(None, both),
        P(None, both),
        P(both),
        P(None, both),
        P(both),
        P(seq, None, row),
    )
    out_specs = (
        P(row, seq, None),
        P(row, seq, None),
        P(seq),
        P(seq, None, row),
        P(seq, None, row),
        P(both, None, None),
        P(None, None, both),
        P(None, None, both),
        P(None, both),
        P(None, both),
        P(both),
        P(None, both),
        P(both),
        P(seq, None, row),
    )
    return jax.shard_map(on_device, mesh=fine, in_specs=in_specs, out_specs=out_specs, check_vma=False)
```

```python
import functools
import math

import jax
import jax.numpy as jnp
from jax import lax
from jax.experimental import pallas as pl
from jax.experimental.pallas import tpu as pltpu
from jax.sharding import Mesh
from jax.sharding import PartitionSpec as P

epsilon = 1e-05
row_axes = ("y", "x")
group_axes = ("z", "c")
seq_axes = ("o", "z", "c")
team_axes = ("y", "x", "z", "c")
bf16 = jnp.bfloat16
f32 = jnp.float32
lanes = 128
huge_step = 1e6
vmem_bytes = 48 * 1024 * 1024


def apply_silu(values):
    return values * jax.nn.sigmoid(values)


def silu_slope(values):
    sigmoid_of = jax.nn.sigmoid(values)
    return sigmoid_of * (1.0 + values * (1.0 - sigmoid_of))


def softplus(values):
    tail = jnp.exp(-jnp.abs(values))
    series = tail * (1.0 + tail * (-1 / 2 + tail * (1 / 3 + tail * (-1 / 4 + tail * (1 / 5 - tail * (1 / 6))))))
    return jnp.maximum(values, 0.0) + jnp.where(tail < 0.05, series, jnp.log(1.0 + tail))


def dot(a, b, contract):
    return lax.dot_general(a, b, (contract, ((), ())), preferred_element_type=f32)


def chosen(values, label, mods, axis=1):
    wide = values.shape[axis] // mods
    parts = [lax.slice_in_dim(values, m * wide, (m + 1) * wide, axis=axis) for m in range(mods)]
    picked = parts[0]
    for m in range(1, mods):
        picked = jnp.where(label == m, parts[m], picked)
    return picked


def placed(values, label, mods, axis=1):
    wide = values.astype(f32)
    return jnp.concatenate([jnp.where(label == m, wide, 0.0) for m in range(mods)], axis=axis).astype(values.dtype)


start_column, label_column, fact_columns = 3, 4, 8


def columns_of(facts):
    missing = facts.shape[1] - facts.shape[0]
    return jnp.transpose(jnp.concatenate([facts, jnp.zeros((missing, facts.shape[1]), f32)], axis=0))


def label_column_of(facts_ref):
    return jnp.concatenate(
        [columns_of(facts_ref[j])[:, label_column : label_column + 1] for j in range(facts_ref.shape[0])], axis=0
    )


params = functools.partial(pltpu.CompilerParams, vmem_limit_bytes=vmem_bytes)


def everything(array):
    return pl.BlockSpec(array.shape, lambda i, rank=len(array.shape): (0,) * rank)


def scalars():
    return pl.BlockSpec(memory_space=pltpu.SMEM)


def shape(dims, dtype):
    return jax.ShapeDtypeStruct(dims, dtype)


def cost(flops, nbytes):
    return pl.CostEstimate(flops=int(flops), bytes_accessed=int(nbytes), transcendentals=0)


def assemble(weight_ref, whole):
    pieces, mods, some, wide = weight_ref.shape
    for i in range(pieces):
        for m in range(mods):
            whole[i * some : (i + 1) * some, m * wide : (m + 1) * wide] = weight_ref[i, m]


def lead_kernel(mods, places, x_ref, facts_ref, weight_ref, out_ref, whole):
    @pl.when(pl.program_id(0) == 0)
    def _():
        assemble(weight_ref, whole)

    some, here, wide = x_ref.shape
    label = label_column_of(facts_ref)
    picked = chosen(dot(x_ref[...].reshape(some * here, wide), whole[...], ((1,), (0,))), label, mods)
    for j in range(some):
        out_ref[places[pl.program_id(0) * some + j]] = picked[j * here : (j + 1) * here].astype(out_ref.dtype)


def lead_product(places, x, facts, weight, dtype):
    pieces, here, wide = x.shape
    groups, mods, some, mine = weight.shape
    outs = [shape((pieces, here, mine), dtype), shape((groups * some, mods * mine), bf16)]
    return pl.pallas_call(
        functools.partial(lead_kernel, mods),
        grid=(pieces // 4,),
        in_specs=[
            scalars(),
            pl.BlockSpec((4, here, wide), lambda i: (i, 0, 0)),
            pl.BlockSpec((4, fact_columns, here), lambda i: (i, 0, 0)),
            everything(weight),
        ],
        out_specs=[everything(out) for out in outs],
        out_shape=outs,
        compiler_params=params(),
        cost_estimate=cost(2 * pieces * here * wide * mods * mine, 2 * pieces * here * wide),
        name="lead_product",
    )(places, x, facts, weight)


def lead_pieces_kernel(mods, count, places, facts_ref, weight_ref, *refs):
    pieces = refs[:count]
    out_ref, whole, all_ref, buffer, in_sems, out_sems = refs[count:]
    _, some, here, wide = buffer.shape
    assemble(weight_ref, whole)

    def fetch(i):
        return [
            pltpu.make_async_copy(pieces[i * some + j], buffer.at[i % 2, j], in_sems.at[i % 2, j]) for j in range(some)
        ]

    def store(i):
        return pltpu.make_async_copy(buffer.at[i % 2], all_ref.at[pl.ds(i * some, some)], out_sems.at[i % 2])

    steps = count // some
    for copy in fetch(0):
        copy.start()
    for i in range(steps):
        if i + 1 < steps:
            if i:
                store(i - 1).wait()
            for copy in fetch(i + 1):
                copy.start()
        for copy in fetch(i):
            copy.wait()
        store(i).start()
        label = label_column_of(facts_ref.at[i * some : (i + 1) * some])
        picked = chosen(dot(buffer[i % 2].reshape(some * here, wide), whole[...], ((1,), (0,))), label, mods)
        for j in range(some):
            out_ref[places[i * some + j]] = picked[j * here : (j + 1) * here].astype(out_ref.dtype)
    for i in range(max(steps - 2, 0), steps):
        store(i).wait()


def lead_pieces(places, pieces, facts, weight, dtype):
    here, wide = pieces[0].shape
    count, some = len(pieces), 4
    groups, mods, features, mine = weight.shape
    outs = [
        shape((count, here, mine), dtype),
        shape((groups * features, mods * mine), bf16),
        shape((count, here, wide), bf16),
    ]
    vmem, there = pl.BlockSpec(memory_space=pltpu.VMEM), pl.BlockSpec(memory_space=pl.ANY)
    return pl.pallas_call(
        functools.partial(lead_pieces_kernel, mods, count),
        in_specs=[scalars(), vmem, vmem] + [there] * count,
        out_specs=[vmem, vmem, there],
        out_shape=outs,
        scratch_shapes=[
            pltpu.VMEM((2, some, here, wide), bf16),
            pltpu.SemaphoreType.DMA((2, some)),
            pltpu.SemaphoreType.DMA((2,)),
        ],
        compiler_params=params(),
        cost_estimate=cost(2 * count * here * wide * mods * mine, 4 * count * here * wide),
        name="lead_pieces",
    )(places, facts, weight, *pieces)


def trail_kernel(mods, count, skipped, *refs):
    lefts, facts_ref, weights = refs[:count], refs[count], refs[count + 1 : 2 * count + 1]
    outs = refs[2 * count + 1 + skipped :]
    some, here, mine = lefts[0].shape
    label = label_column_of(facts_ref)
    total = None
    for left, weight in zip(lefts, weights):
        term = dot(placed(left[...].reshape(some * here, mine), label, mods), weight[...], ((1,), (1,)))
        total = term if total is None else total + term
    total = total.astype(bf16).reshape(some, here, -1)
    if len(outs) == 1:
        outs[0][...] = total
    else:
        is_far = pl.program_id(0) < pl.num_programs(0) // 2

        @pl.when(is_far)
        def _():
            outs[0][...] = total

        @pl.when(jnp.logical_not(is_far))
        def _():
            outs[1][...] = total


def trail_product(lefts, facts, weights, mods, ks=None, beside=()):
    pieces, here, mine = lefts[0].shape
    features = weights[0].shape[0]
    if ks is None:
        steps, outs = pieces // 4, [shape((pieces, here, features), bf16)]
        out_specs = [pl.BlockSpec((4, here, features), lambda i: (i, 0, 0))]

        def block(i):
            return (i, 0, 0)
    else:
        steps, outs = 4, [shape((8, here, features), bf16)] * 2
        out_specs = [
            pl.BlockSpec((4, here, features), lambda i: (jnp.minimum(i, 1), 0, 0)),
            pl.BlockSpec((4, here, features), lambda i: (jnp.maximum(i - 2, 0), 0, 0)),
        ]

        def block(i):
            return (2 * jnp.where(i % 2 == 0, ks[0], ks[1]) + jnp.where(i < 2, 1, 0), 0, 0)

    return pl.pallas_call(
        functools.partial(trail_kernel, mods, len(lefts), len(beside)),
        grid=(steps,),
        in_specs=[pl.BlockSpec((4, here, mine), block) for _ in lefts]
        + [pl.BlockSpec((4, fact_columns, here), block)]
        + [everything(weight) for weight in weights]
        + [pl.BlockSpec(memory_space=pl.ANY) for _ in beside],
        out_specs=out_specs,
        out_shape=outs,
        compiler_params=params(),
        cost_estimate=cost(
            8 * steps * here * features * mods * mine * len(lefts), 8 * steps * here * features
        ),
        name="trail_product",
    )(*lefts, facts, *weights, *beside)


def grad_kernel(mods, x_ref, d_ref, facts_ref, *refs):
    out_ref, spread = refs[-2:]
    pieces, here, mine = d_ref.shape

    @pl.when(pl.program_id(0) == 0)
    def _():
        for i in range(pieces):
            label = columns_of(facts_ref[i])[:, label_column : label_column + 1]
            spread[i * here : (i + 1) * here] = placed(d_ref[i], label, mods)

    out_ref[0] = dot(x_ref[...], spread[...], ((0,), (0,))).astype(out_ref.dtype)


def feature_grad(x, d, facts, mods, groups, dtype, beside=()):
    pieces, here, wide = x.shape
    mine = d.shape[2]
    some = min(256, wide)
    out = shape((wide // some, some, mods * mine), dtype)
    grad = pl.pallas_call(
        functools.partial(grad_kernel, mods),
        grid=(wide // some,),
        in_specs=[
            pl.BlockSpec((pieces * here, some), lambda i: (0, i)),
            everything(d),
            everything(facts),
        ]
        + [pl.BlockSpec(memory_space=pl.ANY) for _ in beside],
        out_specs=pl.BlockSpec((1, some, mods * mine), lambda i: (i, 0, 0)),
        out_shape=out,
        scratch_shapes=[pltpu.VMEM((pieces * here, mods * mine), bf16)],
        compiler_params=params(),
        cost_estimate=cost(6 * pieces * here * wide * mods * mine, 2 * pieces * here * wide),
        name="feature_grad",
    )(x.reshape(pieces * here, wide), d, facts, *beside)
    return grad.reshape(groups, wide // groups, mods * mine)


def settle_kernel(got_ref, weight_ref, out_ref, sum_ref):
    mods, _, mine = out_ref.shape

    @pl.when(pl.program_id(0) == 0)
    def _():
        sum_ref[...] = jnp.zeros_like(sum_ref)

    for m in range(mods):
        grad = got_ref[0, :, m * mine : (m + 1) * mine].astype(f32)
        out_ref[m] = grad
        sum_ref[...] += grad * weight_ref[m].astype(f32)


def settle(got, weight):
    sources, some, columns = got.shape
    mods, _, wide = weight.shape
    mine = wide // sources
    item = pl.BlockSpec((mods, some, mine), lambda i: (0, 0, i))
    outs = [shape(weight.shape, f32), shape((some, mine), f32)]
    return pl.pallas_call(
        settle_kernel,
        grid=(sources,),
        in_specs=[pl.BlockSpec((1, some, columns), lambda i: (i, 0, 0)), item],
        out_specs=[item, everything(outs[1])],
        out_shape=outs,
        compiler_params=params(),
        cost_estimate=cost(0, 8 * mods * some * wide),
        name="settle",
    )(got, weight)


def conv_kernel(mods, conv_ref, before_ref, facts_ref, row_label_ref, taps_ref, bias_ref, xdt_ref, xbc_ref, pre_ref, proj_ref, carried, line):
    rows, here, mine = conv_ref.shape

    @pl.when(pl.program_id(0) == 0)
    def _():
        carried[...] = before_ref[...]

    for r in range(rows):
        block = conv_ref[r].astype(f32)
        line[:8] = carried[r]
        line[8:] = block
        facts = columns_of(facts_ref[r, 0])
        pre = bias_ref[...] + taps_ref[0:1] * block
        for lag in range(1, taps_ref.shape[0]):
            pre = pre + taps_ref[lag : lag + 1] * (facts[:, lag - 1 : lag] * line[8 - lag : 8 - lag + here])
        carried[r] = block[here - 8 :]
        pre_ref[r] = pre
        low = apply_silu(pre).astype(bf16)
        wide = chosen(dot(low, xdt_ref[...], ((1,), (0,))), facts[:, label_column : label_column + 1], mods)
        small = chosen(dot(xbc_ref[...], low, ((1,), (1,))), row_label_ref[0, r : r + 1], mods, 0)
        proj_ref[r, 0, :here] = wide.astype(bf16)
        proj_ref[r, 0, here:] = small.astype(bf16)


def conv_block(conv_in, before, facts, row_label, taps, bias, xdt, xbc):
    rows, length, mine = conv_in.shape
    blocks, _, here = row_label.shape
    mods = xdt.shape[1] // here
    narrow = xbc.shape[0] // mods
    item = pl.BlockSpec((rows, here, mine), lambda i: (0, i, 0))
    return pl.pallas_call(
        functools.partial(conv_kernel, mods),
        grid=(blocks,),
        in_specs=[
            item,
            everything(before),
            pl.BlockSpec((rows, 1, fact_columns, here), lambda i: (0, i, 0, 0)),
            pl.BlockSpec((1, rows, here), lambda i: (i, 0, 0)),
        ]
        + [everything(array) for array in (taps, bias, xdt, xbc)],
        out_specs=[item, pl.BlockSpec((rows, 1, here + narrow, here), lambda i: (0, i, 0, 0))],
        out_shape=[shape(conv_in.shape, f32), shape((rows, blocks, here + narrow, here), bf16)],
        scratch_shapes=[pltpu.VMEM((rows, 8, mine), f32), pltpu.VMEM((8 + here, mine), f32)],
        compiler_params=params(),
        cost_estimate=cost(20000 * rows * length * mine, 10 * rows * length * mine),
        name="conv_block",
    )(conv_in, before, facts, row_label, taps, bias, xdt, xbc)


def coefficient_lines(proj_ref, rows, here, line):
    narrow = proj_ref.shape[2] - here
    for r in range(rows):
        small = proj_ref[r, 0, here:].astype(f32)
        small = jnp.concatenate([small, jnp.zeros((here - narrow, here), f32)], axis=0)
        turned = jnp.transpose(small)
        line[r * here : (r + 1) * here] = turned
        line[(rows + r) * here : (rows + r + 1) * here] = pltpu.roll(turned, here - narrow // 2, 1)


def coefficient_tiles(proj_ref, rows, here, expand_ref, turned, tiles):
    narrow = proj_ref.shape[2] - here
    for r in range(rows):
        small = proj_ref[r, 0, here:].astype(f32)
        small = jnp.transpose(jnp.concatenate([small, jnp.zeros((here - narrow, here), f32)], axis=0))
        turned[pl.ds(r, here, stride=2 * rows), :] = small
        turned[pl.ds(rows + r, here, stride=2 * rows), :] = pltpu.roll(small, here - narrow // 2, 1)
    some = 256
    for i in range(turned.shape[0] // some):
        part = slice(i * some, (i + 1) * some)
        tiles[part] = dot(turned[part].astype(bf16), expand_ref[...], ((1,), (0,)))


def scan_lines(r, rows, here, value, line):
    line[r * here : (r + 1) * here] = value
    line[(rows + r) * here : (rows + r + 1) * here] = value


def forward_kernel(
    mods, proj_ref, pre_ref, facts_ref, gate_ref, dtw_ref, dtb_ref, rate_ref, skip_ref, start_ref, expand_ref,
    gated_ref, scanned_ref, dt_ref, kept_ref, end_ref, held, step_line, drive_line, turned, tiles, out_line,
):
    rows, here, mine = pre_ref.shape
    pieces, subl, _ = rate_ref.shape

    @pl.when(pl.program_id(0) == 0)
    def _():
        held[...] = start_ref[...]

    coefficient_tiles(proj_ref, rows, here, expand_ref, turned, tiles)
    for r in range(rows):
        facts = columns_of(facts_ref[r, 0])
        label = facts[:, label_column : label_column + 1]
        dt_pre = chosen(dot(proj_ref[r, 0, :here], dtw_ref[...], ((1,), (0,))) + dtb_ref[...], label, mods)
        dt_ref[r] = dt_pre
        step = softplus(dt_pre)
        scan_lines(r, rows, here, step * apply_silu(pre_ref[r]), drive_line)
        scan_lines(r, rows, here, jnp.where(facts[:, start_column : start_column + 1] > 0, huge_step, step), step_line)

    def one(t, state):
        lines = pl.ds(t, subl, stride=here)
        step, drive = step_line[lines, :], drive_line[lines, :]
        spot = pl.ds(pl.multiple_of(t * subl, subl), subl)
        emitted = None
        following = []
        for j in range(pieces):
            kept_ref[t, j] = state[j]
            decay = jnp.exp2(step * rate_ref[j])
            now = decay * state[j] + drive * tiles[spot, j * mine : (j + 1) * mine]
            term = now * tiles[spot, (pieces + j) * mine : (pieces + j + 1) * mine]
            emitted = term if emitted is None else emitted + term
            following.append(now)
        out_line[lines, :] = emitted
        return tuple(following)

    def eight(block, state):
        for i in range(8):
            state = one(block * 8 + i, state)
        return state

    state = lax.fori_loop(0, here // 8, eight, tuple(held[j] for j in range(pieces)))
    for j in range(pieces):
        held[j] = state[j]
        end_ref[j] = state[j]
    for r in range(rows):
        emitted = out_line[r * here : (r + 1) * here] + out_line[(rows + r) * here : (rows + r + 1) * here]
        scanned = emitted + skip_ref[...] * apply_silu(pre_ref[r])
        scanned_ref[r] = scanned
        gated_ref[r] = (scanned * apply_silu(gate_ref[r])).astype(bf16)


def scan_forward(proj, pre, facts, gate, dtw, dtb, rates2, skip, start):
    rows, length, mine = pre.shape
    _, blocks, deep, here = proj.shape
    pieces, subl, _ = rates2.shape
    item = pl.BlockSpec((rows, here, mine), lambda i: (0, i, 0))
    line = pltpu.VMEM((subl * here, mine), f32)
    expand = (jnp.arange(here)[:, None] == jnp.arange(2 * pieces * mine)[None, :] // mine).astype(bf16)
    return pl.pallas_call(
        functools.partial(forward_kernel, dtw.shape[1] // mine),
        grid=(blocks,),
        in_specs=[
            pl.BlockSpec((rows, 1, deep, here), lambda i: (0, i, 0, 0)),
            item,
            pl.BlockSpec((rows, 1, fact_columns, here), lambda i: (0, i, 0, 0)),
            item,
        ]
        + [everything(array) for array in (dtw, dtb, rates2, skip, start, expand)],
        out_specs=[
            item,
            item,
            item,
            pl.BlockSpec((here, pieces, subl, mine), lambda i: (i, 0, 0, 0)),
            everything(start),
        ],
        out_shape=[
            shape(pre.shape, bf16),
            shape(pre.shape, f32),
            shape(pre.shape, f32),
            shape((length, pieces, subl, mine), f32),
            shape(start.shape, f32),
        ],
        scratch_shapes=[pltpu.VMEM(start.shape, f32), line, line, line]
        + [pltpu.VMEM((subl * here, 2 * pieces * mine), f32), line],
        compiler_params=params(),
        cost_estimate=cost(5500 * length * pieces * subl * mine, 5 * length * pieces * subl * mine),
        name="scan_forward",
    )(proj, pre, facts, gate, dtw, dtb, rates2, skip, start, expand)


def backward_kernel(
    mods, tables, proj_ref, pre_ref, facts_ref, gate_ref, scanned_ref, dt_ref, d_gated_ref, kept_ref, dtw_ref, rate2_ref,
    rate_ref, skip_ref, last_ref, carry_ref, sum_ref, expand_ref, _, d_gate_ref, d_proj_ref, d_act_ref, dtw_grad_ref, dtb_grad_ref,
    skip_grad_ref, rate_sum_ref, carry_out_ref, carried, later, products, step_line, drive_line, turned, tiles, back_line,
    pulled_line, weighted_line, small_line,
):
    rows, here, mine = pre_ref.shape
    blocks = tables.shape[0] // rows
    narrow = proj_ref.shape[2] - here
    pieces, subl, _ = rate_ref.shape
    place = blocks - 1 - pl.program_id(0)

    @pl.when(pl.program_id(0) == 0)
    def _():
        carried[...] = carry_ref[...]
        later[...] = last_ref[...]
        for ref in (rate_sum_ref, dtw_grad_ref, dtb_grad_ref, skip_grad_ref):
            ref[...] = jnp.zeros_like(ref)

    coefficient_tiles(proj_ref, rows, here, expand_ref, turned, tiles)
    for r in range(rows):
        facts = columns_of(facts_ref[r, 0])
        step, activated = softplus(dt_ref[r]), apply_silu(pre_ref[r])
        gate, d_gated = gate_ref[r], d_gated_ref[r]
        d_scan = d_gated * apply_silu(gate)
        d_gate_ref[tables[r * blocks + place]] = (d_gated * scanned_ref[r] * silu_slope(gate)).astype(bf16)
        skip_grad_ref[...] += jnp.sum(d_scan * activated, axis=0, keepdims=True)
        scan_lines(r, rows, here, d_scan, back_line)
        scan_lines(r, rows, here, step * activated, drive_line)
        scan_lines(r, rows, here, jnp.where(facts[:, start_column : start_column + 1] > 0, huge_step, step), step_line)

    def one(t, carry, state):
        lines = pl.ds(t, subl, stride=here)
        step, drive, back = step_line[lines, :], drive_line[lines, :], back_line[lines, :]
        row = pl.ds(pl.multiple_of(t * subl, subl), subl)
        pulled_sum, weighted_sum = None, None
        new_carry, new_state, terms, sums = [], [], [], []
        for j in range(pieces):
            before = kept_ref[t, j]
            decay = jnp.exp2(step * rate2_ref[j])
            adjoint = back * tiles[row, (pieces + j) * mine : (pieces + j + 1) * mine] + carry[j]
            passed = decay * adjoint
            pulled = passed * before
            weighted = adjoint * tiles[row, j * mine : (j + 1) * mine]
            first = pulled * rate_ref[j]
            pulled_sum = first if pulled_sum is None else pulled_sum + first
            weighted_sum = weighted if weighted_sum is None else weighted_sum + weighted
            terms.append((adjoint * drive, back * state[j]))
            sums.append(pulled * step)
            new_carry.append(passed)
            new_state.append(before)
        pulled_line[lines, :] = pulled_sum
        weighted_line[lines, :] = weighted_sum
        return new_carry, new_state, terms, sums

    def eight(k, loop):
        carry, state, rates = loop
        block = here // 8 - 1 - k
        rates = list(rates)
        for i in (6, 4, 2, 0):
            t = block * 8 + i
            carry, state, terms_b, sums_b = one(t + 1, carry, state)
            carry, state, terms_a, sums_a = one(t, carry, state)
            spot = pl.ds(pl.multiple_of(t * subl, 16), 16)
            for j in range(pieces):
                rates[j] = rates[j] + (sums_a[j] + sums_b[j])
                for part in range(2):
                    column = (part * pieces + j) * mine
                    products[spot, column : column + mine] = jnp.concatenate(
                        [terms_a[j][part], terms_b[j][part]], axis=0
                    ).astype(bf16)
        return tuple(carry), tuple(state), tuple(rates)

    begin = tuple(tuple(ref[j] for j in range(pieces)) for ref in (carried, later, rate_sum_ref))
    carry, state, rates = lax.fori_loop(0, here // 8, eight, begin)
    for j in range(pieces):
        carried[j] = carry[j]
        later[j] = state[j]
        rate_sum_ref[j] = rates[j]
        carry_out_ref[j] = carry[j]
    small_line[...] = dot(products[...], sum_ref[...], ((1,), (0,)))
    for r in range(rows):
        label = columns_of(facts_ref[r, 0])[:, label_column : label_column + 1]
        dt_pre, activated = dt_ref[r], apply_silu(pre_ref[r])
        near, far = slice(r * here, (r + 1) * here), slice((rows + r) * here, (rows + r + 1) * here)
        weighted = weighted_line[near] + weighted_line[far]
        d_step = pulled_line[near] + pulled_line[far] + activated * weighted
        d_act_ref[r] = back_line[near] * skip_ref[...] + softplus(dt_pre) * weighted
        d_dt = placed((d_step * jax.nn.sigmoid(dt_pre)).astype(bf16), label, mods)
        dtw_grad_ref[...] += dot(proj_ref[r, 0, :here], d_dt, ((0,), (0,)))
        dtb_grad_ref[...] += jnp.sum(d_dt.astype(f32), axis=0, keepdims=True)
        d_proj_ref[r, 0, :here] = dot(d_dt, dtw_ref[...], ((1,), (1,))).astype(bf16)
        one_half = small_line[pl.ds(r, here, stride=subl), :]
        other_half = small_line[pl.ds(rows + r, here, stride=subl), :]
        small = jnp.transpose(one_half + pltpu.roll(other_half, narrow // 2, 1))
        d_proj_ref[r, 0, here:] = small[:narrow].astype(bf16)


def scan_backward(
    tables, proj, pre, facts, gate, scanned, dt_pre, d_gated, kept, dtw, rates2, rates, skip, last, carry, beside
):
    rows, length, mine = pre.shape
    _, blocks, deep, here = proj.shape
    pieces, subl, _ = rates2.shape
    item = pl.BlockSpec((rows, here, mine), lambda i: (0, blocks - 1 - i, 0))
    proj_item = pl.BlockSpec((rows, 1, deep, here), lambda i: (0, blocks - 1 - i, 0, 0))
    columns = 2 * pieces * mine
    expand = (jnp.arange(here)[:, None] == jnp.arange(columns)[None, :] // mine).astype(bf16)
    summing = (jnp.arange(columns)[:, None] // mine == jnp.arange(lanes)[None, :]).astype(bf16)
    d_gate = shape((rows * blocks, here, mine), bf16)
    line = pltpu.VMEM((subl * here, mine), f32)
    small = [shape((here, dtw.shape[1]), f32), shape((1, dtw.shape[1]), f32), shape((1, mine), f32), shape(carry.shape, f32)]
    return pl.pallas_call(
        functools.partial(backward_kernel, dtw.shape[1] // mine),
        grid=(blocks,),
        in_specs=[
            scalars(),
            proj_item,
            item,
            pl.BlockSpec((rows, 1, fact_columns, here), lambda i: (0, blocks - 1 - i, 0, 0)),
            item,
            item,
            item,
            item,
            pl.BlockSpec((here, pieces, subl, mine), lambda i: (blocks - 1 - i, 0, 0, 0)),
        ]
        + [everything(array) for array in (dtw, rates2, rates, skip, last, carry, summing, expand)]
        + [pl.BlockSpec(memory_space=pl.ANY)],
        out_specs=[everything(d_gate), proj_item, item] + [everything(array) for array in small + [carry]],
        out_shape=[d_gate, shape(proj.shape, bf16), shape(pre.shape, f32)] + small + [shape(carry.shape, f32)],
        scratch_shapes=[pltpu.VMEM(carry.shape, f32)] * 2 + [pltpu.VMEM((subl * here, columns), bf16)] + [line] * 3
        + [pltpu.VMEM((subl * here, columns), f32)] + [line] * 4,
        compiler_params=params(),
        cost_estimate=cost(7500 * length * pieces * subl * mine, 5 * length * pieces * subl * mine),
        name="scan_backward",
    )(tables, proj, pre, facts, gate, scanned, dt_pre, d_gated, kept, dtw, rates2, rates, skip, last, carry, summing, expand, beside)


def deconv_kernel(
    mods, tables, d_proj_ref, conv_ref, pre_ref, d_act_ref, facts_ref, row_label_ref, taps_ref, xdt_ref, xbc_ref,
    d_conv_ref, xdt_grad_ref, xbc_grad_ref, taps_grad_ref, bias_grad_ref, head_ref, tail_ref, carried, line,
):
    rows, here, mine = pre_ref.shape
    blocks = tables.shape[0] // rows
    taps = taps_ref.shape[0]
    place = blocks - 1 - pl.program_id(0)

    @pl.when(pl.program_id(0) == 0)
    def _():
        carried[...] = jnp.zeros_like(carried)
        for ref in (xdt_grad_ref, xbc_grad_ref, taps_grad_ref, bias_grad_ref):
            ref[...] = jnp.zeros_like(ref)

    for r in range(rows):
        facts = columns_of(facts_ref[r, 0])
        pre = pre_ref[r]
        low = apply_silu(pre).astype(bf16)
        d_rank = placed(d_proj_ref[r, 0, :here], facts[:, label_column : label_column + 1], mods)
        d_small = placed(d_proj_ref[r, 0, here:], row_label_ref[0, r : r + 1], mods, 0)
        xdt_grad_ref[...] += dot(low, d_rank, ((0,), (0,)))
        xbc_grad_ref[...] += dot(d_small, low, ((1,), (0,)))
        d_act = d_act_ref[r] + dot(d_rank, xdt_ref[...], ((1,), (1,))) + dot(d_small, xbc_ref[...], ((0,), (0,)))
        d_pre = d_act * silu_slope(pre)
        source = conv_ref[r].astype(f32)
        total = taps_ref[0:1] * d_pre
        bias_grad_ref[...] += jnp.sum(d_pre, axis=0, keepdims=True)
        taps_grad_ref[0:1] += jnp.sum(source * d_pre, axis=0, keepdims=True)
        for lag in range(1, taps):
            kept = facts[:, lag - 1 : lag] * d_pre
            line[:here] = kept
            line[here:] = carried[r, lag - 1]
            carried[r, lag - 1] = kept[:8]
            moved = line[lag : lag + here]
            total = total + taps_ref[lag : lag + 1] * moved
            taps_grad_ref[lag : lag + 1] += jnp.sum(source * moved, axis=0, keepdims=True)
        d_conv_ref[tables[r * blocks + place]] = total.astype(bf16)

        @pl.when(pl.program_id(0) == 0)
        def _():
            tail_ref[r] = total[here - 8 :]

    head_ref[...] = carried[...]


def deconv_block(tables, d_proj, conv_in, pre, d_act, facts, row_label, taps, xdt, xbc):
    rows, length, mine = pre.shape
    _, blocks, deep, here = d_proj.shape
    item = pl.BlockSpec((rows, here, mine), lambda i: (0, blocks - 1 - i, 0))
    outs = [
        shape((rows * blocks, here, mine), bf16),
        shape(xdt.shape, f32),
        shape(xbc.shape, f32),
        shape(taps.shape, f32),
        shape((1, mine), f32),
        shape((rows, taps.shape[0] - 1, 8, mine), f32),
        shape((rows, 8, mine), f32),
    ]
    return pl.pallas_call(
        functools.partial(deconv_kernel, xdt.shape[1] // here),
        grid=(blocks,),
        in_specs=[
            scalars(),
            pl.BlockSpec((rows, 1, deep, here), lambda i: (0, blocks - 1 - i, 0, 0)),
            item,
            item,
            item,
            pl.BlockSpec((rows, 1, fact_columns, here), lambda i: (0, blocks - 1 - i, 0, 0)),
            pl.BlockSpec((1, rows, here), lambda i: (blocks - 1 - i, 0, 0)),
        ]
        + [everything(array) for array in (taps, xdt, xbc)],
        out_specs=[everything(array) for array in outs],
        out_shape=outs,
        scratch_shapes=[pltpu.VMEM(outs[5].shape, f32), pltpu.VMEM((here + 8, mine), f32)],
        compiler_params=params(),
        cost_estimate=cost(30000 * rows * length * mine, 14 * rows * length * mine),
        name="deconv_block",
    )(tables, d_proj, conv_in, pre, d_act, facts, row_label, taps, xdt, xbc)


def passed_along(value, axis, by):
    size = lax.axis_size(axis)
    return lax.ppermute(value, axis, [(i, i + by) for i in range(size) if 0 <= i + by < size])


def shifted(value, by):
    size = lax.axis_size("z")
    return value if by % size == 0 else lax.ppermute(value, "z", [(i, (i + by) % size) for i in range(size)])


def swapped(value):
    return lax.ppermute(value, "c", [(0, 1), (1, 0)])


def hop(value, second):
    depth = lax.axis_size("z")

    def place(y, x, z, c):
        return ((y * 2 + x) * depth + z) * 2 + c

    pairs = [
        (place(y, x, z, c), place(y, 1 - x, z, c) if (c == 1) == second else place(1 - y, x, z, c))
        for y in range(2)
        for x in range(2)
        for z in range(depth)
        for c in range(2)
    ]
    return lax.ppermute(value, team_axes, pairs)


def relative_places():
    depth = lax.axis_size("z")
    y, x, z, c = (lax.axis_index(name) for name in team_axes)
    n = jnp.arange(4)[None, None, :]
    core = (c + jnp.arange(2)[None, :, None]) % 2
    back = (z - jnp.arange(depth)[:, None, None]) % depth
    one, two = n % 2, n // 2
    flip_x = jnp.where(core == 0, one, two)
    flip_y = jnp.where(core == 0, two, one)
    return (((((y + flip_y) % 2) * 2 + (x + flip_x) % 2) * depth + back) * 2 + core).reshape(-1)


def nothing(*refs):
    pass


def tied(value, *others):
    there = pl.BlockSpec(memory_space=pl.ANY)
    return pl.pallas_call(
        nothing,
        in_specs=[there] * (1 + len(others)),
        out_specs=there,
        out_shape=shape(value.shape, value.dtype),
        input_output_aliases={0: 0},
        name="tied",
    )(value, *others)


def team_gather(value, weight):
    near, first, second, third = {0: value}, {}, {}, {}

    def hops(k):
        first[k], second[k] = hop(near[k], False), hop(near[k], True)

    near[1], near[3] = shifted(value, 1), shifted(value, 3)
    weight = exchanged(tied(weight, near[1]))
    hops(0)
    near[2] = shifted(tied(value, first[0], second[0]), 2)
    third[0] = hop(first[0], True)
    near[1] = tied(near[1], first[0], second[0])
    hops(1)
    third[1] = hop(first[1], True)
    near[3] = tied(near[3], third[0], first[1], second[1])
    hops(3)
    third[3] = hop(first[3], True)
    near[2] = tied(near[2], third[1], first[3], second[3], weight)
    hops(2)
    third[2] = hop(first[2], True)
    parts = []
    for k in range(4):
        pieces = [near[k], first[k], second[k], third[k]]
        parts += pieces + [swapped(piece) for piece in pieces]
    return parts, [first[2], second[2], third[3]], weight


def team_scatter(made, beside):
    def added(*terms):
        return sum(term.astype(f32) for term in terms)

    groups = [(1, 2), (3, 0)]
    far, near = {}, {}
    for i, ks in enumerate(groups):
        away, here = made(ks, [beside[i]])
        far[i] = swapped(away).reshape((len(ks), 4) + away.shape[1:])
        near[i] = here.reshape((len(ks), 4) + here.shape[1:])
    total = None
    for i, ks in enumerate(groups):
        payload = added(near[i][:, 2:], far[i][:, 2:]).astype(bf16)
        come = hop(payload, True)
        last = hop(added(near[i][:, 1], far[i][:, 1], come[:, 1]).astype(bf16), False)
        held = added(near[i][:, 0], far[i][:, 0], come[:, 0], last)
        for j, k in enumerate(ks):
            own = shifted(held[j].astype(bf16), -k).astype(f32) if k else held[j]
            total = own if total is None else total + own
    return total


def exchanged(parts):
    return lax.all_to_all(parts, group_axes, 0, 0, tiled=True)


def spread_weight(weight):
    outer, group = lax.axis_size("o"), lax.axis_size(group_axes)
    mods, here, wide = weight.shape
    each = wide // (outer * group)
    parts = weight.reshape(mods, here, outer, group, each)
    parts = jnp.transpose(parts, (3, 0, 1, 2, 4)).reshape(group, mods, here, outer * each)
    return parts


def through_outer(got):
    return got if lax.axis_size("o") == 1 else lax.all_gather(got, "o", axis=0, tiled=True)


def spread_done(parts):
    return through_outer(exchanged(parts))


def collect(parts):
    if lax.axis_size("o") > 1:
        parts = lax.psum_scatter(parts, "o", scatter_dimension=0, tiled=True)
    return exchanged(parts.astype(bf16))


def settled(got, weight):
    outer, group = lax.axis_size("o"), lax.axis_size(group_axes)
    mods, here, wide = weight.shape
    if outer == 1:
        grad, sums = settle(got, weight)
        return grad, jnp.sum(sums, axis=1)
    got = got.astype(f32).reshape(group, here, mods, outer, wide // (outer * group))
    grad = jnp.transpose(got, (2, 1, 3, 0, 4)).reshape(weight.shape)
    return grad, jnp.sum(grad * weight.astype(f32), axis=(0, 2))


def outer_gathered(value, axis):
    return value if lax.axis_size("o") == 1 else lax.all_gather(value, "o", axis=axis, tiled=True)


def outer_summed(value, axis):
    if lax.axis_size("o") == 1:
        return value
    return lax.psum_scatter(value, "o", scatter_dimension=axis, tiled=True)


def half_of(value, axis, name, other):
    return lax.dynamic_index_in_dim(value, (lax.axis_index(name) + other) % 2, axis, False)


def team_sum(value, beside, final):
    depth = lax.axis_size("z")
    z = lax.axis_index("z")

    def halved(value, axis, name, pairs, *others):
        sent = half_of(value, axis, name, 1).astype(bf16)
        sent = lax.ppermute(tied(sent, *others) if others else sent, name, pairs)
        return half_of(value, axis, name, 0).astype(f32) + sent.astype(f32)

    swap = [(0, 1), (1, 0)]
    held = halved(value, 3, "c", swap)
    held = halved(held, 0, "y", swap)
    held = halved(held, 0, "x", swap, *beside[:1])
    if beside[1:]:
        held = tied(held, *beside[1:])
    own = lax.dynamic_index_in_dim(held, z, 0, False)
    for k in range(1, depth):
        own = own + shifted(lax.dynamic_index_in_dim(held, (z + k) % depth, 0, False).astype(bf16), k).astype(f32)
    own = own.astype(bf16)
    back = jnp.stack([own] + [shifted(own, k) for k in range(1, depth)])
    rolled = back[(z - jnp.arange(depth)) % depth]

    def doubled(value, axis, name):
        other = lax.ppermute(value, name, swap)
        flag = lax.axis_index(name) == 0
        return jnp.stack([jnp.where(flag, value, other), jnp.where(flag, other, value)], axis=axis)

    wide = doubled(doubled(rolled, 0, "x"), 0, "y")
    return doubled(tied(wide, *final) if final else wide, 3, "c")


def entering_state(passing, local_end, backward):
    count, place = lax.axis_size("o"), lax.axis_index("o")
    decays = lax.all_gather(passing.astype(bf16), "o")
    ends = lax.all_gather(local_end.astype(bf16), "o")
    state = jnp.zeros_like(local_end)
    for i in range(count):
        source = count - 1 - i if backward else i
        ahead = source > place if backward else source < place
        state = jnp.where(ahead, decays[source].astype(f32) * state + ends[source].astype(f32), state)
    return state


def on_device(
    tokens,
    cotangent,
    modality,
    starts,
    row_lengths,
    norm_gain,
    in_x_weight,
    in_z_weight,
    xdt_weight,
    xbc_weight,
    dt_weight,
    dt_bias,
    conv_weight,
    conv_bias,
    log_rates,
    skip_gain,
    out_weight,
):
    outer, group = lax.axis_size("o"), lax.axis_size(group_axes)
    rows, here = modality.shape
    width = tokens.shape[-1]
    mods = in_x_weight.shape[1]
    taps, states, rank = conv_weight.shape[0], log_rates.shape[0], dt_weight.shape[0]
    margin = taps - 1
    local_len = group * here
    own_row = lax.axis_index(row_axes)
    count = rows * local_len

    depth = lax.axis_size("z")
    place_z = lax.axis_index("z")

    def lead(weight):
        return jnp.transpose(weight, (1, 0, 2))

    features = norm_gain.shape[0]
    packed = jnp.concatenate(
        [modality.astype(f32).reshape(-1), starts.astype(f32).reshape(-1), norm_gain.astype(f32)]
    )
    packed = jnp.stack([packed] + [shifted(packed, k) for k in range(1, depth)])
    packed = packed[(place_z - jnp.arange(depth)) % depth]
    others, first_core = swapped(packed), lax.axis_index("c") == 0
    packed = jnp.stack([jnp.where(first_core, packed, others), jnp.where(first_core, others, packed)], axis=1)
    labels = packed[:, :, : 2 * rows * here].astype(jnp.int32).reshape(depth, 2, 2, rows, here)
    labels = jnp.transpose(labels, (2, 3, 0, 1, 4)).reshape(2, rows, local_len)
    modality, starts = labels[0], labels[1]
    gain = outer_gathered(packed[:, :, 2 * rows * here :].reshape(-1, features), 0).reshape(width)

    inputs = tokens[0].astype(f32)
    inv_rms = lax.rsqrt(jnp.mean(inputs * inputs, axis=-1, keepdims=True) + epsilon)
    scaled = inputs * inv_rms
    wz = spread_done(spread_weight(lead(in_z_weight)))
    normed_pieces, last_pieces, wx = team_gather((scaled * gain).astype(bf16), spread_weight(lead(in_x_weight)))
    wx = through_outer(wx)
    position = lax.axis_index(seq_axes) * here + jnp.arange(here, dtype=jnp.int32)
    own_valid = (position < lax.dynamic_index_in_dim(row_lengths, own_row, 0, False)).astype(f32)[:, None]
    upstream = cotangent[0].astype(f32)
    own_back = (upstream * own_valid).astype(bf16)
    own_back = tied(own_back, *last_pieces)
    d_branch = lax.all_gather(own_back, team_axes)
    xdt = outer_gathered(xdt_weight, 0)
    xbc = outer_gathered(xbc_weight, 2)
    dtw = outer_gathered(dt_weight, 2)
    dtb = outer_gathered(dt_bias, 1).astype(f32)
    conv_w = outer_gathered(conv_weight, 1).astype(f32)
    conv_b = outer_gathered(conv_bias, 0).astype(f32)
    log_r = outer_gathered(log_rates, 1).astype(f32)
    skip = outer_gathered(skip_gain, 0).astype(f32)
    mine = skip.shape[0]
    places = relative_places()
    pieces_of = lax.axis_size(team_axes)
    relative = jnp.zeros((pieces_of,), jnp.int32).at[places].set(jnp.arange(pieces_of, dtype=jnp.int32))

    counted = jnp.cumsum(starts, axis=1)
    send_keep = counted[:, -1:] - counted[:, local_len - margin :] == 0
    counted_ext = jnp.concatenate([jnp.zeros((rows, margin), jnp.int32), counted], axis=1)
    facts = [counted - counted_ext[:, margin - lag : margin - lag + local_len] == 0 for lag in range(1, taps)]
    facts = [f.astype(f32) for f in facts] + [starts.astype(f32), modality.astype(f32)]
    facts += [jnp.zeros_like(facts[0])] * (fact_columns - len(facts))
    facts = jnp.stack([f.reshape(rows, group, here) for f in facts], axis=2)
    row_label = jnp.transpose(modality.reshape(rows, group, here), (1, 0, 2)).astype(f32)
    facts_flat = facts.reshape(pieces_of, fact_columns, here)
    facts_there = facts_flat[places]
    in_order = jnp.arange(pieces_of, dtype=jnp.int32)

    conv_in, wx_f, normed = lead_pieces(places, normed_pieces, facts_there, wx, bf16)
    conv_in = conv_in.reshape(rows, local_len, mine)
    gate_in, wz_f = lead_product(places, normed, facts_there, wz, f32)
    gate_in = gate_in.reshape(rows, local_len, mine)

    before = jnp.zeros((rows, 8, mine), f32)
    if outer > 1:
        outgoing = jnp.where(send_keep[:, :, None], conv_in[:, local_len - margin :, :], jnp.zeros((), bf16))
        incoming = passed_along(outgoing, "o", 1).astype(f32)
        before = jnp.pad(incoming, ((0, 0), (8 - margin, 0), (0, 0)))
    halves = 2
    pieces = states // halves
    narrow = 2 * states
    xdt_f = xdt.reshape(mine, mods * rank)
    xbc_f = jnp.transpose(xbc.reshape(2, halves, pieces, mods, mine), (3, 1, 0, 2, 4)).reshape(mods * narrow, mine)
    dt_f = dtw.reshape(rank, mods * mine)
    pre, proj_part = conv_block(conv_in, before, facts, row_label, conv_w, conv_b[None], xdt_f, xbc_f)

    def summed(part, beside, final):
        return team_sum(part.reshape((2, 2, depth, 2) + part.shape[2:]), beside, final).reshape(part.shape)

    proj = summed(proj_part, [facts, gate_in], [])
    wo = spread_done(tied(spread_weight(lead(out_weight)), proj))
    d_gated, wo_f = lead_product(in_order, d_branch, facts_flat, wo, f32)
    d_gated = d_gated.reshape(rows, local_len, mine)
    decay_coef = -jnp.exp(log_r)

    def per_state(values):
        split = jnp.transpose(values.reshape(halves, pieces, mine), (1, 0, 2))
        return jnp.repeat(split, rows, axis=1)

    rates = per_state(decay_coef)
    rates2 = rates * (1.0 / math.log(2.0))
    zero_state = jnp.zeros((pieces, halves * rows, mine), f32)
    skip_row = skip[None]
    dtb_row = dtb.reshape(1, mods * mine)

    def ahead(start):
        return scan_forward(proj, pre, facts, gate_in, dt_f, dtb_row, rates2, skip_row, start)

    gated, scanned, dt_pre, kept, last_state = ahead(zero_state)
    if outer > 1:
        steps = jnp.sum(jax.nn.softplus(dt_pre), axis=1)
        unbroken = (jnp.sum(starts, axis=1) == 0).astype(f32)[:, None]
        passing = jnp.exp2(jnp.concatenate([steps] * halves, axis=0)[None] * rates2)
        passing = passing * jnp.concatenate([unbroken] * halves, axis=0)[None]
        gated, scanned, dt_pre, kept, last_state = ahead(entering_state(passing, last_state, False))
    gated = gated.reshape(pieces_of, here, mine)
    branch = trail_product([gated], facts_flat, [wo_f], mods)[0].reshape(count, width)
    own_branch = lax.psum_scatter(branch, team_axes, scatter_dimension=0, tiled=True).astype(f32)
    block_out = (inputs + own_valid * own_branch).astype(bf16)[None]
    grad_type = f32 if outer > 1 else bf16

    def weight_grad(x, d, there, *beside):
        return feature_grad(x, d, there, mods, outer * group, grad_type, beside)

    out_parts = weight_grad(d_branch, gated, facts_flat)

    def back(carry):
        return scan_backward(
            relative, proj, pre, facts, gate_in, scanned, dt_pre, d_gated, kept, dt_f, rates2, rates, skip_row, last_state,
            carry, out_parts,
        )

    results = back(zero_state)
    if outer > 1:
        results = back(entering_state(passing, results[-1], True))
    d_gate, d_proj_part, d_act, dtw_grad, dtb_grad, skip_grad, rate_total, _ = results
    z_parts = weight_grad(normed, d_gate, facts_there)
    out_got, z_got = collect(out_parts), collect(z_parts)
    d_proj = summed(tied(d_proj_part, out_got), [z_parts], [])
    out_weight_grad = lead(settled(out_got, lead(out_weight))[0])
    in_z_grad, gain_z = settled(z_got, lead(in_z_weight))
    rate_total = jnp.sum(rate_total.reshape(pieces, halves, rows, mine), axis=2)
    rate_total = jnp.transpose(rate_total, (1, 0, 2)).reshape(states, mine)
    log_rates_grad = outer_summed(decay_coef * rate_total, 1)
    skip_gain_grad = outer_summed(skip_grad[0], 0)
    dt_weight_grad = outer_summed(dtw_grad.reshape(rank, mods, mine), 2)
    dt_bias_grad = outer_summed(dtb_grad.reshape(mods, mine), 1)
    d_conv, xdt_grad, xbc_grad, taps_grad, bias_grad, head, tail = deconv_block(
        relative, d_proj, conv_in, pre, d_act, facts, row_label, conv_w, xdt_f, xbc_f
    )
    if outer > 1:
        early = jnp.stack(
            [jnp.pad(head[:, lag - 1, :lag], ((0, 0), (margin - lag, 0), (0, 0))) for lag in range(1, taps)], axis=1
        )
        taps_grad = taps_grad.at[1:].add(jnp.sum(early * incoming[:, None], axis=(0, 2)))
        returned = jnp.sum(early * conv_w[None, 1:, None, :], axis=1)
        returned = passed_along(returned.astype(bf16), "o", -1).astype(f32)
        returned = jnp.where(send_keep[:, :, None], returned, 0.0)
        fixed = (tail[:, 8 - margin :] + returned).astype(bf16)
        spots = relative[jnp.arange(rows) * group + group - 1]
        d_conv = d_conv.at[spots, here - margin :].set(fixed)
    xdt_grad = outer_summed(xdt_grad.reshape(mine, mods, rank), 0)
    xbc_grad = jnp.transpose(xbc_grad.reshape(mods, halves, 2, pieces, mine), (2, 1, 3, 0, 4)).reshape(narrow, mods, mine)
    xbc_grad = outer_summed(xbc_grad, 2)
    conv_weight_grad = outer_summed(taps_grad, 1)
    conv_bias_grad = outer_summed(bias_grad[0], 0)
    x_parts = weight_grad(normed, d_conv, facts_there)
    d_scaled = team_scatter(
        lambda ks, others: trail_product([d_conv, d_gate], facts_there, [wx_f, wz_f], mods, ks, others), [z_got, x_parts]
    )
    d_scaled = d_scaled * gain
    in_x_grad, gain_x = settled(collect(x_parts), lead(in_x_weight))
    d_inputs = inv_rms * (d_scaled - scaled * jnp.mean(d_scaled * scaled, axis=-1, keepdims=True))
    tokens_grad = (upstream + d_inputs).astype(bf16)[None]
    gain_part = gain_x + gain_z
    for name in row_axes:
        gain_part = gain_part + lax.ppermute(gain_part, name, [(0, 1), (1, 0)])
    norm_gain_grad = gain_part / norm_gain.astype(f32)
    in_x_grad, in_z_grad = lead(in_x_grad), lead(in_z_grad)
    return (
        block_out,
        tokens_grad,
        norm_gain_grad,
        in_x_grad,
        in_z_grad,
        xdt_grad,
        xbc_grad,
        dt_weight_grad,
        dt_bias_grad,
        conv_weight_grad,
        conv_bias_grad,
        log_rates_grad,
        skip_gain_grad,
        out_weight_grad,
    )


def solution(mesh):
    rows, seq = mesh.shape["row"], mesh.shape["seq"]
    across = 2 if rows % 2 == 0 else 1
    cores = 2 if seq % 2 == 0 else 1
    along = next(n for n in (4, 3, 2, 1) if (seq // cores) % n == 0)
    fine = Mesh(
        mesh.devices.reshape(rows // across, across, seq // (along * cores), along, cores), ("y", "x", "o", "z", "c")
    )
    row, seq, both = row_axes, seq_axes, row_axes + seq_axes
    in_specs = (
        P(row, seq, None),
        P(row, seq, None),
        P(None, seq),
        P(None, seq),
        P(),
        P(seq),
        P(seq, None, row),
        P(seq, None, row),
        P(both, None, None),
        P(None, None, both),
        P(None, None, both),
        P(None, both),
        P(None, both),
        P(both),
        P(None, both),
        P(both),
        P(seq, None, row),
    )
    out_specs = (
        P(row, seq, None),
        P(row, seq, None),
        P(seq),
        P(seq, None, row),
        P(seq, None, row),
        P(both, None, None),
        P(None, None, both),
        P(None, None, both),
        P(None, both),
        P(None, both),
        P(both),
        P(None, both),
        P(both),
        P(seq, None, row),
    )
    return jax.shard_map(on_device, mesh=fine, in_specs=in_specs, out_specs=out_specs, check_vma=False)
```

```python
import functools
import math

import jax
import jax.numpy as jnp
from jax import lax
from jax.experimental import pallas as pl
from jax.experimental.pallas import tpu as pltpu
from jax.sharding import Mesh
from jax.sharding import PartitionSpec as P

epsilon = 1e-05
row_axes = ("y", "x")
group_axes = ("z", "c")
seq_axes = ("o", "z", "c")
team_axes = ("y", "x", "z", "c")
bf16 = jnp.bfloat16
f32 = jnp.float32
lanes = 128
huge_step = 1e6
vmem_bytes = 48 * 1024 * 1024


def apply_silu(values):
    return values * jax.nn.sigmoid(values)


def silu_slope(values):
    sigmoid_of = jax.nn.sigmoid(values)
    return sigmoid_of * (1.0 + values * (1.0 - sigmoid_of))


def softplus(values):
    tail = jnp.exp(-jnp.abs(values))
    series = tail * (1.0 + tail * (-1 / 2 + tail * (1 / 3 + tail * (-1 / 4 + tail * (1 / 5 - tail * (1 / 6))))))
    return jnp.maximum(values, 0.0) + jnp.where(tail < 0.05, series, jnp.log(1.0 + tail))


def dot(a, b, contract):
    return lax.dot_general(a, b, (contract, ((), ())), preferred_element_type=f32)


def chosen(values, label, mods, axis=1):
    wide = values.shape[axis] // mods
    parts = [lax.slice_in_dim(values, m * wide, (m + 1) * wide, axis=axis) for m in range(mods)]
    picked = parts[0]
    for m in range(1, mods):
        picked = jnp.where(label == m, parts[m], picked)
    return picked


def placed(values, label, mods, axis=1):
    wide = values.astype(f32)
    return jnp.concatenate([jnp.where(label == m, wide, 0.0) for m in range(mods)], axis=axis).astype(values.dtype)


start_column, label_column, fact_columns = 3, 4, 8


def columns_of(facts):
    missing = facts.shape[1] - facts.shape[0]
    return jnp.transpose(jnp.concatenate([facts, jnp.zeros((missing, facts.shape[1]), f32)], axis=0))


def label_column_of(facts_ref):
    return jnp.concatenate(
        [columns_of(facts_ref[j])[:, label_column : label_column + 1] for j in range(facts_ref.shape[0])], axis=0
    )


params = functools.partial(pltpu.CompilerParams, vmem_limit_bytes=vmem_bytes)


def everything(array):
    return pl.BlockSpec(array.shape, lambda i, rank=len(array.shape): (0,) * rank)


def scalars():
    return pl.BlockSpec(memory_space=pltpu.SMEM)


def shape(dims, dtype):
    return jax.ShapeDtypeStruct(dims, dtype)


def cost(flops, nbytes):
    return pl.CostEstimate(flops=int(flops), bytes_accessed=int(nbytes), transcendentals=0)


def assemble(weight_ref, whole):
    pieces, mods, some, wide = weight_ref.shape
    for i in range(pieces):
        for m in range(mods):
            whole[i * some : (i + 1) * some, m * wide : (m + 1) * wide] = weight_ref[i, m]


def lead_kernel(mods, places, x_ref, facts_ref, weight_ref, out_ref, whole):
    @pl.when(pl.program_id(0) == 0)
    def _():
        assemble(weight_ref, whole)

    some, here, wide = x_ref.shape
    label = label_column_of(facts_ref)
    picked = chosen(dot(x_ref[...].reshape(some * here, wide), whole[...], ((1,), (0,))), label, mods)
    for j in range(some):
        out_ref[places[pl.program_id(0) * some + j]] = picked[j * here : (j + 1) * here].astype(out_ref.dtype)


def lead_product(places, x, facts, weight, dtype):
    pieces, here, wide = x.shape
    groups, mods, some, mine = weight.shape
    outs = [shape((pieces, here, mine), dtype), shape((groups * some, mods * mine), bf16)]
    return pl.pallas_call(
        functools.partial(lead_kernel, mods),
        grid=(pieces // 4,),
        in_specs=[
            scalars(),
            pl.BlockSpec((4, here, wide), lambda i: (i, 0, 0)),
            pl.BlockSpec((4, fact_columns, here), lambda i: (i, 0, 0)),
            everything(weight),
        ],
        out_specs=[everything(out) for out in outs],
        out_shape=outs,
        compiler_params=params(),
        cost_estimate=cost(2 * pieces * here * wide * mods * mine, 2 * pieces * here * wide),
        name="lead_product",
    )(places, x, facts, weight)


def lead_pieces_kernel(mods, count, places, facts_ref, weight_ref, *refs):
    pieces = refs[:count]
    out_ref, whole, all_ref, buffer, in_sems, out_sems = refs[count:]
    _, some, here, wide = buffer.shape
    assemble(weight_ref, whole)

    def fetch(i):
        return [
            pltpu.make_async_copy(pieces[i * some + j], buffer.at[i % 2, j], in_sems.at[i % 2, j]) for j in range(some)
        ]

    def store(i):
        return pltpu.make_async_copy(buffer.at[i % 2], all_ref.at[pl.ds(i * some, some)], out_sems.at[i % 2])

    steps = count // some
    for copy in fetch(0):
        copy.start()
    for i in range(steps):
        if i + 1 < steps:
            if i:
                store(i - 1).wait()
            for copy in fetch(i + 1):
                copy.start()
        for copy in fetch(i):
            copy.wait()
        store(i).start()
        label = label_column_of(facts_ref.at[i * some : (i + 1) * some])
        picked = chosen(dot(buffer[i % 2].reshape(some * here, wide), whole[...], ((1,), (0,))), label, mods)
        for j in range(some):
            out_ref[places[i * some + j]] = picked[j * here : (j + 1) * here].astype(out_ref.dtype)
    for i in range(max(steps - 2, 0), steps):
        store(i).wait()


def lead_pieces(places, pieces, facts, weight, dtype):
    here, wide = pieces[0].shape
    count, some = len(pieces), 4
    groups, mods, features, mine = weight.shape
    outs = [
        shape((count, here, mine), dtype),
        shape((groups * features, mods * mine), bf16),
        shape((count, here, wide), bf16),
    ]
    vmem, there = pl.BlockSpec(memory_space=pltpu.VMEM), pl.BlockSpec(memory_space=pl.ANY)
    return pl.pallas_call(
        functools.partial(lead_pieces_kernel, mods, count),
        in_specs=[scalars(), vmem, vmem] + [there] * count,
        out_specs=[vmem, vmem, there],
        out_shape=outs,
        scratch_shapes=[
            pltpu.VMEM((2, some, here, wide), bf16),
            pltpu.SemaphoreType.DMA((2, some)),
            pltpu.SemaphoreType.DMA((2,)),
        ],
        compiler_params=params(),
        cost_estimate=cost(2 * count * here * wide * mods * mine, 4 * count * here * wide),
        name="lead_pieces",
    )(places, facts, weight, *pieces)


def trail_kernel(mods, count, skipped, *refs):
    lefts, facts_ref, weights = refs[:count], refs[count], refs[count + 1 : 2 * count + 1]
    outs = refs[2 * count + 1 + skipped :]
    some, here, mine = lefts[0].shape
    label = label_column_of(facts_ref)
    total = None
    for left, weight in zip(lefts, weights):
        term = dot(placed(left[...].reshape(some * here, mine), label, mods), weight[...], ((1,), (1,)))
        total = term if total is None else total + term
    total = total.astype(bf16).reshape(some, here, -1)
    if len(outs) == 1:
        outs[0][...] = total
    else:
        is_far = pl.program_id(0) < pl.num_programs(0) // 2

        @pl.when(is_far)
        def _():
            outs[0][...] = total

        @pl.when(jnp.logical_not(is_far))
        def _():
            outs[1][...] = total


def trail_product(lefts, facts, weights, mods, ks=None, beside=()):
    pieces, here, mine = lefts[0].shape
    features = weights[0].shape[0]
    if ks is None:
        steps, outs = pieces // 4, [shape((pieces, here, features), bf16)]
        out_specs = [pl.BlockSpec((4, here, features), lambda i: (i, 0, 0))]

        def block(i):
            return (i, 0, 0)
    else:
        steps, outs = 4, [shape((8, here, features), bf16)] * 2
        out_specs = [
            pl.BlockSpec((4, here, features), lambda i: (jnp.minimum(i, 1), 0, 0)),
            pl.BlockSpec((4, here, features), lambda i: (jnp.maximum(i - 2, 0), 0, 0)),
        ]

        def block(i):
            return (2 * jnp.where(i % 2 == 0, ks[0], ks[1]) + jnp.where(i < 2, 1, 0), 0, 0)

    return pl.pallas_call(
        functools.partial(trail_kernel, mods, len(lefts), len(beside)),
        grid=(steps,),
        in_specs=[pl.BlockSpec((4, here, mine), block) for _ in lefts]
        + [pl.BlockSpec((4, fact_columns, here), block)]
        + [everything(weight) for weight in weights]
        + [pl.BlockSpec(memory_space=pl.ANY) for _ in beside],
        out_specs=out_specs,
        out_shape=outs,
        compiler_params=params(),
        cost_estimate=cost(
            8 * steps * here * features * mods * mine * len(lefts), 8 * steps * here * features
        ),
        name="trail_product",
    )(*lefts, facts, *weights, *beside)


def grad_kernel(mods, x_ref, d_ref, facts_ref, *refs):
    out_ref, spread = refs[-2:]
    pieces, here, mine = d_ref.shape

    @pl.when(pl.program_id(0) == 0)
    def _():
        for i in range(pieces):
            label = columns_of(facts_ref[i])[:, label_column : label_column + 1]
            spread[i * here : (i + 1) * here] = placed(d_ref[i], label, mods)

    out_ref[0] = dot(x_ref[...], spread[...], ((0,), (0,))).astype(out_ref.dtype)


def feature_grad(x, d, facts, mods, groups, dtype, beside=()):
    pieces, here, wide = x.shape
    mine = d.shape[2]
    some = min(256, wide)
    out = shape((wide // some, some, mods * mine), dtype)
    grad = pl.pallas_call(
        functools.partial(grad_kernel, mods),
        grid=(wide // some,),
        in_specs=[
            pl.BlockSpec((pieces * here, some), lambda i: (0, i)),
            everything(d),
            everything(facts),
        ]
        + [pl.BlockSpec(memory_space=pl.ANY) for _ in beside],
        out_specs=pl.BlockSpec((1, some, mods * mine), lambda i: (i, 0, 0)),
        out_shape=out,
        scratch_shapes=[pltpu.VMEM((pieces * here, mods * mine), bf16)],
        compiler_params=params(),
        cost_estimate=cost(6 * pieces * here * wide * mods * mine, 2 * pieces * here * wide),
        name="feature_grad",
    )(x.reshape(pieces * here, wide), d, facts, *beside)
    return grad.reshape(groups, wide // groups, mods * mine)


def settle_kernel(got_ref, weight_ref, out_ref, sum_ref):
    mods, _, mine = out_ref.shape

    @pl.when(pl.program_id(0) == 0)
    def _():
        sum_ref[...] = jnp.zeros_like(sum_ref)

    for m in range(mods):
        grad = got_ref[0, :, m * mine : (m + 1) * mine].astype(f32)
        out_ref[m] = grad
        sum_ref[...] += grad * weight_ref[m].astype(f32)


def settle(got, weight):
    sources, some, columns = got.shape
    mods, _, wide = weight.shape
    mine = wide // sources
    item = pl.BlockSpec((mods, some, mine), lambda i: (0, 0, i))
    outs = [shape(weight.shape, f32), shape((some, mine), f32)]
    return pl.pallas_call(
        settle_kernel,
        grid=(sources,),
        in_specs=[pl.BlockSpec((1, some, columns), lambda i: (i, 0, 0)), item],
        out_specs=[item, everything(outs[1])],
        out_shape=outs,
        compiler_params=params(),
        cost_estimate=cost(0, 8 * mods * some * wide),
        name="settle",
    )(got, weight)


def conv_kernel(mods, conv_ref, before_ref, facts_ref, row_label_ref, taps_ref, bias_ref, xdt_ref, xbc_ref, pre_ref, proj_ref, carried, line):
    rows, here, mine = conv_ref.shape

    @pl.when(pl.program_id(0) == 0)
    def _():
        carried[...] = before_ref[...]

    for r in range(rows):
        block = conv_ref[r].astype(f32)
        line[:8] = carried[r]
        line[8:] = block
        facts = columns_of(facts_ref[r, 0])
        pre = bias_ref[...] + taps_ref[0:1] * block
        for lag in range(1, taps_ref.shape[0]):
            pre = pre + taps_ref[lag : lag + 1] * (facts[:, lag - 1 : lag] * line[8 - lag : 8 - lag + here])
        carried[r] = block[here - 8 :]
        pre_ref[r] = pre
        low = apply_silu(pre).astype(bf16)
        wide = chosen(dot(low, xdt_ref[...], ((1,), (0,))), facts[:, label_column : label_column + 1], mods)
        small = chosen(dot(xbc_ref[...], low, ((1,), (1,))), row_label_ref[0, r : r + 1], mods, 0)
        proj_ref[r, 0, :here] = wide.astype(bf16)
        proj_ref[r, 0, here:] = small.astype(bf16)


def conv_block(conv_in, before, facts, row_label, taps, bias, xdt, xbc):
    rows, length, mine = conv_in.shape
    blocks, _, here = row_label.shape
    mods = xdt.shape[1] // here
    narrow = xbc.shape[0] // mods
    item = pl.BlockSpec((rows, here, mine), lambda i: (0, i, 0))
    return pl.pallas_call(
        functools.partial(conv_kernel, mods),
        grid=(blocks,),
        in_specs=[
            item,
            everything(before),
            pl.BlockSpec((rows, 1, fact_columns, here), lambda i: (0, i, 0, 0)),
            pl.BlockSpec((1, rows, here), lambda i: (i, 0, 0)),
        ]
        + [everything(array) for array in (taps, bias, xdt, xbc)],
        out_specs=[item, pl.BlockSpec((rows, 1, here + narrow, here), lambda i: (0, i, 0, 0))],
        out_shape=[shape(conv_in.shape, f32), shape((rows, blocks, here + narrow, here), bf16)],
        scratch_shapes=[pltpu.VMEM((rows, 8, mine), f32), pltpu.VMEM((8 + here, mine), f32)],
        compiler_params=params(),
        cost_estimate=cost(20000 * rows * length * mine, 10 * rows * length * mine),
        name="conv_block",
    )(conv_in, before, facts, row_label, taps, bias, xdt, xbc)


def coefficient_lines(proj_ref, rows, here, line):
    narrow = proj_ref.shape[2] - here
    for r in range(rows):
        small = proj_ref[r, 0, here:].astype(f32)
        small = jnp.concatenate([small, jnp.zeros((here - narrow, here), f32)], axis=0)
        turned = jnp.transpose(small)
        line[r * here : (r + 1) * here] = turned
        line[(rows + r) * here : (rows + r + 1) * here] = pltpu.roll(turned, here - narrow // 2, 1)


def coefficient_tiles(proj_ref, rows, here, expand_ref, turned, tiles):
    narrow = proj_ref.shape[2] - here
    for r in range(rows):
        small = proj_ref[r, 0, here:].astype(f32)
        small = jnp.transpose(jnp.concatenate([small, jnp.zeros((here - narrow, here), f32)], axis=0))
        turned[pl.ds(r, here, stride=2 * rows), :] = small
        turned[pl.ds(rows + r, here, stride=2 * rows), :] = pltpu.roll(small, here - narrow // 2, 1)
    some = 256
    for i in range(turned.shape[0] // some):
        part = slice(i * some, (i + 1) * some)
        tiles[part] = dot(turned[part].astype(bf16), expand_ref[...], ((1,), (0,)))


def scan_lines(r, rows, here, value, line):
    line[r * here : (r + 1) * here] = value
    line[(rows + r) * here : (rows + r + 1) * here] = value


def forward_kernel(
    mods, proj_ref, pre_ref, facts_ref, gate_ref, dtw_ref, dtb_ref, rate_ref, skip_ref, start_ref, expand_ref,
    gated_ref, scanned_ref, dt_ref, kept_ref, end_ref, held, step_line, drive_line, turned, tiles, out_line,
):
    rows, here, mine = pre_ref.shape
    pieces, subl, _ = rate_ref.shape

    @pl.when(pl.program_id(0) == 0)
    def _():
        held[...] = start_ref[...]

    coefficient_tiles(proj_ref, rows, here, expand_ref, turned, tiles)
    for r in range(rows):
        facts = columns_of(facts_ref[r, 0])
        label = facts[:, label_column : label_column + 1]
        dt_pre = chosen(dot(proj_ref[r, 0, :here], dtw_ref[...], ((1,), (0,))) + dtb_ref[...], label, mods)
        dt_ref[r] = dt_pre
        step = softplus(dt_pre)
        scan_lines(r, rows, here, step * apply_silu(pre_ref[r]), drive_line)
        scan_lines(r, rows, here, jnp.where(facts[:, start_column : start_column + 1] > 0, huge_step, step), step_line)

    def one(t, state):
        lines = pl.ds(t, subl, stride=here)
        step, drive = step_line[lines, :], drive_line[lines, :]
        spot = pl.ds(pl.multiple_of(t * subl, subl), subl)
        emitted = None
        following = []
        for j in range(pieces):
            kept_ref[t, j] = state[j]
            decay = jnp.exp2(step * rate_ref[j])
            now = decay * state[j] + drive * tiles[spot, j * mine : (j + 1) * mine]
            term = now * tiles[spot, (pieces + j) * mine : (pieces + j + 1) * mine]
            emitted = term if emitted is None else emitted + term
            following.append(now)
        out_line[lines, :] = emitted
        return tuple(following)

    def eight(block, state):
        for i in range(8):
            state = one(block * 8 + i, state)
        return state

    state = lax.fori_loop(0, here // 8, eight, tuple(held[j] for j in range(pieces)))
    for j in range(pieces):
        held[j] = state[j]
        end_ref[j] = state[j]
    for r in range(rows):
        emitted = out_line[r * here : (r + 1) * here] + out_line[(rows + r) * here : (rows + r + 1) * here]
        scanned = emitted + skip_ref[...] * apply_silu(pre_ref[r])
        scanned_ref[r] = scanned
        gated_ref[r] = (scanned * apply_silu(gate_ref[r])).astype(bf16)


def scan_forward(proj, pre, facts, gate, dtw, dtb, rates2, skip, start):
    rows, length, mine = pre.shape
    _, blocks, deep, here = proj.shape
    pieces, subl, _ = rates2.shape
    item = pl.BlockSpec((rows, here, mine), lambda i: (0, i, 0))
    line = pltpu.VMEM((subl * here, mine), f32)
    expand = (jnp.arange(here)[:, None] == jnp.arange(2 * pieces * mine)[None, :] // mine).astype(bf16)
    return pl.pallas_call(
        functools.partial(forward_kernel, dtw.shape[1] // mine),
        grid=(blocks,),
        in_specs=[
            pl.BlockSpec((rows, 1, deep, here), lambda i: (0, i, 0, 0)),
            item,
            pl.BlockSpec((rows, 1, fact_columns, here), lambda i: (0, i, 0, 0)),
            item,
        ]
        + [everything(array) for array in (dtw, dtb, rates2, skip, start, expand)],
        out_specs=[
            item,
            item,
            item,
            pl.BlockSpec((here, pieces, subl, mine), lambda i: (i, 0, 0, 0)),
            everything(start),
        ],
        out_shape=[
            shape(pre.shape, bf16),
            shape(pre.shape, f32),
            shape(pre.shape, f32),
            shape((length, pieces, subl, mine), f32),
            shape(start.shape, f32),
        ],
        scratch_shapes=[pltpu.VMEM(start.shape, f32), line, line, line]
        + [pltpu.VMEM((subl * here, 2 * pieces * mine), f32), line],
        compiler_params=params(),
        cost_estimate=cost(5500 * length * pieces * subl * mine, 5 * length * pieces * subl * mine),
        name="scan_forward",
    )(proj, pre, facts, gate, dtw, dtb, rates2, skip, start, expand)


def backward_kernel(
    mods, tables, proj_ref, pre_ref, facts_ref, gate_ref, scanned_ref, dt_ref, d_gated_ref, kept_ref, dtw_ref, rate2_ref,
    rate_ref, skip_ref, last_ref, carry_ref, sum_ref, expand_ref, _, d_gate_ref, d_proj_ref, d_act_ref, dtw_grad_ref, dtb_grad_ref,
    skip_grad_ref, rate_sum_ref, carry_out_ref, carried, later, products, step_line, drive_line, turned, tiles, back_line,
    pulled_line, weighted_line, small_line,
):
    rows, here, mine = pre_ref.shape
    blocks = tables.shape[0] // rows
    narrow = proj_ref.shape[2] - here
    pieces, subl, _ = rate_ref.shape
    place = blocks - 1 - pl.program_id(0)

    @pl.when(pl.program_id(0) == 0)
    def _():
        carried[...] = carry_ref[...]
        later[...] = last_ref[...]
        for ref in (rate_sum_ref, dtw_grad_ref, dtb_grad_ref, skip_grad_ref):
            ref[...] = jnp.zeros_like(ref)

    coefficient_tiles(proj_ref, rows, here, expand_ref, turned, tiles)
    for r in range(rows):
        facts = columns_of(facts_ref[r, 0])
        step, activated = softplus(dt_ref[r]), apply_silu(pre_ref[r])
        gate, d_gated = gate_ref[r], d_gated_ref[r]
        d_scan = d_gated * apply_silu(gate)
        d_gate_ref[tables[r * blocks + place]] = (d_gated * scanned_ref[r] * silu_slope(gate)).astype(bf16)
        skip_grad_ref[...] += jnp.sum(d_scan * activated, axis=0, keepdims=True)
        scan_lines(r, rows, here, d_scan, back_line)
        scan_lines(r, rows, here, step * activated, drive_line)
        scan_lines(r, rows, here, jnp.where(facts[:, start_column : start_column + 1] > 0, huge_step, step), step_line)

    def one(t, carry, state):
        lines = pl.ds(t, subl, stride=here)
        step, drive, back = step_line[lines, :], drive_line[lines, :], back_line[lines, :]
        row = pl.ds(pl.multiple_of(t * subl, subl), subl)
        pulled_sum, weighted_sum = None, None
        new_carry, new_state, terms, sums = [], [], [], []
        for j in range(pieces):
            before = kept_ref[t, j]
            decay = jnp.exp2(step * rate2_ref[j])
            adjoint = back * tiles[row, (pieces + j) * mine : (pieces + j + 1) * mine] + carry[j]
            passed = decay * adjoint
            pulled = passed * before
            weighted = adjoint * tiles[row, j * mine : (j + 1) * mine]
            first = pulled * rate_ref[j]
            pulled_sum = first if pulled_sum is None else pulled_sum + first
            weighted_sum = weighted if weighted_sum is None else weighted_sum + weighted
            terms.append((adjoint * drive, back * state[j]))
            sums.append(pulled * step)
            new_carry.append(passed)
            new_state.append(before)
        pulled_line[lines, :] = pulled_sum
        weighted_line[lines, :] = weighted_sum
        return new_carry, new_state, terms, sums

    def eight(k, loop):
        carry, state, rates = loop
        block = here // 8 - 1 - k
        rates = list(rates)
        for i in (6, 4, 2, 0):
            t = block * 8 + i
            carry, state, terms_b, sums_b = one(t + 1, carry, state)
            carry, state, terms_a, sums_a = one(t, carry, state)
            spot = pl.ds(pl.multiple_of(t * subl, 16), 16)
            for j in range(pieces):
                rates[j] = rates[j] + (sums_a[j] + sums_b[j])
                for part in range(2):
                    column = (part * pieces + j) * mine
                    products[spot, column : column + mine] = jnp.concatenate(
                        [terms_a[j][part], terms_b[j][part]], axis=0
                    ).astype(bf16)
        return tuple(carry), tuple(state), tuple(rates)

    begin = tuple(tuple(ref[j] for j in range(pieces)) for ref in (carried, later, rate_sum_ref))
    carry, state, rates = lax.fori_loop(0, here // 8, eight, begin)
    for j in range(pieces):
        carried[j] = carry[j]
        later[j] = state[j]
        rate_sum_ref[j] = rates[j]
        carry_out_ref[j] = carry[j]
    small_line[...] = dot(products[...], sum_ref[...], ((1,), (0,)))
    for r in range(rows):
        label = columns_of(facts_ref[r, 0])[:, label_column : label_column + 1]
        dt_pre, activated = dt_ref[r], apply_silu(pre_ref[r])
        near, far = slice(r * here, (r + 1) * here), slice((rows + r) * here, (rows + r + 1) * here)
        weighted = weighted_line[near] + weighted_line[far]
        d_step = pulled_line[near] + pulled_line[far] + activated * weighted
        d_act_ref[r] = back_line[near] * skip_ref[...] + softplus(dt_pre) * weighted
        d_dt = placed((d_step * jax.nn.sigmoid(dt_pre)).astype(bf16), label, mods)
        dtw_grad_ref[...] += dot(proj_ref[r, 0, :here], d_dt, ((0,), (0,)))
        dtb_grad_ref[...] += jnp.sum(d_dt.astype(f32), axis=0, keepdims=True)
        d_proj_ref[r, 0, :here] = dot(d_dt, dtw_ref[...], ((1,), (1,))).astype(bf16)
        one_half = small_line[pl.ds(r, here, stride=subl), :]
        other_half = small_line[pl.ds(rows + r, here, stride=subl), :]
        small = jnp.transpose(one_half + pltpu.roll(other_half, narrow // 2, 1))
        d_proj_ref[r, 0, here:] = small[:narrow].astype(bf16)


def scan_backward(
    tables, proj, pre, facts, gate, scanned, dt_pre, d_gated, kept, dtw, rates2, rates, skip, last, carry, beside
):
    rows, length, mine = pre.shape
    _, blocks, deep, here = proj.shape
    pieces, subl, _ = rates2.shape
    item = pl.BlockSpec((rows, here, mine), lambda i: (0, blocks - 1 - i, 0))
    proj_item = pl.BlockSpec((rows, 1, deep, here), lambda i: (0, blocks - 1 - i, 0, 0))
    columns = 2 * pieces * mine
    expand = (jnp.arange(here)[:, None] == jnp.arange(columns)[None, :] // mine).astype(bf16)
    summing = (jnp.arange(columns)[:, None] // mine == jnp.arange(lanes)[None, :]).astype(bf16)
    d_gate = shape((rows * blocks, here, mine), bf16)
    line = pltpu.VMEM((subl * here, mine), f32)
    small = [shape((here, dtw.shape[1]), f32), shape((1, dtw.shape[1]), f32), shape((1, mine), f32), shape(carry.shape, f32)]
    return pl.pallas_call(
        functools.partial(backward_kernel, dtw.shape[1] // mine),
        grid=(blocks,),
        in_specs=[
            scalars(),
            proj_item,
            item,
            pl.BlockSpec((rows, 1, fact_columns, here), lambda i: (0, blocks - 1 - i, 0, 0)),
            item,
            item,
            item,
            item,
            pl.BlockSpec((here, pieces, subl, mine), lambda i: (blocks - 1 - i, 0, 0, 0)),
        ]
        + [everything(array) for array in (dtw, rates2, rates, skip, last, carry, summing, expand)]
        + [pl.BlockSpec(memory_space=pl.ANY)],
        out_specs=[everything(d_gate), proj_item, item] + [everything(array) for array in small + [carry]],
        out_shape=[d_gate, shape(proj.shape, bf16), shape(pre.shape, f32)] + small + [shape(carry.shape, f32)],
        scratch_shapes=[pltpu.VMEM(carry.shape, f32)] * 2 + [pltpu.VMEM((subl * here, columns), bf16)] + [line] * 3
        + [pltpu.VMEM((subl * here, columns), f32)] + [line] * 4,
        compiler_params=params(),
        cost_estimate=cost(7500 * length * pieces * subl * mine, 5 * length * pieces * subl * mine),
        name="scan_backward",
    )(tables, proj, pre, facts, gate, scanned, dt_pre, d_gated, kept, dtw, rates2, rates, skip, last, carry, summing, expand, beside)


def deconv_kernel(
    mods, tables, d_proj_ref, conv_ref, pre_ref, d_act_ref, facts_ref, row_label_ref, taps_ref, xdt_ref, xbc_ref,
    d_conv_ref, xdt_grad_ref, xbc_grad_ref, taps_grad_ref, bias_grad_ref, head_ref, tail_ref, carried, line,
):
    rows, here, mine = pre_ref.shape
    blocks = tables.shape[0] // rows
    taps = taps_ref.shape[0]
    place = blocks - 1 - pl.program_id(0)

    @pl.when(pl.program_id(0) == 0)
    def _():
        carried[...] = jnp.zeros_like(carried)
        for ref in (xdt_grad_ref, xbc_grad_ref, taps_grad_ref, bias_grad_ref):
            ref[...] = jnp.zeros_like(ref)

    for r in range(rows):
        facts = columns_of(facts_ref[r, 0])
        pre = pre_ref[r]
        low = apply_silu(pre).astype(bf16)
        d_rank = placed(d_proj_ref[r, 0, :here], facts[:, label_column : label_column + 1], mods)
        d_small = placed(d_proj_ref[r, 0, here:], row_label_ref[0, r : r + 1], mods, 0)
        xdt_grad_ref[...] += dot(low, d_rank, ((0,), (0,)))
        xbc_grad_ref[...] += dot(d_small, low, ((1,), (0,)))
        d_act = d_act_ref[r] + dot(d_rank, xdt_ref[...], ((1,), (1,))) + dot(d_small, xbc_ref[...], ((0,), (0,)))
        d_pre = d_act * silu_slope(pre)
        source = conv_ref[r].astype(f32)
        total = taps_ref[0:1] * d_pre
        bias_grad_ref[...] += jnp.sum(d_pre, axis=0, keepdims=True)
        taps_grad_ref[0:1] += jnp.sum(source * d_pre, axis=0, keepdims=True)
        for lag in range(1, taps):
            kept = facts[:, lag - 1 : lag] * d_pre
            line[:here] = kept
            line[here:] = carried[r, lag - 1]
            carried[r, lag - 1] = kept[:8]
            moved = line[lag : lag + here]
            total = total + taps_ref[lag : lag + 1] * moved
            taps_grad_ref[lag : lag + 1] += jnp.sum(source * moved, axis=0, keepdims=True)
        d_conv_ref[tables[r * blocks + place]] = total.astype(bf16)

        @pl.when(pl.program_id(0) == 0)
        def _():
            tail_ref[r] = total[here - 8 :]

    head_ref[...] = carried[...]


def deconv_block(tables, d_proj, conv_in, pre, d_act, facts, row_label, taps, xdt, xbc):
    rows, length, mine = pre.shape
    _, blocks, deep, here = d_proj.shape
    item = pl.BlockSpec((rows, here, mine), lambda i: (0, blocks - 1 - i, 0))
    outs = [
        shape((rows * blocks, here, mine), bf16),
        shape(xdt.shape, f32),
        shape(xbc.shape, f32),
        shape(taps.shape, f32),
        shape((1, mine), f32),
        shape((rows, taps.shape[0] - 1, 8, mine), f32),
        shape((rows, 8, mine), f32),
    ]
    return pl.pallas_call(
        functools.partial(deconv_kernel, xdt.shape[1] // here),
        grid=(blocks,),
        in_specs=[
            scalars(),
            pl.BlockSpec((rows, 1, deep, here), lambda i: (0, blocks - 1 - i, 0, 0)),
            item,
            item,
            item,
            pl.BlockSpec((rows, 1, fact_columns, here), lambda i: (0, blocks - 1 - i, 0, 0)),
            pl.BlockSpec((1, rows, here), lambda i: (blocks - 1 - i, 0, 0)),
        ]
        + [everything(array) for array in (taps, xdt, xbc)],
        out_specs=[everything(array) for array in outs],
        out_shape=outs,
        scratch_shapes=[pltpu.VMEM(outs[5].shape, f32), pltpu.VMEM((here + 8, mine), f32)],
        compiler_params=params(),
        cost_estimate=cost(30000 * rows * length * mine, 14 * rows * length * mine),
        name="deconv_block",
    )(tables, d_proj, conv_in, pre, d_act, facts, row_label, taps, xdt, xbc)


def passed_along(value, axis, by):
    size = lax.axis_size(axis)
    return lax.ppermute(value, axis, [(i, i + by) for i in range(size) if 0 <= i + by < size])


def shifted(value, by):
    size = lax.axis_size("z")
    return value if by % size == 0 else lax.ppermute(value, "z", [(i, (i + by) % size) for i in range(size)])


def swapped(value):
    return lax.ppermute(value, "c", [(0, 1), (1, 0)])


def hop(value, second):
    depth = lax.axis_size("z")

    def place(y, x, z, c):
        return ((y * 2 + x) * depth + z) * 2 + c

    pairs = [
        (place(y, x, z, c), place(y, 1 - x, z, c) if (c == 1) == second else place(1 - y, x, z, c))
        for y in range(2)
        for x in range(2)
        for z in range(depth)
        for c in range(2)
    ]
    return lax.ppermute(value, team_axes, pairs)


def relative_places():
    depth = lax.axis_size("z")
    y, x, z, c = (lax.axis_index(name) for name in team_axes)
    n = jnp.arange(4)[None, None, :]
    core = (c + jnp.arange(2)[None, :, None]) % 2
    back = (z - jnp.arange(depth)[:, None, None]) % depth
    one, two = n % 2, n // 2
    flip_x = jnp.where(core == 0, one, two)
    flip_y = jnp.where(core == 0, two, one)
    return (((((y + flip_y) % 2) * 2 + (x + flip_x) % 2) * depth + back) * 2 + core).reshape(-1)


def nothing(*refs):
    pass


def tied(value, *others):
    there = pl.BlockSpec(memory_space=pl.ANY)
    return pl.pallas_call(
        nothing,
        in_specs=[there] * (1 + len(others)),
        out_specs=there,
        out_shape=shape(value.shape, value.dtype),
        input_output_aliases={0: 0},
        name="tied",
    )(value, *others)


def team_gather(value, weight):
    near, first, second, third = {0: value}, {}, {}, {}

    def hops(k):
        first[k], second[k] = hop(near[k], False), hop(near[k], True)

    near[1], near[3] = shifted(value, 1), shifted(value, 3)
    weight = exchanged(tied(weight, near[1]))
    hops(0)
    near[2] = shifted(tied(value, first[0], second[0]), 2)
    third[0] = hop(first[0], True)
    near[1] = tied(near[1], first[0], second[0])
    hops(1)
    third[1] = hop(first[1], True)
    near[3] = tied(near[3], third[0], first[1], second[1])
    hops(3)
    third[3] = hop(first[3], True)
    near[2] = tied(near[2], third[1], first[3], second[3], weight)
    hops(2)
    third[2] = hop(first[2], True)
    parts = []
    for k in range(4):
        pieces = [near[k], first[k], second[k], third[k]]
        parts += pieces + [swapped(piece) for piece in pieces]
    return parts, [third[2], second[2], third[3]], weight


def team_scatter(made, beside):
    def added(*terms):
        return sum(term.astype(f32) for term in terms)

    groups = [(1, 2), (3, 0)]
    far, near = {}, {}
    for i, ks in enumerate(groups):
        away, here = made(ks, [beside[i]])
        far[i] = swapped(away).reshape((len(ks), 4) + away.shape[1:])
        near[i] = here.reshape((len(ks), 4) + here.shape[1:])
    total = None
    for i, ks in enumerate(groups):
        payload = added(near[i][:, 2:], far[i][:, 2:]).astype(bf16)
        come = hop(payload, True)
        last = hop(added(near[i][:, 1], far[i][:, 1], come[:, 1]).astype(bf16), False)
        held = added(near[i][:, 0], far[i][:, 0], come[:, 0], last)
        for j, k in enumerate(ks):
            own = shifted(held[j].astype(bf16), -k).astype(f32) if k else held[j]
            total = own if total is None else total + own
    return total


def exchanged(parts):
    return lax.all_to_all(parts, group_axes, 0, 0, tiled=True)


def spread_weight(weight):
    outer, group = lax.axis_size("o"), lax.axis_size(group_axes)
    mods, here, wide = weight.shape
    each = wide // (outer * group)
    parts = weight.reshape(mods, here, outer, group, each)
    parts = jnp.transpose(parts, (3, 0, 1, 2, 4)).reshape(group, mods, here, outer * each)
    return parts


def through_outer(got):
    return got if lax.axis_size("o") == 1 else lax.all_gather(got, "o", axis=0, tiled=True)


def spread_done(parts):
    return through_outer(exchanged(parts))


def collect(parts):
    if lax.axis_size("o") > 1:
        parts = lax.psum_scatter(parts, "o", scatter_dimension=0, tiled=True)
    return exchanged(parts.astype(bf16))


def settled(got, weight):
    outer, group = lax.axis_size("o"), lax.axis_size(group_axes)
    mods, here, wide = weight.shape
    if outer == 1:
        grad, sums = settle(got, weight)
        return grad, jnp.sum(sums, axis=1)
    got = got.astype(f32).reshape(group, here, mods, outer, wide // (outer * group))
    grad = jnp.transpose(got, (2, 1, 3, 0, 4)).reshape(weight.shape)
    return grad, jnp.sum(grad * weight.astype(f32), axis=(0, 2))


def outer_gathered(value, axis):
    return value if lax.axis_size("o") == 1 else lax.all_gather(value, "o", axis=axis, tiled=True)


def outer_summed(value, axis):
    if lax.axis_size("o") == 1:
        return value
    return lax.psum_scatter(value, "o", scatter_dimension=axis, tiled=True)


def half_of(value, axis, name, other):
    return lax.dynamic_index_in_dim(value, (lax.axis_index(name) + other) % 2, axis, False)


def team_sum(value, beside, final):
    depth = lax.axis_size("z")
    z = lax.axis_index("z")

    def halved(value, axis, name, pairs, *others):
        sent = half_of(value, axis, name, 1).astype(bf16)
        sent = lax.ppermute(tied(sent, *others) if others else sent, name, pairs)
        return half_of(value, axis, name, 0).astype(f32) + sent.astype(f32)

    swap = [(0, 1), (1, 0)]
    held = halved(value, 3, "c", swap)
    held = halved(held, 0, "y", swap)
    held = halved(held, 0, "x", swap, *beside[:1])
    if beside[1:]:
        held = tied(held, *beside[1:])
    own = lax.dynamic_index_in_dim(held, z, 0, False)
    for k in range(1, depth):
        own = own + shifted(lax.dynamic_index_in_dim(held, (z + k) % depth, 0, False).astype(bf16), k).astype(f32)
    own = own.astype(bf16)
    back = jnp.stack([own] + [shifted(own, k) for k in range(1, depth)])
    rolled = back[(z - jnp.arange(depth)) % depth]

    def doubled(value, axis, name):
        other = lax.ppermute(value, name, swap)
        flag = lax.axis_index(name) == 0
        return jnp.stack([jnp.where(flag, value, other), jnp.where(flag, other, value)], axis=axis)

    wide = doubled(doubled(rolled, 0, "x"), 0, "y")
    return doubled(tied(wide, *final) if final else wide, 3, "c")


def entering_state(passing, local_end, backward):
    count, place = lax.axis_size("o"), lax.axis_index("o")
    decays = lax.all_gather(passing.astype(bf16), "o")
    ends = lax.all_gather(local_end.astype(bf16), "o")
    state = jnp.zeros_like(local_end)
    for i in range(count):
        source = count - 1 - i if backward else i
        ahead = source > place if backward else source < place
        state = jnp.where(ahead, decays[source].astype(f32) * state + ends[source].astype(f32), state)
    return state


def on_device(
    tokens,
    cotangent,
    modality,
    starts,
    row_lengths,
    norm_gain,
    in_x_weight,
    in_z_weight,
    xdt_weight,
    xbc_weight,
    dt_weight,
    dt_bias,
    conv_weight,
    conv_bias,
    log_rates,
    skip_gain,
    out_weight,
):
    outer, group = lax.axis_size("o"), lax.axis_size(group_axes)
    rows, here = modality.shape
    width = tokens.shape[-1]
    mods = in_x_weight.shape[1]
    taps, states, rank = conv_weight.shape[0], log_rates.shape[0], dt_weight.shape[0]
    margin = taps - 1
    local_len = group * here
    own_row = lax.axis_index(row_axes)
    count = rows * local_len

    depth = lax.axis_size("z")
    place_z = lax.axis_index("z")

    def lead(weight):
        return jnp.transpose(weight, (1, 0, 2))

    features = norm_gain.shape[0]
    packed = jnp.concatenate(
        [modality.astype(f32).reshape(-1), starts.astype(f32).reshape(-1), norm_gain.astype(f32)]
    )
    packed = jnp.stack([packed] + [shifted(packed, k) for k in range(1, depth)])
    packed = packed[(place_z - jnp.arange(depth)) % depth]
    others, first_core = swapped(packed), lax.axis_index("c") == 0
    packed = jnp.stack([jnp.where(first_core, packed, others), jnp.where(first_core, others, packed)], axis=1)
    labels = packed[:, :, : 2 * rows * here].astype(jnp.int32).reshape(depth, 2, 2, rows, here)
    labels = jnp.transpose(labels, (2, 3, 0, 1, 4)).reshape(2, rows, local_len)
    modality, starts = labels[0], labels[1]
    gain = outer_gathered(packed[:, :, 2 * rows * here :].reshape(-1, features), 0).reshape(width)

    inputs = tokens[0].astype(f32)
    inv_rms = lax.rsqrt(jnp.mean(inputs * inputs, axis=-1, keepdims=True) + epsilon)
    scaled = inputs * inv_rms
    wz = spread_done(spread_weight(lead(in_z_weight)))
    normed_pieces, last_pieces, wx = team_gather((scaled * gain).astype(bf16), spread_weight(lead(in_x_weight)))
    wx = through_outer(wx)
    position = lax.axis_index(seq_axes) * here + jnp.arange(here, dtype=jnp.int32)
    own_valid = (position < lax.dynamic_index_in_dim(row_lengths, own_row, 0, False)).astype(f32)[:, None]
    upstream = cotangent[0].astype(f32)
    own_back = (upstream * own_valid).astype(bf16)
    own_back = tied(own_back, *last_pieces)
    d_branch = lax.all_gather(own_back, team_axes)
    xdt = outer_gathered(xdt_weight, 0)
    xbc = outer_gathered(xbc_weight, 2)
    dtw = outer_gathered(dt_weight, 2)
    dtb = outer_gathered(dt_bias, 1).astype(f32)
    conv_w = outer_gathered(conv_weight, 1).astype(f32)
    conv_b = outer_gathered(conv_bias, 0).astype(f32)
    log_r = outer_gathered(log_rates, 1).astype(f32)
    skip = outer_gathered(skip_gain, 0).astype(f32)
    mine = skip.shape[0]
    places = relative_places()
    pieces_of = lax.axis_size(team_axes)
    relative = jnp.zeros((pieces_of,), jnp.int32).at[places].set(jnp.arange(pieces_of, dtype=jnp.int32))

    counted = jnp.cumsum(starts, axis=1)
    send_keep = counted[:, -1:] - counted[:, local_len - margin :] == 0
    counted_ext = jnp.concatenate([jnp.zeros((rows, margin), jnp.int32), counted], axis=1)
    facts = [counted - counted_ext[:, margin - lag : margin - lag + local_len] == 0 for lag in range(1, taps)]
    facts = [f.astype(f32) for f in facts] + [starts.astype(f32), modality.astype(f32)]
    facts += [jnp.zeros_like(facts[0])] * (fact_columns - len(facts))
    facts = jnp.stack([f.reshape(rows, group, here) for f in facts], axis=2)
    row_label = jnp.transpose(modality.reshape(rows, group, here), (1, 0, 2)).astype(f32)
    facts_flat = facts.reshape(pieces_of, fact_columns, here)
    facts_there = facts_flat[places]
    in_order = jnp.arange(pieces_of, dtype=jnp.int32)

    conv_in, wx_f, normed = lead_pieces(places, normed_pieces, facts_there, wx, bf16)
    conv_in = conv_in.reshape(rows, local_len, mine)
    gate_in, wz_f = lead_product(places, normed, facts_there, wz, f32)
    gate_in = gate_in.reshape(rows, local_len, mine)

    before = jnp.zeros((rows, 8, mine), f32)
    if outer > 1:
        outgoing = jnp.where(send_keep[:, :, None], conv_in[:, local_len - margin :, :], jnp.zeros((), bf16))
        incoming = passed_along(outgoing, "o", 1).astype(f32)
        before = jnp.pad(incoming, ((0, 0), (8 - margin, 0), (0, 0)))
    halves = 2
    pieces = states // halves
    narrow = 2 * states
    xdt_f = xdt.reshape(mine, mods * rank)
    xbc_f = jnp.transpose(xbc.reshape(2, halves, pieces, mods, mine), (3, 1, 0, 2, 4)).reshape(mods * narrow, mine)
    dt_f = dtw.reshape(rank, mods * mine)
    pre, proj_part = conv_block(conv_in, before, facts, row_label, conv_w, conv_b[None], xdt_f, xbc_f)

    def summed(part, beside, final):
        return team_sum(part.reshape((2, 2, depth, 2) + part.shape[2:]), beside, final).reshape(part.shape)

    proj = summed(proj_part, [facts, gate_in], [])
    wo = spread_done(tied(spread_weight(lead(out_weight)), proj))
    d_gated, wo_f = lead_product(in_order, d_branch, facts_flat, wo, f32)
    d_gated = d_gated.reshape(rows, local_len, mine)
    decay_coef = -jnp.exp(log_r)

    def per_state(values):
        split = jnp.transpose(values.reshape(halves, pieces, mine), (1, 0, 2))
        return jnp.repeat(split, rows, axis=1)

    rates = per_state(decay_coef)
    rates2 = rates * (1.0 / math.log(2.0))
    zero_state = jnp.zeros((pieces, halves * rows, mine), f32)
    skip_row = skip[None]
    dtb_row = dtb.reshape(1, mods * mine)

    def ahead(start):
        return scan_forward(proj, pre, facts, gate_in, dt_f, dtb_row, rates2, skip_row, start)

    gated, scanned, dt_pre, kept, last_state = ahead(zero_state)
    if outer > 1:
        steps = jnp.sum(jax.nn.softplus(dt_pre), axis=1)
        unbroken = (jnp.sum(starts, axis=1) == 0).astype(f32)[:, None]
        passing = jnp.exp2(jnp.concatenate([steps] * halves, axis=0)[None] * rates2)
        passing = passing * jnp.concatenate([unbroken] * halves, axis=0)[None]
        gated, scanned, dt_pre, kept, last_state = ahead(entering_state(passing, last_state, False))
    gated = gated.reshape(pieces_of, here, mine)
    branch = trail_product([gated], facts_flat, [wo_f], mods)[0].reshape(count, width)
    own_branch = lax.psum_scatter(branch, team_axes, scatter_dimension=0, tiled=True).astype(f32)
    block_out = (inputs + own_valid * own_branch).astype(bf16)[None]
    grad_type = f32 if outer > 1 else bf16

    def weight_grad(x, d, there, *beside):
        return feature_grad(x, d, there, mods, outer * group, grad_type, beside)

    out_parts = weight_grad(d_branch, gated, facts_flat)

    def back(carry):
        return scan_backward(
            relative, proj, pre, facts, gate_in, scanned, dt_pre, d_gated, kept, dt_f, rates2, rates, skip_row, last_state,
            carry, out_parts,
        )

    results = back(zero_state)
    if outer > 1:
        results = back(entering_state(passing, results[-1], True))
    d_gate, d_proj_part, d_act, dtw_grad, dtb_grad, skip_grad, rate_total, _ = results
    z_parts = weight_grad(normed, d_gate, facts_there)
    out_got, z_got = collect(out_parts), collect(z_parts)
    d_proj = summed(tied(d_proj_part, out_got), [z_parts], [])
    out_weight_grad = lead(settled(out_got, lead(out_weight))[0])
    in_z_grad, gain_z = settled(z_got, lead(in_z_weight))
    rate_total = jnp.sum(rate_total.reshape(pieces, halves, rows, mine), axis=2)
    rate_total = jnp.transpose(rate_total, (1, 0, 2)).reshape(states, mine)
    log_rates_grad = outer_summed(decay_coef * rate_total, 1)
    skip_gain_grad = outer_summed(skip_grad[0], 0)
    dt_weight_grad = outer_summed(dtw_grad.reshape(rank, mods, mine), 2)
    dt_bias_grad = outer_summed(dtb_grad.reshape(mods, mine), 1)
    d_conv, xdt_grad, xbc_grad, taps_grad, bias_grad, head, tail = deconv_block(
        relative, d_proj, conv_in, pre, d_act, facts, row_label, conv_w, xdt_f, xbc_f
    )
    if outer > 1:
        early = jnp.stack(
            [jnp.pad(head[:, lag - 1, :lag], ((0, 0), (margin - lag, 0), (0, 0))) for lag in range(1, taps)], axis=1
        )
        taps_grad = taps_grad.at[1:].add(jnp.sum(early * incoming[:, None], axis=(0, 2)))
        returned = jnp.sum(early * conv_w[None, 1:, None, :], axis=1)
        returned = passed_along(returned.astype(bf16), "o", -1).astype(f32)
        returned = jnp.where(send_keep[:, :, None], returned, 0.0)
        fixed = (tail[:, 8 - margin :] + returned).astype(bf16)
        spots = relative[jnp.arange(rows) * group + group - 1]
        d_conv = d_conv.at[spots, here - margin :].set(fixed)
    xdt_grad = outer_summed(xdt_grad.reshape(mine, mods, rank), 0)
    xbc_grad = jnp.transpose(xbc_grad.reshape(mods, halves, 2, pieces, mine), (2, 1, 3, 0, 4)).reshape(narrow, mods, mine)
    xbc_grad = outer_summed(xbc_grad, 2)
    conv_weight_grad = outer_summed(taps_grad, 1)
    conv_bias_grad = outer_summed(bias_grad[0], 0)
    x_parts = weight_grad(normed, d_conv, facts_there)
    d_scaled = team_scatter(
        lambda ks, others: trail_product([d_conv, d_gate], facts_there, [wx_f, wz_f], mods, ks, others), [z_got, x_parts]
    )
    d_scaled = d_scaled * gain
    in_x_grad, gain_x = settled(collect(x_parts), lead(in_x_weight))
    d_inputs = inv_rms * (d_scaled - scaled * jnp.mean(d_scaled * scaled, axis=-1, keepdims=True))
    tokens_grad = (upstream + d_inputs).astype(bf16)[None]
    gain_part = gain_x + gain_z
    for name in row_axes:
        gain_part = gain_part + lax.ppermute(gain_part, name, [(0, 1), (1, 0)])
    norm_gain_grad = gain_part / norm_gain.astype(f32)
    in_x_grad, in_z_grad = lead(in_x_grad), lead(in_z_grad)
    return (
        block_out,
        tokens_grad,
        norm_gain_grad,
        in_x_grad,
        in_z_grad,
        xdt_grad,
        xbc_grad,
        dt_weight_grad,
        dt_bias_grad,
        conv_weight_grad,
        conv_bias_grad,
        log_rates_grad,
        skip_gain_grad,
        out_weight_grad,
    )


def solution(mesh):
    rows, seq = mesh.shape["row"], mesh.shape["seq"]
    across = 2 if rows % 2 == 0 else 1
    cores = 2 if seq % 2 == 0 else 1
    along = next(n for n in (4, 3, 2, 1) if (seq // cores) % n == 0)
    fine = Mesh(
        mesh.devices.reshape(rows // across, across, seq // (along * cores), along, cores), ("y", "x", "o", "z", "c")
    )
    row, seq, both = row_axes, seq_axes, row_axes + seq_axes
    in_specs = (
        P(row, seq, None),
        P(row, seq, None),
        P(None, seq),
        P(None, seq),
        P(),
        P(seq),
        P(seq, None, row),
        P(seq, None, row),
        P(both, None, None),
        P(None, None, both),
        P(None, None, both),
        P(None, both),
        P(None, both),
        P(both),
        P(None, both),
        P(both),
        P(seq, None, row),
    )
    out_specs = (
        P(row, seq, None),
        P(row, seq, None),
        P(seq),
        P(seq, None, row),
        P(seq, None, row),
        P(both, None, None),
        P(None, None, both),
        P(None, None, both),
        P(None, both),
        P(None, both),
        P(both),
        P(None, both),
        P(both),
        P(seq, None, row),
    )
    return jax.shard_map(on_device, mesh=fine, in_specs=in_specs, out_specs=out_specs, check_vma=False)
```
